512 devices in a mesh: gx: 32 (over z, x), gy: 16 (over y, core).
Axes of the slice: x: 4, y: 8, z: 8, core: 2. Of those that a mesh axis runs over, the one named last changes fastest.
Arguments:
- probe_data: float32 [2, 3, 65536], P(None, None, ('gx', 'gy')), may hold values from -10 to 10
- conductivity: float32 [160, 80, 640], P('gx', 'gy'), may hold values from 0.5 to 10
- support: int32 [32, 16, 128], P('gx', 'gy'), may hold values 0 or 1
- face_tags: int32 [2, 32, 16], P(None, 'gx', 'gy'), may hold values 0 or 1
- probe_nodes: int32 [65536], P(('gx', 'gy')), may hold values from 0 to 15999
Outputs:
- source_estimate: float32 [2, 3, 160, 80, 640], P(None, None, 'gx', 'gy')
- data_residual: float32 [2, 3, 65536], P(None, None, ('gx', 'gy'))
The draws below stay inside these ranges and needn't reach their ends.
Inputs may be any that keep to these rules, and one draw needn't show every extreme that they name: `probe_nodes`: probe p lies in the block of device p // 128 (gx-major), as a node index of that block flattened with the third dimension fastest.
All inputs are finite; a program needn't handle non-finite values. No bound on the sum of `support` or of `face_tags` on one device may be relied on, other than what follows from the above.
Results may differ from the reference program's by a relative error of at most 0.0008.
Values sent between devices are 32-bit elements; how exact they have to be, the bound alone decides.
A program may use at most 128 MiB of HBM per device.

```python
import math
import jax
import jax.numpy as jnp
import numpy as np
from jax import lax

EX = 1
EY = 1
EZ = 128
PROBE_DEV = 128
STEPS = 2
ITERS = 2
EXG = 32
EYG = 16
NX = 160
NY = 80
NZ = 640
PROBES = 65536
NODES_DEV = 16000
N_GX = 32
N_GY = 16


def draw_probe_data(key, part):
    key = jax.random.fold_in(key, 11)
    key_main = jax.random.fold_in(key, 0)
    devices_all = N_GX * N_GY
    position = jnp.arange(PROBES) // PROBE_DEV
    growth = jnp.sqrt(1.0 + 2.0 * position.astype(jnp.float32) / max(devices_all - 1, 1))
    values = jax.random.truncated_normal(key_main, -4.0, 4.0, (STEPS, 3, PROBES), jnp.float32)
    return values * growth


def with_ends(entries, own_key, least, high):
    shape = entries.shape
    spot = [jax.random.randint(jax.random.fold_in(own_key, axis), (), 0, shape[axis]) for axis in range(len(shape))]
    entries = entries.at[tuple(spot)].set(least)
    longest = shape.index(max(shape))
    spot[longest] = (spot[longest] + 1) % shape[longest]
    return entries.at[tuple(spot)].set(high)


def shard_levels(own_key, dims, cuts, low, high):
    loudness, own = 1.0, jax.random.fold_in(own_key, 6)
    for dim, blocks in cuts:
        steps = jnp.exp(jax.random.uniform(jax.random.fold_in(own, dim), (blocks,), jnp.float32, low / len(cuts), high / len(cuts)))
        loudness = loudness * jnp.repeat(steps, dims[dim] // blocks).reshape([-1 if axis == dim else 1 for axis in range(len(dims))])
    return loudness


def setup_inputs(seed: int = 0) -> dict:
    key_of = jax.random.split(jax.random.key(seed), 6)
    return {
        "probe_data": draw_probe_data(jax.random.fold_in(key_of[5], 71), 0),
        "conductivity": jnp.clip(jnp.exp(math.log(10.0) - 2.9957323 * jax.random.uniform(key_of[1], (NX, NY, NZ), jnp.float32) ** shard_levels(key_of[1], (NX, NY, NZ), ((0, 32), (1, 16)), -0.2, 0.2)), 0.5, 10.0),
        "support": with_ends((jax.random.randint(key_of[2], (EXG, EYG, EZ), 0, 2) < 1).astype(jnp.int32), jax.random.fold_in(key_of[2], 1), 0, 1),
        "face_tags": with_ends((jax.random.randint(key_of[3], (2, EXG, EYG), 0, 2) < 1).astype(jnp.int32), jax.random.fold_in(key_of[3], 1), 0, 1),
        "probe_nodes": with_ends(jax.random.randint(key_of[4], (PROBES,), 0, NODES_DEV), jax.random.fold_in(key_of[4], 1), 0, NODES_DEV - 1).astype(jnp.int32),
    }


STEP_SIZE = 0.02
LIFT_HALF = 5.0
DRIVE_GAIN = 50.0
HIGHEST = lax.Precision.HIGHEST

def lobatto_derivative():
    radical = math.sqrt(3.0 / 7.0)
    points = np.array([-1.0, -radical, 0.0, radical, 1.0])
    legendre = (35.0 * points ** 4 - 30.0 * points ** 2 + 3.0) / 8.0
    matrix = np.zeros((5, 5))
    for row_idx in range(5):
        for col_idx in range(5):
            if row_idx != col_idx:
                matrix[row_idx, col_idx] = legendre[row_idx] / (legendre[col_idx] * (points[row_idx] - points[col_idx]))
    matrix[0, 0] = -5.0
    matrix[4, 4] = 5.0
    return jnp.asarray(matrix, dtype=jnp.float32)

def normal_cross(axis_id, orient, vector):
    blank_part = jnp.zeros_like(vector[0])
    if axis_id == 0:
        return [blank_part, -orient * vector[2], orient * vector[1]]
    if axis_id == 1:
        return [orient * vector[2], blank_part, -orient * vector[0]]
    return [-orient * vector[1], orient * vector[0], blank_part]

def face_flux(inner, outer, axis_id, orient):
    jumps = outer - inner
    jump_e = [jumps[0], jumps[1], jumps[2]]
    jump_h = [jumps[3], jumps[4], jumps[5]]
    turn_h = normal_cross(axis_id, orient, jump_h)
    turn_e = normal_cross(axis_id, orient, jump_e)
    pieces = []
    for member in range(3):
        retain = 0.0 if member == axis_id else 1.0
        pieces.append(turn_h[member] + retain * jump_e[member])
    for member in range(3):
        retain = 0.0 if member == axis_id else 1.0
        pieces.append(retain * jump_h[member] - turn_e[member])
    return LIFT_HALF * jnp.stack(pieces)

def add_faces(change, fields, ghost_low, ghost_high, axis_dim):
    extent = fields.shape
    blocks = fields.reshape(extent[:axis_dim] + (extent[axis_dim] // 5, 5) + extent[axis_dim + 1:])
    low_faces = lax.index_in_dim(blocks, 0, axis_dim + 1, keepdims=False)
    high_faces = lax.index_in_dim(blocks, 4, axis_dim + 1, keepdims=False)
    elements = low_faces.shape[axis_dim]
    outer_low = jnp.concatenate([jnp.expand_dims(ghost_low, axis_dim), lax.slice_in_dim(high_faces, 0, elements - 1, axis=axis_dim)], axis=axis_dim)
    outer_high = jnp.concatenate([lax.slice_in_dim(low_faces, 1, elements, axis=axis_dim), jnp.expand_dims(ghost_high, axis_dim)], axis=axis_dim)
    fix_low = face_flux(low_faces, outer_low, axis_dim - 1, -1.0)
    fix_high = face_flux(high_faces, outer_high, axis_dim - 1, 1.0)
    middle_zero = jnp.zeros_like(fix_low)
    stacked = jnp.stack([fix_low, middle_zero, middle_zero, middle_zero, fix_high], axis=axis_dim + 1)
    return change + stacked.reshape(extent)

def derivative_first(fields, lobatto):
    extent = fields.shape
    blocks = fields.reshape(extent[0], extent[1] // 5, 5, extent[2], extent[3])
    return jnp.einsum('ij,cejyz->ceiyz', lobatto, blocks, precision=HIGHEST).reshape(extent)

def derivative_second(fields, lobatto):
    extent = fields.shape
    blocks = fields.reshape(extent[0], extent[1], extent[2] // 5, 5, extent[3])
    return jnp.einsum('ij,cxejz->cxeiz', lobatto, blocks, precision=HIGHEST).reshape(extent)

def derivative_third(fields, lobatto):
    extent = fields.shape
    blocks = fields.reshape(extent[0], extent[1], extent[2], extent[3] // 5, 5)
    return jnp.einsum('ij,cxyej->cxyei', lobatto, blocks, precision=HIGHEST).reshape(extent)

def evaluate(fields, ghosts, conduct, tag_nodes, lobatto):
    grad_x = derivative_first(fields, lobatto)
    grad_y = derivative_second(fields, lobatto)
    grad_z = derivative_third(fields, lobatto)
    curl_e = [grad_y[2] - grad_z[1], grad_z[0] - grad_x[2], grad_x[1] - grad_y[0]]
    curl_h = [grad_y[5] - grad_z[4], grad_z[3] - grad_x[5], grad_x[4] - grad_y[3]]
    change = jnp.stack([curl_h[0] - conduct * fields[0], curl_h[1] - conduct * fields[1], curl_h[2] - conduct * fields[2], -curl_e[0], -curl_e[1], -curl_e[2]])
    change = add_faces(change, fields, ghosts[0], ghosts[1], 1)
    change = add_faces(change, fields, ghosts[2], ghosts[3], 2)
    mirror = jnp.array([-1.0, -1.0, -1.0, 1.0, 1.0, 1.0], dtype=jnp.float32)[:, None, None]
    bottom = mirror * tag_nodes[0] * fields[:, :, :, 0]
    top_ghost = mirror * tag_nodes[1] * fields[:, :, :, -1]
    return add_faces(change, fields, bottom, top_ghost, 3)

def reference(probe_data, conductivity, support, face_tags, probe_nodes):
    lobatto = lobatto_derivative()
    support_nodes = jnp.repeat(jnp.repeat(jnp.repeat(support, 5, axis=0), 5, axis=1), 5, axis=2).astype(jnp.float32)
    tag_nodes = jnp.repeat(jnp.repeat(face_tags, 5, axis=1), 5, axis=2).astype(jnp.float32)
    which = jnp.arange(PROBES, dtype=jnp.int32) // PROBE_DEV
    row_block = which // N_GY
    col_block = which % N_GY
    span_y = 5 * EY
    span_z = 5 * EZ
    local_x = probe_nodes // (span_y * span_z)
    local_y = probe_nodes // span_z % span_y
    local_z = probe_nodes % span_z
    flat_index = (((row_block * (5 * EX) + local_x) * NY + col_block * span_y + local_y) * NZ + local_z).astype(jnp.int32)
    plane_x = jnp.zeros((6, NY, NZ), jnp.float32)
    plane_y = jnp.zeros((6, NX, NZ), jnp.float32)
    ghosts = (plane_x, plane_x, plane_y, plane_y)

    def apply_rates(fields):
        return evaluate(fields, ghosts, conductivity, tag_nodes, lobatto)

    def forward(amounts):
        fields = jnp.zeros((6, NX, NY, NZ), jnp.float32)
        blank_three = jnp.zeros((3, NX, NY, NZ), jnp.float32)
        records = []
        for moment in range(STEPS):
            forcing = jnp.concatenate([-DRIVE_GAIN * support_nodes * amounts[moment], blank_three])
            slope_one = apply_rates(fields) + forcing
            middle = fields + STEP_SIZE * slope_one
            slope_two = apply_rates(middle) + forcing
            fields = fields + 0.5 * STEP_SIZE * (slope_one + slope_two)
            records.append(jnp.take(fields[0:3].reshape(3, -1), flat_index, axis=1))
        return jnp.stack(records)

    def adjoint(values):
        blank_source = jnp.zeros((STEPS, 3, NX, NY, NZ), jnp.float32)
        return jax.vjp(forward, blank_source)[1](values)[0]
    data_scale = jnp.sqrt(jnp.sum(probe_data * probe_data))
    left_vector = probe_data / data_scale
    raw_right = adjoint(left_vector)
    source_scale = jnp.sqrt(jnp.sum(raw_right * raw_right))
    right_vector = raw_right / source_scale
    direction = right_vector
    estimate = jnp.zeros_like(right_vector)
    phi_bar = data_scale
    rho_bar = source_scale
    for sweep in range(ITERS):
        raw_left = forward(right_vector) - source_scale * left_vector
        data_scale = jnp.sqrt(jnp.sum(raw_left * raw_left))
        left_vector = raw_left / data_scale
        rho_value = jnp.sqrt(rho_bar * rho_bar + data_scale * data_scale)
        cosine = rho_bar / rho_value
        sine_value = data_scale / rho_value
        phi_step = cosine * phi_bar
        phi_bar = sine_value * phi_bar
        estimate = estimate + phi_step / rho_value * direction
        if sweep < ITERS - 1:
            raw_right = adjoint(left_vector) - data_scale * right_vector
            source_scale = jnp.sqrt(jnp.sum(raw_right * raw_right))
            right_vector = raw_right / source_scale
            theta_next = sine_value * source_scale
            rho_bar = -cosine * source_scale
            direction = right_vector - theta_next / rho_value * direction
    return (estimate, phi_bar * left_vector)
```

```python
import functools
import math

import jax
import jax.numpy as jnp
import numpy as np
from jax import lax
from jax.experimental import pallas as pl
from jax.experimental.pallas import tpu as pltpu
from jax.sharding import PartitionSpec as P

MESH = pl.DeviceIdType.MESH
F32 = jnp.float32
BF16 = jnp.bfloat16

STEP_SIZE = 0.02
LIFT_HALF = 5.0
DRIVE_GAIN = 50.0
NX_CHIPS = 4
CORES = 2
ROWS = 80
QROWS = 56
HALF = 640
WIDE = 1280
FACES = 4
CHARS = (
    ((1, 2, 1.0), (2, 1, -1.0)),
    ((1, 2, -1.0), (2, 1, 1.0)),
    ((0, 2, -1.0), (2, 0, 1.0)),
    ((0, 2, 1.0), (2, 0, -1.0)),
)
SIDES = ((0, 4, 0), (0, 0, 4), (1, 4, 0), (1, 0, 4))


def lobatto_scaled():
    radical = math.sqrt(3.0 / 7.0)
    points = np.array([-1.0, -radical, 0.0, radical, 1.0])
    legendre = (35.0 * points**4 - 30.0 * points**2 + 3.0) / 8.0
    weights = 0.1 / legendre**2
    matrix = np.zeros((5, 5))
    for i in range(5):
        for j in range(5):
            if i != j:
                matrix[i, j] = legendre[i] / (legendre[j] * (points[i] - points[j]))
    root = np.sqrt(weights)
    return matrix * root[:, None] / root[None, :], root


def row_of(comp, i, j):
    return comp * 25 + 5 * i + j


def split_np(matrix):
    high = np.asarray(matrix, np.float32).astype(jnp.bfloat16)
    low = (np.asarray(matrix, np.float32) - high.astype(np.float32)).astype(jnp.bfloat16)
    return high, low


def tables():
    deriv, root = lobatto_scaled()
    deriv = STEP_SIZE * deriv
    curl = np.zeros((ROWS, ROWS))
    turn = np.zeros((QROWS, ROWS))
    for i in range(5):
        for j in range(5):
            for k in range(5):
                curl[row_of(0, i, j), row_of(2, i, k)] += deriv[j, k]
                curl[row_of(1, i, j), row_of(2, k, j)] -= deriv[i, k]
                curl[row_of(2, i, j), row_of(1, k, j)] += deriv[i, k]
                curl[row_of(2, i, j), row_of(0, i, k)] -= deriv[j, k]
            turn[row_of(0, i, j), row_of(1, i, j)] = 1.0
            turn[row_of(1, i, j), row_of(0, i, j)] = -1.0
    high, low = split_np(curl)
    inner = np.zeros((ROWS + 64, 256), jnp.bfloat16)
    inner[:ROWS, 0:80] = high
    inner[:ROWS, 80:160] = high
    inner[:ROWS, 160:240] = low
    inner[ROWS : ROWS + QROWS, 0:80] = turn.astype(jnp.bfloat16)
    inner[ROWS : ROWS + QROWS, 80:160] = turn.astype(jnp.bfloat16)

    send_e = np.zeros((64, 256), jnp.bfloat16)
    send_h = np.zeros((64, 256), jnp.bfloat16)
    lift = np.zeros((2 * ROWS, 128), jnp.bfloat16)
    for face in range(FACES):
        axis, node_out, node_in = SIDES[face]
        for slot in range(16):
            char = slot if slot < 8 else 8 + slot % 2
            which, along = char // 5, char % 5
            comp_e, comp_h, sign = CHARS[face][which]
            spot_out = (node_out, along) if axis == 0 else (along, node_out)
            spot_in = (node_in, along) if axis == 0 else (along, node_in)
            at = face * 16 + slot
            for part in (0, 80):
                send_e[at, part + row_of(comp_e, *spot_out)] = 1.0
                send_h[at, part + row_of(comp_h, *spot_out)] = sign
            for part in (0, 64):
                lift[row_of(comp_e, *spot_in), part + at] = 1.0
                lift[ROWS + row_of(comp_h, *spot_in), part + at] = sign

    columns = np.zeros((5, ROWS), np.float32)
    strength = STEP_SIZE * LIFT_HALF
    for comp in range(3):
        for i in range(5):
            for j in range(5):
                row = row_of(comp, i, j)
                columns[0, row] = root[i] * root[j]
                columns[1, row] = 1.0 / (root[i] * root[j])
                count = (i in (0, 4)) * (comp != 0) + (j in (0, 4)) * (comp != 1)
                columns[2, row] = strength * count
                columns[3, row] = strength * (count + (comp != 2))
                columns[4, row] = strength * (comp != 2)
    spread = np.ascontiguousarray(np.broadcast_to(columns[:, :, None], (5, ROWS, 128)))

    order = np.zeros((HALF, HALF), jnp.bfloat16)
    for z in range(HALF):
        order[z, (z % 5) * 128 + z // 5] = 1.0
    return inner, send_e, send_h, lift, spread, order


def split(value):
    high = value.astype(BF16)
    return high, (value - high.astype(F32)).astype(BF16)


def dot(a, b):
    return jnp.dot(a, b, preferred_element_type=F32)


def dot_nt(a, b):
    return lax.dot_general(a, b, (((1,), (1,)), ((), ())), preferred_element_type=F32)


def lanes(block):
    return slice(block * 128, block * 128 + 128)


def kernel(
    n_gx, n_gy, data_ref, cond_ref, supp_ref, tags_ref, nodes_ref, inner_ref, send_e_ref, send_h_ref, lift_ref,
    spread_ref, order_ref, est_ref, res_ref,
    fields, rates, saved, rhs, prod, ghost_rhs, sig, gain, pick_row, pick_lane, pick_back, left, unit, record,
    source, basis, scalars, perm, send_buf, recv_buf, red_buf, send_sem, recv_sem, red_send_sem, red_recv_sem,
):
    deriv, root = lobatto_scaled()
    deriv = STEP_SIZE * deriv
    gx, gy = lax.axis_index("gx"), lax.axis_index("gy")
    x_at, z_at = lax.rem(gx, NX_CHIPS), lax.div(gx, NX_CHIPS)
    core_at, y_at = lax.rem(gy, CORES), lax.div(gy, CORES)
    n_z, n_y, n_xc = n_gx // NX_CHIPS, n_gy // CORES, NX_CHIPS * CORES
    sizes = (n_xc, n_z, n_y)

    def partner(phase, step):
        if phase == 0:
            spot = lax.rem(x_at * CORES + core_at + step, n_xc)
            return (z_at * NX_CHIPS + lax.div(spot, CORES), y_at * CORES + lax.rem(spot, CORES))
        if phase == 1:
            return (lax.rem(z_at + step, n_z) * NX_CHIPS + x_at, gy)
        return (gx, lax.rem(y_at + step, n_y) * CORES + core_at)

    beside = (
        (lax.rem(gx + 1, n_gx), gy),
        (lax.rem(gx + n_gx - 1, n_gx), gy),
        (gx, lax.rem(gy + 1, n_gy)),
        (gx, lax.rem(gy + n_gy - 1, n_gy)),
    )
    strength = STEP_SIZE * LIFT_HALF
    open_faces = (
        jnp.where(gx > 0, strength, 0.0).astype(F32),
        jnp.where(gx < n_gx - 1, strength, 0.0).astype(F32),
        jnp.where(gy > 0, strength, 0.0).astype(F32),
        jnp.where(gy < n_gy - 1, strength, 0.0).astype(F32),
    )

    barrier = pltpu.get_barrier_semaphore()
    greeted = 0
    for device in beside:
        pl.semaphore_signal(barrier, inc=1, device_id=device, device_id_type=MESH)
        greeted += 1
    for phase in range(3):
        for step in range(1, sizes[phase]):
            pl.semaphore_signal(barrier, inc=1, device_id=partner(phase, step), device_id_type=MESH)
            greeted += 1

    tag_low = tags_ref[0, 0, 0].astype(F32)
    tag_high = tags_ref[1, 0, 0].astype(F32)
    perm[...] = jnp.zeros_like(perm)
    for comp in range(3):
        for i in range(5):
            perm[comp * 25 + i * 5 : comp * 25 + i * 5 + 5, :] = cond_ref[i]
    high, low = split(perm[0:ROWS, :])
    order = order_ref[...]
    for k in range(5):
        both = dot(jnp.concatenate([high, low], axis=0), order_ref[:, lanes(k)])
        own = spread_ref[3 if k in (0, 4) else 2]
        sig[:, lanes(k)] = STEP_SIZE * (both[0:ROWS] + both[ROWS : 2 * ROWS]) + own
    support = supp_ref[0].astype(F32)
    for k in range(5):
        gain[:, lanes(k)] = (-DRIVE_GAIN * STEP_SIZE * float(root[k])) * support * spread_ref[0]

    node = nodes_ref[...].astype(F32)
    pair = jnp.floor((node + 0.5) * (1.0 / HALF))
    depth = node - float(HALF) * pair
    element = jnp.floor((depth + 0.5) * 0.2)
    inside = depth - 5.0 * element
    weight = jnp.zeros_like(node)
    for k in range(5):
        weight = jnp.where(inside == float(k), float(1.0 / root[k]), weight)
    row_id = lax.broadcasted_iota(jnp.int32, (ROWS, 128), 0)
    comp_id = (row_id >= 25).astype(jnp.int32) + (row_id >= 50).astype(jnp.int32) + (row_id >= 75).astype(jnp.int32)
    spot_id = (row_id - 25 * comp_id).astype(F32)
    pick_row[...] = jnp.where(spot_id == pair, spread_ref[1] * weight, 0.0)
    sub_id = lax.broadcasted_iota(jnp.int32, (128, 128), 0).astype(F32)
    for k in range(5):
        hot = jnp.where((sub_id == element) & (inside == float(k)), 1.0, 0.0)
        pick_lane[lanes(k), :] = hot.astype(BF16)
        flipped = jnp.transpose(hot).astype(BF16)
        pick_back[0:128, lanes(k)] = flipped
        pick_back[128:256, lanes(k)] = flipped

    left[...] = jnp.zeros_like(left)
    left[0, 0:3, :] = data_ref[0]
    left[1, 0:3, :] = data_ref[1]
    basis[0] = jnp.zeros_like(basis[0])
    rhs[240:256, :] = jnp.zeros((16, WIDE), BF16)
    sub8 = lax.broadcasted_iota(jnp.int32, (8, 128), 0)
    lane56 = lax.broadcasted_iota(jnp.int32, (QROWS, 128), 1)

    pl.semaphore_wait(barrier, greeted)

    def reduce_send(index, phase, row):
        red_buf[index, phase, 0] = row
        for step in range(1, sizes[phase]):
            pltpu.make_async_remote_copy(
                src_ref=red_buf.at[index, phase, 0],
                dst_ref=red_buf.at[index, phase, step],
                send_sem=red_send_sem.at[index, phase],
                recv_sem=red_recv_sem.at[index, phase],
                device_id=partner(phase, step),
                device_id_type=MESH,
            ).start()

    def reduce_take(index, phase):
        if sizes[phase] == 1:
            return red_buf[index, phase, 0]
        others = red_buf.at[index, phase, pl.ds(1, sizes[phase] - 1)]
        pltpu.make_async_copy(others, others, red_recv_sem.at[index, phase]).wait()
        pltpu.make_async_copy(others, others, red_send_sem.at[index, phase]).wait()
        total = red_buf[index, phase, 0]
        for step in range(1, sizes[phase]):
            total = total + red_buf[index, phase, step]
        return total

    def whole(row):
        return jnp.sum(row, axis=1, keepdims=True)

    def data_squares():
        return jnp.sum(left[0] * left[0] + left[1] * left[1], axis=0, keepdims=True)

    def source_squares():
        total = jnp.zeros((ROWS, 128), F32)
        for moment in range(2):
            for k in range(5):
                piece = source[moment, :, lanes(k)]
                total = total + piece * piece
        return jnp.sum(total, axis=0, keepdims=True)

    def apply_rates(step, hook):
        for block in range(10):
            high, low = split(fields[:, lanes(block)])
            rhs[0:80, lanes(block)] = high
            rhs[80:160, lanes(block)] = low
            rhs[160:240, lanes(block)] = high
        out = dot(send_e_ref[...], rhs[:, 0:HALF]) + dot(send_h_ref[...], rhs[:, HALF:WIDE])
        copies = []
        for face in range(FACES):
            base = face * 16
            packed = jnp.zeros((8, 128), F32)
            for k in range(5):
                send_buf[step, face, 8 * k : 8 * k + 8, :] = out[base : base + 8, lanes(k)]
                if k < 4:
                    packed = jnp.where((sub8 >= 2 * k) & (sub8 < 2 * k + 2), out[base + 8 : base + 16, lanes(k)], packed)
            send_buf[step, face, 40:48, :] = packed
            send_buf[step, face, 48:56, :] = out[base + 8 : base + 16, lanes(4)]
            copy = pltpu.make_async_remote_copy(
                src_ref=send_buf.at[step, face],
                dst_ref=recv_buf.at[step, face],
                send_sem=send_sem.at[step, face],
                recv_sem=recv_sem.at[step, face],
                device_id=beside[face],
                device_id_type=MESH,
            )
            copy.start()
            copies.append(copy)

        hook()
        prod[...] = dot(inner_ref[...], rhs[...])
        for half in range(2):
            own0, other0 = half * 5, (1 - half) * 5
            sign = 1.0 if half == 0 else -1.0
            for k in range(5):
                slope = None
                for m in range(5):
                    if m != k and abs(deriv[k, m]) > 1e-12:
                        term = float(deriv[k, m]) * prod[80:136, lanes(other0 + m)]
                        slope = term if slope is None else slope + term
                decay = sig[:, lanes(k)] if half == 0 else spread_ref[3 if k in (0, 4) else 2]
                change = sign * prod[0:80, lanes(other0 + k)] - decay * fields[:, lanes(own0 + k)]
                upper = change[0:QROWS] - sign * slope
                if k in (0, 4):
                    own_low, turn_low = fields[0:QROWS, lanes(own0)], prod[80:136, lanes(other0)]
                    own_high, turn_high = fields[0:QROWS, lanes(own0 + 4)], prod[80:136, lanes(other0 + 4)]
                    if half == 1:
                        turn_low, turn_high = -turn_low, -turn_high
                    if k == 0:
                        inward = pltpu.roll(own_high + turn_high, 1, 1)
                        edge = (tag_low * -sign) * (own_low - turn_low)
                        incoming = jnp.where(lane56 == 0, edge, inward)
                    else:
                        inward = pltpu.roll(own_low - turn_low, 127, 1)
                        edge = (tag_high * -sign) * (own_high + turn_high)
                        incoming = jnp.where(lane56 == 127, edge, inward)
                    upper = upper + spread_ref[4][0:QROWS] * incoming
                rates[0:QROWS, lanes(own0 + k)] = upper
                rates[QROWS:ROWS, lanes(own0 + k)] = change[QROWS:ROWS]

        for copy in copies:
            copy.wait()
        for face in range(FACES):
            for k in range(5):
                packed = recv_buf[step, face, 40:48, :] if k < 4 else recv_buf[step, face, 48:56, :]
                start = 2 * k if k < 4 else 0
                packed = jnp.where((sub8 >= start) & (sub8 < start + 2), packed, 0.0)
                piece = jnp.concatenate([recv_buf[step, face, 8 * k : 8 * k + 8, :], packed], axis=0)
                high, low = split(open_faces[face] * piece)
                ghost_rhs[face * 16 : face * 16 + 16, lanes(k)] = high
                ghost_rhs[64 + face * 16 : 64 + face * 16 + 16, lanes(k)] = low
        lifted = dot(lift_ref[...], ghost_rhs[...])
        rates[:, 0:HALF] += lifted[0:ROWS]
        rates[:, HALF:WIDE] += lifted[ROWS : 2 * ROWS]

    def inject(moment):
        values = jnp.where(
            comp_id == 0, left[moment, 0:1, :], jnp.where(comp_id == 1, left[moment, 1:2, :], left[moment, 2:3, :])
        )
        high, low = split(pick_row[...] * values)
        return dot(jnp.concatenate([high, low], axis=1), pick_back[...])

    def gather(halves, moment):
        both = dot(halves, pick_lane[...])
        chosen = (both[0:ROWS] + both[ROWS : 2 * ROWS]) * pick_row[...]
        out = jnp.zeros((8, 128), F32)
        for comp in range(3):
            part = jnp.sum(jnp.where(comp_id == comp, chosen, 0.0), axis=0, keepdims=True)
            out = jnp.where(sub8 == comp, part, out)
        record[moment] = out

    def nothing():
        pass

    def sweep(turn, carry):
        first = turn * 6
        data_red, source_red = turn * 2, turn * 2 + 1

        fields[:, 0:HALF] = inject(1)
        fields[:, HALF:WIDE] = jnp.zeros((ROWS, HALF), F32)
        apply_rates(first, lambda: reduce_send(data_red, 0, data_squares()))
        for k in range(5):
            source[1, :, lanes(k)] = gain[:, lanes(k)] * (fields[:, lanes(k)] + 0.5 * rates[:, lanes(k)])
        for block in range(10):
            piece = rates[:, lanes(block)]
            saved[:, lanes(block)] = fields[:, lanes(block)] + piece
            fields[:, lanes(block)] = piece

        def second():
            reduce_send(data_red, 1, reduce_take(data_red, 0))

        apply_rates(first + 1, second)
        fields[:, 0:HALF] = inject(0) + saved[:, 0:HALF] + 0.5 * rates[:, 0:HALF]
        fields[:, HALF:WIDE] = saved[:, HALF:WIDE] + 0.5 * rates[:, HALF:WIDE]

        def third():
            reduce_send(data_red, 2, reduce_take(data_red, 1))

        apply_rates(first + 2, third)
        beta = jnp.sqrt(whole(reduce_take(data_red, 2)))
        inverse = 1.0 / beta
        scalars[turn, 0] = jnp.broadcast_to(beta, (8, 128))
        for k in range(5):
            part = gain[:, lanes(k)] * (fields[:, lanes(k)] + 0.5 * rates[:, lanes(k)])
            part = part * inverse - beta * basis[turn, 0, :, lanes(k)]
            source[0, :, lanes(k)] = part
            source[1, :, lanes(k)] = source[1, :, lanes(k)] * inverse - beta * basis[turn, 1, :, lanes(k)]
            fields[:, lanes(k)] = gain[:, lanes(k)] * part
        fields[:, HALF:WIDE] = jnp.zeros((ROWS, HALF), F32)
        unit[...] = left[...] * inverse

        apply_rates(first + 3, lambda: reduce_send(source_red, 0, source_squares()))
        for block in range(10):
            fields[:, lanes(block)] = fields[:, lanes(block)] + 0.5 * rates[:, lanes(block)]

        def fifth():
            gather(rhs[0:160, 0:HALF], 0)
            reduce_send(source_red, 1, reduce_take(source_red, 0))

        apply_rates(first + 4, fifth)
        for k in range(5):
            drive = gain[:, lanes(k)] * source[1, :, lanes(k)]
            start = fields[:, lanes(k)]
            saved[:, lanes(k)] = start + drive
            fields[:, lanes(k)] = start + 0.5 * (rates[:, lanes(k)] + drive)
            fields[:, lanes(5 + k)] = fields[:, lanes(5 + k)] + 0.5 * rates[:, lanes(5 + k)]

        def sixth():
            reduce_send(source_red, 2, reduce_take(source_red, 1))

        apply_rates(first + 5, sixth)
        halves = split(saved[:, 0:HALF] + rates[:, 0:HALF])
        gather(jnp.concatenate(halves, axis=0), 1)
        alpha = jnp.sqrt(whole(reduce_take(source_red, 2)))
        scalars[turn, 1] = jnp.broadcast_to(alpha, (8, 128))
        inverse = 1.0 / alpha
        for moment in range(2):
            basis[turn + 1, moment] = source[moment] * inverse
            left[moment] = record[moment] * inverse - alpha * unit[moment]
        return carry

    lax.fori_loop(0, 2, sweep, 0)

    reduce_send(4, 0, data_squares())
    for turn in range(2):
        for moment in range(2):
            high, low = split(basis[turn + 1, moment])
            both = dot_nt(jnp.concatenate([high, low], axis=0), order)
            perm[(turn * 2 + moment) * ROWS : (turn * 2 + moment + 1) * ROWS, :] = both[0:ROWS] + both[ROWS : 2 * ROWS]
    reduce_send(4, 1, reduce_take(4, 0))
    reduce_send(4, 2, reduce_take(4, 1))
    beta_3 = jnp.sqrt(whole(reduce_take(4, 2)))
    beta_1, alpha_1 = scalars[0, 0][0:1, :], scalars[0, 1][0:1, :]
    beta_2, alpha_2 = scalars[1, 0][0:1, :], scalars[1, 1][0:1, :]
    rho_1 = jnp.sqrt(alpha_1 * alpha_1 + beta_2 * beta_2)
    cosine, sine = alpha_1 / rho_1, beta_2 / rho_1
    step_1 = cosine * beta_1 / rho_1
    phi_bar = sine * beta_1
    theta = sine * alpha_2
    rho_bar = -cosine * alpha_2
    rho_2 = jnp.sqrt(rho_bar * rho_bar + beta_3 * beta_3)
    step_2 = rho_bar / rho_2 * phi_bar / rho_2
    use_1 = (step_1 - step_2 * theta / rho_1)[:, 0:1]
    use_2 = step_2[:, 0:1]
    use_left = (phi_bar / rho_2)[:, 0:1]
    for moment in range(2):
        res_ref[moment] = (left[moment] * use_left)[0:3, :]
        for comp in range(3):
            for i in range(5):
                at = comp * 25 + i * 5
                one = perm[moment * ROWS + at : moment * ROWS + at + 5, :]
                two = perm[(2 + moment) * ROWS + at : (2 + moment) * ROWS + at + 5, :]
                est_ref[moment, comp, i] = use_1 * one + use_2 * two


def solution(mesh):
    n_gx, n_gy = mesh.shape["gx"], mesh.shape["gy"]
    inner, send_e, send_h, lift, spread, order = tables()

    def shards(probe_data, conductivity, support, face_tags, probe_nodes):
        vmem = pl.BlockSpec(memory_space=pltpu.VMEM)
        smem = pl.BlockSpec(memory_space=pltpu.SMEM)
        return pl.pallas_call(
            functools.partial(kernel, n_gx, n_gy),
            out_shape=(
                jax.ShapeDtypeStruct((2, 3, 5, 5, HALF), F32),
                jax.ShapeDtypeStruct((2, 3, 128), F32),
            ),
            in_specs=[vmem, vmem, vmem, smem] + [vmem] * 7,
            out_specs=(vmem, vmem),
            scratch_shapes=[
                pltpu.VMEM((ROWS, WIDE), F32),
                pltpu.VMEM((ROWS, WIDE), F32),
                pltpu.VMEM((ROWS, WIDE), F32),
                pltpu.VMEM((256, WIDE), BF16),
                pltpu.VMEM((ROWS + 64, WIDE), F32),
                pltpu.VMEM((128, HALF), BF16),
                pltpu.VMEM((ROWS, HALF), F32),
                pltpu.VMEM((ROWS, HALF), F32),
                pltpu.VMEM((ROWS, 128), F32),
                pltpu.VMEM((HALF, 128), BF16),
                pltpu.VMEM((256, HALF), BF16),
                pltpu.VMEM((2, 8, 128), F32),
                pltpu.VMEM((2, 8, 128), F32),
                pltpu.VMEM((2, 8, 128), F32),
                pltpu.VMEM((2, ROWS, HALF), F32),
                pltpu.VMEM((3, 2, ROWS, HALF), F32),
                pltpu.VMEM((2, 2, 8, 128), F32),
                pltpu.VMEM((4 * ROWS, HALF), F32),
                pltpu.VMEM((12, FACES, QROWS, 128), F32),
                pltpu.VMEM((12, FACES, QROWS, 128), F32),
                pltpu.VMEM((5, 3, 8, 1, 128), F32),
                pltpu.SemaphoreType.DMA((12, FACES)),
                pltpu.SemaphoreType.DMA((12, FACES)),
                pltpu.SemaphoreType.DMA((5, 3)),
                pltpu.SemaphoreType.DMA((5, 3)),
            ],
            compiler_params=pltpu.CompilerParams(
                collective_id=0, has_side_effects=True, vmem_limit_bytes=40 * 1024 * 1024
            ),
        )(
            probe_data, conductivity, support, face_tags, probe_nodes.reshape(1, 128),
            jnp.asarray(inner), jnp.asarray(send_e), jnp.asarray(send_h), jnp.asarray(lift), jnp.asarray(spread),
            jnp.asarray(order),
        )

    return jax.shard_map(
        shards,
        mesh=mesh,
        in_specs=(
            P(None, None, ("gx", "gy")),
            P("gx", "gy", None),
            P("gx", "gy", None),
            P(None, "gx", "gy"),
            P(("gx", "gy")),
        ),
        out_specs=(P(None, None, "gx", "gy", None), P(None, None, ("gx", "gy"))),
        check_vma=False,
    )
```

```python
import functools
import math

import jax
import jax.numpy as jnp
import numpy as np
from jax import lax
from jax.experimental import pallas as pl
from jax.experimental.pallas import tpu as pltpu
from jax.sharding import PartitionSpec as P

MESH = pl.DeviceIdType.MESH
F32 = jnp.float32
BF16 = jnp.bfloat16

STEP_SIZE = 0.02
LIFT_HALF = 5.0
DRIVE_GAIN = 50.0
NX_CHIPS = 4
CORES = 2
ROWS = 80
QROWS = 56
HALF = 640
WIDE = 1280
INNER = 144
SENT = 96
FACES = 4
DIAGS = ((-1, -1), (-1, 1), (1, -1), (1, 1))
CHARS = (
    ((1, 2, 1.0), (2, 1, -1.0)),
    ((1, 2, -1.0), (2, 1, 1.0)),
    ((0, 2, -1.0), (2, 0, 1.0)),
    ((0, 2, 1.0), (2, 0, -1.0)),
)
SIDES = ((0, 4, 0), (0, 0, 4), (1, 4, 0), (1, 0, 4))


def lobatto_scaled():
    radical = math.sqrt(3.0 / 7.0)
    points = np.array([-1.0, -radical, 0.0, radical, 1.0])
    legendre = (35.0 * points**4 - 30.0 * points**2 + 3.0) / 8.0
    weights = 0.1 / legendre**2
    matrix = np.zeros((5, 5))
    for i in range(5):
        for j in range(5):
            if i != j:
                matrix[i, j] = legendre[i] / (legendre[j] * (points[i] - points[j]))
    root = np.sqrt(weights)
    return matrix * root[:, None] / root[None, :], root


def row_of(comp, i, j):
    return comp * 25 + 5 * i + j


def split_np(matrix):
    high = np.asarray(matrix, np.float32).astype(jnp.bfloat16)
    low = (np.asarray(matrix, np.float32) - high.astype(np.float32)).astype(jnp.bfloat16)
    return high, low


def tables():
    deriv, root = lobatto_scaled()
    deriv = STEP_SIZE * deriv
    curl = np.zeros((ROWS, ROWS))
    turn = np.zeros((QROWS, ROWS))
    for i in range(5):
        for j in range(5):
            for k in range(5):
                curl[row_of(0, i, j), row_of(2, i, k)] += deriv[j, k]
                curl[row_of(1, i, j), row_of(2, k, j)] -= deriv[i, k]
                curl[row_of(2, i, j), row_of(1, k, j)] += deriv[i, k]
                curl[row_of(2, i, j), row_of(0, i, k)] -= deriv[j, k]
            turn[row_of(0, i, j), row_of(1, i, j)] = 1.0
            turn[row_of(1, i, j), row_of(0, i, j)] = -1.0
    high, low = split_np(curl)
    inner = np.zeros((INNER, 256), np.float32)
    inner[:ROWS, 0:80] = high
    inner[:ROWS, 80:160] = high
    inner[:ROWS, 160:240] = low
    inner[ROWS : ROWS + QROWS, 0:80] = turn
    inner[ROWS : ROWS + QROWS, 80:160] = turn

    send_e = np.zeros((SENT, 256), np.float32)
    send_h = np.zeros((SENT, 256), np.float32)
    lift = np.zeros((2 * ROWS, 256), np.float32)
    corner = np.zeros((128, 256), np.float32)
    slot_weight = np.zeros(64)
    for face in range(FACES):
        axis, node_out, node_in = SIDES[face]
        for slot in range(16):
            char = slot if slot < 8 else 8 + slot % 2
            which, along = char // 5, char % 5
            comp_e, comp_h, sign = CHARS[face][which]
            spot_out = (node_out, along) if axis == 0 else (along, node_out)
            spot_in = (node_in, along) if axis == 0 else (along, node_in)
            at = face * 16 + slot
            slot_weight[at] = root[0] ** 2 * root[along] ** 2
            for part in (0, 80):
                send_e[at, part + row_of(comp_e, *spot_out)] = 1.0
                send_h[at, part + row_of(comp_h, *spot_out)] = sign
            for part in (0, 64):
                lift[row_of(comp_e, *spot_in), part + at] = 1.0
                lift[ROWS + row_of(comp_h, *spot_in), part + at] = sign
            for diag, (side_x, side_y) in enumerate(DIAGS):
                if axis == 0:
                    if side_x != (-1 if face == 0 else 1):
                        continue
                    other, first = (2 if side_y < 0 else 3), 2
                else:
                    if side_y != (-1 if face == 2 else 1):
                        continue
                    other, first = (0 if side_x < 0 else 1), 0
                if along != SIDES[other][2]:
                    continue
                for number, (other_e, other_h, other_sign) in enumerate(CHARS[other]):
                    only_e = float(comp_e == other_e)
                    both = only_e + sign * other_sign * float(comp_h == other_h)
                    for part in (0, 4, 32, 36):
                        column = diag * 8 + first + number + part
                        corner[at, column] = both
                        corner[64 + at, column] = only_e
    for diag, (side_x, side_y) in enumerate(DIAGS):
        spot = (4 if side_x < 0 else 0, 4 if side_y < 0 else 0)
        for slot in range(8):
            face = ((0 if side_x < 0 else 1), (2 if side_y < 0 else 3))[slot % 4 // 2]
            comp_e, comp_h, sign = CHARS[face][slot % 2]
            for part in (0, 80):
                send_e[64 + diag * 8 + slot, part + row_of(comp_e, *spot)] = 1.0
                send_h[64 + diag * 8 + slot, part + row_of(comp_h, *spot)] = sign
    matrices = np.concatenate([inner, send_e, send_h, lift, corner], axis=0)

    columns = np.zeros((ROWS, 128), np.float32)
    strength = STEP_SIZE * LIFT_HALF
    for comp in range(3):
        for i in range(5):
            for j in range(5):
                row = row_of(comp, i, j)
                columns[row, 0] = root[i] * root[j]
                columns[row, 1] = 1.0 / (root[i] * root[j])
                count = (i in (0, 4)) * (comp != 0) + (j in (0, 4)) * (comp != 1)
                columns[row, 2] = strength * count
                columns[row, 3] = strength * (count + (comp != 2))
                columns[row, 4] = strength * (comp != 2)
    columns[0:64, 5] = (DRIVE_GAIN * STEP_SIZE) ** 2 * slot_weight
    return matrices, columns


def split(value):
    high = value.astype(BF16)
    return high, (value - high.astype(F32)).astype(BF16)


def dot(a, b):
    return jnp.dot(a, b, preferred_element_type=F32)


def dot_nt(a, b):
    return lax.dot_general(a, b, (((1,), (1,)), ((), ())), preferred_element_type=F32)


def lanes(block):
    return slice(block * 128, block * 128 + 128)


def kernel(
    n_gx, n_gy, tags_ref, data_hbm, cond_hbm, supp_hbm, nodes_hbm, mats_hbm, cols_hbm, est_ref, res_ref,
    data_ref, cond_ref, supp_ref, nodes_ref, mats_ref, cols_ref, mats, order, spread,
    fields, second, rates, rhs, prod, ghost_rhs, corner_rhs, sig, gain, gain_out, pick_row, pick_lane, pick_back,
    left, source, ortho, perm, perm_out, beside_support,
    send_buf, recv_buf, send_next, recv_next, send_diag, recv_diag, red_buf,
    load_sem, send_sem, recv_sem, next_send_sem, next_recv_sem, diag_send_sem, diag_recv_sem, red_send_sem, red_recv_sem,
    supp_send_sem, supp_recv_sem,
):
    loads = []
    pairs = (
        (data_hbm, data_ref), (nodes_hbm, nodes_ref), (mats_hbm, mats_ref), (cols_hbm, cols_ref),
        (cond_hbm, cond_ref), (supp_hbm, supp_ref),
    )
    for number, (far, near) in enumerate(pairs):
        load = pltpu.make_async_copy(far, near, load_sem.at[number])
        load.start()
        loads.append(load)

    deriv, root = lobatto_scaled()
    deriv = STEP_SIZE * deriv
    gx, gy = lax.axis_index("gx"), lax.axis_index("gy")
    x_at, z_at = lax.rem(gx, NX_CHIPS), lax.div(gx, NX_CHIPS)
    core_at, y_at = lax.rem(gy, CORES), lax.div(gy, CORES)
    n_z, n_y, n_xc = n_gx // NX_CHIPS, n_gy // CORES, NX_CHIPS * CORES
    sizes = (n_xc, n_z, n_y)

    def partner(phase, step):
        if phase == 0:
            spot = lax.rem(x_at * CORES + core_at + step, n_xc)
            return (z_at * NX_CHIPS + lax.div(spot, CORES), y_at * CORES + lax.rem(spot, CORES))
        if phase == 1:
            return (lax.rem(z_at + step, n_z) * NX_CHIPS + x_at, gy)
        return (gx, lax.rem(y_at + step, n_y) * CORES + core_at)

    def near_by(step_x, step_y):
        return (lax.rem(gx + n_gx + step_x, n_gx), lax.rem(gy + n_gy + step_y, n_gy))

    beside = (near_by(1, 0), near_by(-1, 0), near_by(0, 1), near_by(0, -1))
    across = tuple(near_by(-side_x, -side_y) for side_x, side_y in DIAGS)
    strength = STEP_SIZE * LIFT_HALF
    has = {(0, -1): gx > 0, (0, 1): gx < n_gx - 1, (1, -1): gy > 0, (1, 1): gy < n_gy - 1}
    open_faces = tuple(
        jnp.where(has[key], strength, 0.0).astype(F32) for key in ((0, -1), (0, 1), (1, -1), (1, 1))
    )
    open_diags = tuple(
        jnp.where(has[(0, side_x)] & has[(1, side_y)], strength, 0.0).astype(F32) for side_x, side_y in DIAGS
    )

    barrier = pltpu.get_barrier_semaphore()
    greeted = 0
    for device in beside + across:
        pl.semaphore_signal(barrier, inc=1, device_id=device, device_id_type=MESH)
        greeted += 1
    for phase in range(3):
        for step in range(1, sizes[phase]):
            pl.semaphore_signal(barrier, inc=1, device_id=partner(phase, step), device_id_type=MESH)
            greeted += 1

    def remote(src, dst, sem_out, sem_in, device):
        copy = pltpu.make_async_remote_copy(
            src_ref=src, dst_ref=dst, send_sem=sem_out, recv_sem=sem_in, device_id=device, device_id_type=MESH
        )
        copy.start()
        return copy

    z_id = lax.broadcasted_iota(jnp.int32, (HALF, 128), 0)
    five = 5 * lax.broadcasted_iota(jnp.int32, (HALF, 128), 1)
    for k in range(5):
        order[:, lanes(k)] = jnp.where(z_id == five + k, 1.0, 0.0).astype(BF16)
    rhs[240:256, :] = jnp.zeros((16, WIDE), BF16)
    left[...] = jnp.zeros_like(left)
    perm[...] = jnp.zeros_like(perm)
    sub8 = lax.broadcasted_iota(jnp.int32, (8, 128), 0)
    lane56 = lax.broadcasted_iota(jnp.int32, (QROWS, 128), 1)
    lane1 = lax.broadcasted_iota(jnp.int32, (1, 128), 1)
    row_id = lax.broadcasted_iota(jnp.int32, (ROWS, 128), 0)
    comp_id = (row_id >= 25).astype(jnp.int32) + (row_id >= 50).astype(jnp.int32) + (row_id >= 75).astype(jnp.int32)
    spot_id = (row_id - 25 * comp_id).astype(F32)

    for load in loads:
        load.wait()
    mats[...] = mats_ref[...].astype(BF16)
    at_e, at_h, at_lift, at_corner = INNER, INNER + SENT, INNER + 2 * SENT, INNER + 2 * SENT + 2 * ROWS
    inner = mats.at[0:INNER]
    send_e, send_h = mats.at[at_e:at_h], mats.at[at_h:at_lift]
    lift = mats.at[at_lift:at_corner, 0:128]
    for number in range(3):
        spread[number] = jnp.broadcast_to(cols_ref[:, 2 + number : 3 + number], (ROWS, 128))

    node = nodes_ref[...].astype(F32)
    pair = jnp.floor((node + 0.5) * (1.0 / HALF))
    depth = node - float(HALF) * pair
    element = jnp.floor((depth + 0.5) * 0.2)
    inside = depth - 5.0 * element
    weight = jnp.zeros_like(node)
    for k in range(5):
        weight = jnp.where(inside == float(k), float(1.0 / root[k]), weight)
    pick_row[...] = jnp.where(spot_id == pair, cols_ref[:, 1:2] * weight, 0.0)
    sub_id = lax.broadcasted_iota(jnp.int32, (128, 128), 0).astype(F32)
    for k in range(5):
        hot = jnp.where((sub_id == element) & (inside == float(k)), 1.0, 0.0)
        pick_lane[lanes(k), :] = hot.astype(BF16)
        flipped = jnp.transpose(hot).astype(BF16)
        pick_back[0:128, lanes(k)] = flipped
        pick_back[128:256, lanes(k)] = flipped
    for comp in range(3):
        for moment in range(2):
            left[0, moment, comp : comp + 1, :] = data_ref[comp, moment : moment + 1, :]

    tag_low = tags_ref[0, 0, 0].astype(F32)
    tag_high = tags_ref[0, 0, 1].astype(F32)
    for comp in range(3):
        for i in range(5):
            perm[comp * 25 + i * 5 : comp * 25 + i * 5 + 5, :] = cond_ref[i]
    halves = jnp.concatenate(split(perm[0:ROWS, :]), axis=0)
    for k in range(5):
        both = dot(halves, order[:, lanes(k)])
        sig[:, lanes(k)] = STEP_SIZE * (both[0:ROWS] + both[ROWS : 2 * ROWS]) + spread[1 if k in (0, 4) else 0]
    support = supp_ref[0].astype(F32)
    for k in range(5):
        gain[:, lanes(k)] = (-DRIVE_GAIN * STEP_SIZE * float(root[k])) * support * cols_ref[:, 0:1]
    beside_support[4] = support

    pl.semaphore_wait(barrier, greeted)
    support_copies = [
        remote(
            beside_support.at[4], beside_support.at[face], supp_send_sem.at[face], supp_recv_sem.at[face], beside[face]
        )
        for face in range(FACES)
    ]

    def reduce_send(index, phase, row):
        red_buf[index, phase, 0] = row
        for step in range(1, sizes[phase]):
            remote(
                red_buf.at[index, phase, 0], red_buf.at[index, phase, step], red_send_sem.at[index, phase],
                red_recv_sem.at[index, phase], partner(phase, step),
            )

    def reduce_take(index, phase):
        if sizes[phase] == 1:
            return red_buf[index, phase, 0]
        others = red_buf.at[index, phase, pl.ds(1, sizes[phase] - 1)]
        pltpu.make_async_copy(others, others, red_recv_sem.at[index, phase]).wait()
        pltpu.make_async_copy(others, others, red_send_sem.at[index, phase]).wait()
        total = red_buf[index, phase, 0]
        for step in range(1, sizes[phase]):
            total = total + red_buf[index, phase, step]
        return total

    def whole(value):
        return jnp.sum(jnp.sum(value, axis=0, keepdims=True), axis=1, keepdims=True)

    def packed_row(values):
        row = jnp.zeros((1, 128), F32)
        for number, value in enumerate(values):
            row = jnp.where(lane1 == number, value, row)
        return row

    def entry(row, number):
        return jnp.sum(jnp.where(lane1 == number, row, 0.0), axis=1, keepdims=True)

    def data_dot(a, b):
        return whole(a[0] * b[0] + a[1] * b[1])

    def source_dot(a, b):
        total = jnp.zeros((ROWS, 128), F32)
        for moment in range(2):
            for k in range(5):
                total = total + a[moment, :, lanes(k)] * b[moment, :, lanes(k)]
        return whole(total)

    def load_rhs(ref, blocks=10):
        for block in range(blocks):
            high, low = split(ref[:, lanes(block)])
            rhs[0:80, lanes(block)] = high
            rhs[80:160, lanes(block)] = low
            rhs[160:240, lanes(block)] = high

    def own_rates(field, result, halves):
        if len(halves) == 2:
            prod[...] = dot(inner[...], rhs[...])
        else:
            prod[:, HALF:WIDE] = dot(inner[...], rhs[:, HALF:WIDE])
        for half in halves:
            own0, other0 = half * 5, (1 - half) * 5
            sign = 1.0 if half == 0 else -1.0
            for k in range(5):
                slope = None
                for m in range(5):
                    if m != k and abs(deriv[k, m]) > 1e-12:
                        term = float(deriv[k, m]) * prod[80:136, lanes(other0 + m)]
                        slope = term if slope is None else slope + term
                decay = sig[:, lanes(k)] if half == 0 else spread[1 if k in (0, 4) else 0]
                change = sign * prod[0:80, lanes(other0 + k)] - decay * field[:, lanes(own0 + k)]
                upper = change[0:QROWS] - sign * slope
                if k in (0, 4):
                    own_low, turn_low = field[0:QROWS, lanes(own0)], prod[80:136, lanes(other0)]
                    own_high, turn_high = field[0:QROWS, lanes(own0 + 4)], prod[80:136, lanes(other0 + 4)]
                    if half == 1:
                        turn_low, turn_high = -turn_low, -turn_high
                    if k == 0:
                        inward = pltpu.roll(own_high + turn_high, 1, 1)
                        edge = (tag_low * -sign) * (own_low - turn_low)
                        incoming = jnp.where(lane56 == 0, edge, inward)
                    else:
                        inward = pltpu.roll(own_low - turn_low, 127, 1)
                        edge = (tag_high * -sign) * (own_high + turn_high)
                        incoming = jnp.where(lane56 == 127, edge, inward)
                    upper = upper + spread[2][0:QROWS] * incoming
                result[0:QROWS, lanes(own0 + k)] = upper
                result[QROWS:ROWS, lanes(own0 + k)] = change[QROWS:ROWS]

    def pack_face(out, face, buf):
        base = face * 16
        mixed = jnp.zeros((8, 128), F32)
        for k in range(5):
            buf[8 * k : 8 * k + 8, :] = out[base : base + 8, lanes(k)]
            if k < 4:
                mixed = jnp.where((sub8 >= 2 * k) & (sub8 < 2 * k + 2), out[base + 8 : base + 16, lanes(k)], mixed)
        buf[40:48, :] = mixed
        buf[48:56, :] = out[base + 8 : base + 16, lanes(4)]

    def kept(k):
        start = 2 * k if k < 4 else 0
        return (sub8 >= start) & (sub8 < start + 2)

    def unpack_face(buf, k):
        mixed = buf[40:48, :] if k < 4 else buf[48:56, :]
        return jnp.concatenate([buf[8 * k : 8 * k + 8, :], jnp.where(kept(k), mixed, 0.0)], axis=0)

    def set_ghosts(face, k, piece):
        high, low = split(open_faces[face] * piece)
        ghost_rhs[face * 16 : face * 16 + 16, lanes(k)] = high
        ghost_rhs[64 + face * 16 : 64 + face * 16 + 16, lanes(k)] = low

    def stage(slot, early, make_second, late, merge, halves_1, halves_2, masked, share):
        load_rhs(fields)
        out = dot(send_e[...], rhs[:, 0:HALF]) + dot(send_h[...], rhs[:, HALF:WIDE])
        copies = []
        for face in range(FACES):
            pack_face(out, face, send_buf.at[slot, face])
            copies.append(
                remote(
                    send_buf.at[slot, face], recv_buf.at[slot, face], send_sem.at[slot, face], recv_sem.at[slot, face],
                    beside[face],
                )
            )
        corner_copies = []
        for diag in range(4):
            base = 64 + diag * 8
            for tile in range(3):
                piece = out[base : base + 8, lanes(2 * tile)]
                if tile < 2:
                    piece = jnp.where(sub8 < 4, piece, out[base : base + 8, lanes(2 * tile + 1)])
                send_diag[slot, diag, 8 * tile : 8 * tile + 8, :] = piece
            corner_copies.append(
                remote(
                    send_diag.at[slot, diag], recv_diag.at[slot, diag], diag_send_sem.at[slot, diag],
                    diag_recv_sem.at[slot, diag], across[diag],
                )
            )
        early()
        own_rates(fields, rates, halves_1)
        make_second()
        load_rhs(second)
        out = dot(send_e[0:64, :], rhs[:, 0:HALF])
        if not masked:
            out = out + dot(send_h[0:64, :], rhs[:, HALF:WIDE])
        next_copies = []
        for face in range(FACES):
            pack_face(out, face, send_next.at[slot, face])
            next_copies.append(
                remote(
                    send_next.at[slot, face], recv_next.at[slot, face], next_send_sem.at[slot, face],
                    next_recv_sem.at[slot, face], beside[face],
                )
            )
        late()

        for copy in copies:
            copy.wait()
        for face in range(FACES):
            for k in range(5):
                set_ghosts(face, k, unpack_face(recv_buf.at[slot, face], k))
        merge(dot(lift[...], ghost_rhs[...]))
        load_rhs(second)
        own_rates(second, rates, halves_2)

        for copy in corner_copies:
            copy.wait()
        for two in range(2):
            for k in range(5):
                pieces = []
                for diag in (2 * two, 2 * two + 1):
                    tile = recv_diag[slot, diag, 8 * (k // 2) : 8 * (k // 2) + 8, :]
                    tile = jnp.where(sub8 >= 4 if k % 2 else sub8 < 4, tile, 0.0)
                    pieces.append(open_diags[diag] * tile)
                high, low = split(jnp.concatenate(pieces, axis=0))
                corner_rhs[16 * two : 16 * two + 16, lanes(k)] = high
                corner_rhs[32 + 16 * two : 32 + 16 * two + 16, lanes(k)] = low
        start = at_corner + (64 if masked else 0)
        extra = dot(mats[start : start + 64, 0:64], corner_rhs[...])
        for copy in next_copies:
            copy.wait()
        for face in range(FACES):
            for k in range(5):
                piece = extra[face * 16 : face * 16 + 16, lanes(k)]
                piece = jnp.concatenate([piece[0:8], jnp.where(kept(k), piece[8:16], 0.0)], axis=0)
                if masked:
                    piece = piece + strength * unpack_face(send_buf.at[slot, face ^ 1], k)
                    piece = piece * gain_out[face * 16 : face * 16 + 16, lanes(k)]
                set_ghosts(face, k, unpack_face(recv_next.at[slot, face], k) + share * piece)
        if len(halves_2) == 2:
            lifted = dot(lift[...], ghost_rhs[...])
            rates[:, 0:HALF] += lifted[0:ROWS]
            rates[:, HALF:WIDE] += lifted[ROWS : 2 * ROWS]
        else:
            rates[:, 0:HALF] += dot(lift[0:ROWS, :], ghost_rhs[...])

    def inject(turn, moment):
        values = jnp.where(
            comp_id == 0,
            left[turn, moment, 0:1, :],
            jnp.where(comp_id == 1, left[turn, moment, 1:2, :], left[turn, moment, 2:3, :]),
        )
        high, low = split(pick_row[...] * values)
        return dot(jnp.concatenate([high, low], axis=1), pick_back[...])

    def gather(halves, turn, moment):
        both = dot(halves, pick_lane[...])
        chosen = (both[0:ROWS] + both[ROWS : 2 * ROWS]) * pick_row[...]
        out = jnp.zeros((8, 128), F32)
        for comp in range(3):
            part = jnp.sum(jnp.where(comp_id == comp, chosen, 0.0), axis=0, keepdims=True)
            out = jnp.where(sub8 == comp, part, out)
        left[turn, moment] = out

    def nothing():
        pass

    def to_output_order(vector, number):
        for moment in range(2):
            both = dot_nt(jnp.concatenate(split(vector[moment]), axis=0), order[...])
            at = (number * 2 + moment) * ROWS
            perm_out[at : at + ROWS, :] = both[0:ROWS] + both[ROWS : 2 * ROWS]

    every, electric = (0, 1), (0,)

    def sweep(turn, carry):
        fields[:, 0:HALF] = inject(turn, 1)
        fields[:, HALF:WIDE] = jnp.zeros((ROWS, HALF), F32)

        def second_1():
            second[...] = rates[...]

        def merge_1(lifted):
            second[:, 0:HALF] += lifted[0:ROWS]
            second[:, HALF:WIDE] += lifted[ROWS : 2 * ROWS]

        def late_1():
            @pl.when(turn == 1)
            def _():
                reduce_send(0, 1, reduce_take(0, 0))
                to_output_order(source.at[0], 0)

        stage(turn * 3, nothing, second_1, late_1, merge_1, every, every, False, 1.0)
        for k in range(5):
            source[turn, 1, :, lanes(k)] = gain[:, lanes(k)] * (fields[:, lanes(k)] + 0.5 * second[:, lanes(k)])
        fields[:, 0:HALF] = inject(turn, 0) + fields[:, 0:HALF] + second[:, 0:HALF] + 0.5 * rates[:, 0:HALF]
        fields[:, HALF:WIDE] = second[:, HALF:WIDE] + 0.5 * rates[:, HALF:WIDE]

        def second_2():
            for k in range(5):
                amount = gain[:, lanes(k)] * (fields[:, lanes(k)] + 0.5 * rates[:, lanes(k)])
                source[turn, 0, :, lanes(k)] = amount
                second[:, lanes(k)] = gain[:, lanes(k)] * amount
            second[:, HALF:WIDE] = jnp.zeros((ROWS, HALF), F32)

        def merge_2(lifted):
            for k in range(5):
                amount = source[turn, 0, :, lanes(k)] + 0.5 * gain[:, lanes(k)] * lifted[0:ROWS, lanes(k)]
                source[turn, 0, :, lanes(k)] = amount
                second[:, lanes(k)] = gain[:, lanes(k)] * amount

        def late_2():
            @pl.when(turn == 0)
            def _():
                for copy in support_copies:
                    copy.wait()
                for face in range(FACES):
                    for k in range(5):
                        column = float(root[k] ** 2) * cols_ref[face * 16 : face * 16 + 16, 5:6]
                        gain_out[face * 16 : face * 16 + 16, lanes(k)] = column * beside_support[face]

            @pl.when(turn == 1)
            def _():
                reduce_send(0, 2, reduce_take(0, 1))

        stage(turn * 3 + 1, nothing, second_2, late_2, merge_2, electric, every, True, 0.5)
        fields[:, 0:HALF] = second[:, 0:HALF] + 0.5 * rates[:, 0:HALF]
        fields[:, HALF:WIDE] = 0.5 * rates[:, HALF:WIDE]

        def early_3():
            gather(rhs[0:160, 0:HALF], turn + 1, 0)

        def second_3():
            for k in range(5):
                drive = gain[:, lanes(k)] * source[turn, 1, :, lanes(k)]
                second[:, lanes(k)] = fields[:, lanes(k)] + 0.5 * (rates[:, lanes(k)] + drive)
                fields[:, lanes(k)] = fields[:, lanes(k)] + drive
            second[:, HALF:WIDE] = fields[:, HALF:WIDE] + 0.5 * rates[:, HALF:WIDE]

        def merge_3(lifted):
            second[:, 0:HALF] += 0.5 * lifted[0:ROWS]
            second[:, HALF:WIDE] += 0.5 * lifted[ROWS : 2 * ROWS]

        def late_3():
            @pl.when(turn == 0)
            def _():
                reduce_send(
                    0, 0, packed_row([data_dot(left[0], left[0]), source_dot(source.at[0], source.at[0])])
                )

            @pl.when(turn == 1)
            def _():
                norms = reduce_take(0, 2)
                red_buf[0, 0, 0] = norms
                ratio = entry(norms, 1) / entry(norms, 0)
                for moment in range(2):
                    for k in range(5):
                        ortho[moment, :, lanes(k)] = (
                            source[1, moment, :, lanes(k)] - ratio * source[0, moment, :, lanes(k)]
                        )
                to_output_order(ortho, 1)

        stage(turn * 3 + 2, early_3, second_3, late_3, merge_3, every, electric, False, 0.5)
        halves = split(fields[:, 0:HALF] + rates[:, 0:HALF])
        gather(jnp.concatenate(halves, axis=0), turn + 1, 1)
        return carry

    lax.fori_loop(0, 2, sweep, 0)

    norms = red_buf[0, 0, 0]
    sq_b, sq_g = entry(norms, 0), entry(norms, 1)
    ratio = sq_g / sq_b
    for moment in range(2):
        left[0, moment] = left[1, moment] - ratio * left[0, moment]
        left[2, moment] = left[2, moment] - ratio * left[1, moment]
    p, f, h = left[0], left[1], left[2]
    products = [
        data_dot(p, p), source_dot(ortho, ortho), source_dot(ortho, source.at[0]), data_dot(h, h), data_dot(h, f),
        data_dot(f, f), data_dot(h, p), data_dot(f, p),
    ]
    reduce_send(1, 0, packed_row(products))
    reduce_send(1, 1, reduce_take(1, 0))
    reduce_send(1, 2, reduce_take(1, 1))
    total = reduce_take(1, 2)
    pp, oo, og, hh, hf, ff, hp, fp = (entry(total, number) for number in range(8))
    take = pp / sq_g
    sq_q = jnp.maximum(oo - 2.0 * take * og + take * take * sq_g, 0.0)
    beta_1 = jnp.sqrt(sq_b)
    alpha_1 = jnp.sqrt(ratio)
    beta_2 = jnp.sqrt(take)
    alpha_2 = jnp.sqrt(sq_q / pp)
    sq_w = hh - 2.0 * take * hf + take * take * ff
    sq_beta_3 = jnp.maximum(sq_w / sq_q - 2.0 * (hp - take * fp) / pp + sq_q / pp, 0.0)
    rho_1 = jnp.sqrt(alpha_1 * alpha_1 + beta_2 * beta_2)
    cosine, sine = alpha_1 / rho_1, beta_2 / rho_1
    step_1 = cosine * beta_1 / rho_1
    phi_bar = sine * beta_1
    theta = sine * alpha_2
    rho_bar = -cosine * alpha_2
    rho_2 = jnp.sqrt(rho_bar * rho_bar + sq_beta_3)
    step_2 = rho_bar / rho_2 * phi_bar / rho_2
    on_ortho = step_2 / jnp.sqrt(sq_q)
    on_first = (step_1 - step_2 * theta / rho_1) / jnp.sqrt(sq_g) - on_ortho * take
    on_h = phi_bar / rho_2 / jnp.sqrt(sq_q)
    on_p = phi_bar / rho_2 * jnp.sqrt(sq_q) / pp
    for moment in range(2):
        res_ref[moment] = (on_h * (h[moment] - take * f[moment]) - on_p * p[moment])[0:3, :]
        for comp in range(3):
            for i in range(5):
                at = comp * 25 + i * 5
                one = perm_out[moment * ROWS + at : moment * ROWS + at + 5, :]
                two = perm_out[(2 + moment) * ROWS + at : (2 + moment) * ROWS + at + 5, :]
                est_ref[moment, comp, i] = on_first * one + on_ortho * two


def solution(mesh):
    n_gx, n_gy = mesh.shape["gx"], mesh.shape["gy"]
    matrices, columns = tables()

    def shards(probe_data, conductivity, support, face_tags, probe_nodes):
        vmem = pl.BlockSpec(memory_space=pltpu.VMEM)
        smem = pl.BlockSpec(memory_space=pltpu.SMEM)
        anywhere = pl.BlockSpec(memory_space=pl.ANY)
        return pl.pallas_call(
            functools.partial(kernel, n_gx, n_gy),
            out_shape=(
                jax.ShapeDtypeStruct((2, 3, 5, 5, HALF), F32),
                jax.ShapeDtypeStruct((2, 3, 128), F32),
            ),
            in_specs=[smem] + [anywhere] * 6,
            out_specs=(vmem, vmem),
            scratch_shapes=[
                pltpu.VMEM((3, 2, 128), F32),
                pltpu.VMEM((5, 5, HALF), F32),
                pltpu.VMEM((1, 1, 128), jnp.int32),
                pltpu.VMEM((1, 128), jnp.int32),
                pltpu.VMEM(matrices.shape, F32),
                pltpu.VMEM(columns.shape, F32),
                pltpu.VMEM(matrices.shape, BF16),
                pltpu.VMEM((HALF, HALF), BF16),
                pltpu.VMEM((3, ROWS, 128), F32),
                pltpu.VMEM((ROWS, WIDE), F32),
                pltpu.VMEM((ROWS, WIDE), F32),
                pltpu.VMEM((ROWS, WIDE), F32),
                pltpu.VMEM((256, WIDE), BF16),
                pltpu.VMEM((INNER, WIDE), F32),
                pltpu.VMEM((128, HALF), BF16),
                pltpu.VMEM((64, HALF), BF16),
                pltpu.VMEM((ROWS, HALF), F32),
                pltpu.VMEM((ROWS, HALF), F32),
                pltpu.VMEM((64, HALF), F32),
                pltpu.VMEM((ROWS, 128), F32),
                pltpu.VMEM((HALF, 128), BF16),
                pltpu.VMEM((256, HALF), BF16),
                pltpu.VMEM((3, 2, 8, 128), F32),
                pltpu.VMEM((2, 2, ROWS, HALF), F32),
                pltpu.VMEM((2, ROWS, HALF), F32),
                pltpu.VMEM((ROWS, HALF), F32),
                pltpu.VMEM((4 * ROWS, HALF), F32),
                pltpu.VMEM((5, 1, 128), F32),
                pltpu.VMEM((6, FACES, QROWS, 128), F32),
                pltpu.VMEM((6, FACES, QROWS, 128), F32),
                pltpu.VMEM((6, FACES, QROWS, 128), F32),
                pltpu.VMEM((6, FACES, QROWS, 128), F32),
                pltpu.VMEM((6, 4, 24, 128), F32),
                pltpu.VMEM((6, 4, 24, 128), F32),
                pltpu.VMEM((2, 3, 8, 1, 128), F32),
                pltpu.SemaphoreType.DMA((6,)),
                pltpu.SemaphoreType.DMA((6, FACES)),
                pltpu.SemaphoreType.DMA((6, FACES)),
                pltpu.SemaphoreType.DMA((6, FACES)),
                pltpu.SemaphoreType.DMA((6, FACES)),
                pltpu.SemaphoreType.DMA((6, 4)),
                pltpu.SemaphoreType.DMA((6, 4)),
                pltpu.SemaphoreType.DMA((2, 3)),
                pltpu.SemaphoreType.DMA((2, 3)),
                pltpu.SemaphoreType.DMA((FACES,)),
                pltpu.SemaphoreType.DMA((FACES,)),
            ],
            compiler_params=pltpu.CompilerParams(
                collective_id=0, has_side_effects=True, vmem_limit_bytes=56 * 1024 * 1024
            ),
        )(
            jnp.transpose(face_tags, (1, 2, 0)), jnp.transpose(probe_data, (1, 0, 2)), conductivity, support,
            probe_nodes.reshape(1, 128), jnp.asarray(matrices), jnp.asarray(columns),
        )

    return jax.shard_map(
        shards,
        mesh=mesh,
        in_specs=(
            P(None, None, ("gx", "gy")),
            P("gx", "gy", None),
            P("gx", "gy", None),
            P(None, "gx", "gy"),
            P(("gx", "gy")),
        ),
        out_specs=(P(None, None, "gx", "gy", None), P(None, None, ("gx", "gy"))),
        check_vma=False,
    )
```

```python
import functools
import math

import jax
import jax.numpy as jnp
import numpy as np
from jax import lax
from jax.experimental import pallas as pl
from jax.experimental.pallas import tpu as pltpu
from jax.sharding import PartitionSpec as P

MESH = pl.DeviceIdType.MESH
F32 = jnp.float32
BF16 = jnp.bfloat16

STEP_SIZE = 0.02
LIFT_HALF = 5.0
DRIVE_GAIN = 50.0
ROWS = 80
QROWS = 56
HALF = 640
WIDE = 1280
INNER = 144
SENT = 96
FACES = 4
DIAGS = ((-1, -1), (-1, 1), (1, -1), (1, 1))
CHARS = (
    ((1, 2, 1.0), (2, 1, -1.0)),
    ((1, 2, -1.0), (2, 1, 1.0)),
    ((0, 2, -1.0), (2, 0, 1.0)),
    ((0, 2, 1.0), (2, 0, -1.0)),
)
SIDES = ((0, 4, 0), (0, 0, 4), (1, 4, 0), (1, 0, 4))


def lobatto_scaled():
    radical = math.sqrt(3.0 / 7.0)
    points = np.array([-1.0, -radical, 0.0, radical, 1.0])
    legendre = (35.0 * points**4 - 30.0 * points**2 + 3.0) / 8.0
    weights = 0.1 / legendre**2
    matrix = np.zeros((5, 5))
    for i in range(5):
        for j in range(5):
            if i != j:
                matrix[i, j] = legendre[i] / (legendre[j] * (points[i] - points[j]))
    root = np.sqrt(weights)
    return matrix * root[:, None] / root[None, :], root


def row_of(comp, i, j):
    return comp * 25 + 5 * i + j


def split_np(matrix):
    high = np.asarray(matrix, np.float32).astype(jnp.bfloat16)
    low = (np.asarray(matrix, np.float32) - high.astype(np.float32)).astype(jnp.bfloat16)
    return high, low


def tables():
    deriv, root = lobatto_scaled()
    deriv = STEP_SIZE * deriv
    curl = np.zeros((ROWS, ROWS))
    turn = np.zeros((QROWS, ROWS))
    for i in range(5):
        for j in range(5):
            for k in range(5):
                curl[row_of(0, i, j), row_of(2, i, k)] += deriv[j, k]
                curl[row_of(1, i, j), row_of(2, k, j)] -= deriv[i, k]
                curl[row_of(2, i, j), row_of(1, k, j)] += deriv[i, k]
                curl[row_of(2, i, j), row_of(0, i, k)] -= deriv[j, k]
            turn[row_of(0, i, j), row_of(1, i, j)] = 1.0
            turn[row_of(1, i, j), row_of(0, i, j)] = -1.0
    high, low = split_np(curl)
    inner = np.zeros((INNER, 256), np.float32)
    inner[:ROWS, 0:80] = high
    inner[:ROWS, 80:160] = high
    inner[:ROWS, 160:240] = low
    inner[ROWS : ROWS + QROWS, 0:80] = turn
    inner[ROWS : ROWS + QROWS, 80:160] = turn

    send_e = np.zeros((SENT, 256), np.float32)
    send_h = np.zeros((SENT, 256), np.float32)
    lift = np.zeros((2 * ROWS, 256), np.float32)
    corner = np.zeros((128, 256), np.float32)
    slot_weight = np.zeros(64)
    for face in range(FACES):
        axis, node_out, node_in = SIDES[face]
        for slot in range(16):
            char = slot if slot < 8 else 8 + slot % 2
            which, along = char // 5, char % 5
            comp_e, comp_h, sign = CHARS[face][which]
            spot_out = (node_out, along) if axis == 0 else (along, node_out)
            spot_in = (node_in, along) if axis == 0 else (along, node_in)
            at = face * 16 + slot
            slot_weight[at] = root[0] ** 2 * root[along] ** 2
            for part in (0, 80):
                send_e[at, part + row_of(comp_e, *spot_out)] = 1.0
                send_h[at, part + row_of(comp_h, *spot_out)] = sign
            for part in (0, 64):
                lift[row_of(comp_e, *spot_in), part + at] = 1.0
                lift[ROWS + row_of(comp_h, *spot_in), part + at] = sign
            for diag, (side_x, side_y) in enumerate(DIAGS):
                if axis == 0:
                    if side_x != (-1 if face == 0 else 1):
                        continue
                    other, first = (2 if side_y < 0 else 3), 2
                else:
                    if side_y != (-1 if face == 2 else 1):
                        continue
                    other, first = (0 if side_x < 0 else 1), 0
                if along != SIDES[other][2]:
                    continue
                for number, (other_e, other_h, other_sign) in enumerate(CHARS[other]):
                    only_e = float(comp_e == other_e)
                    both = only_e + sign * other_sign * float(comp_h == other_h)
                    for part in (0, 4, 32, 36):
                        column = diag * 8 + first + number + part
                        corner[at, column] = both
                        corner[64 + at, column] = only_e
    for diag, (side_x, side_y) in enumerate(DIAGS):
        spot = (4 if side_x < 0 else 0, 4 if side_y < 0 else 0)
        for slot in range(8):
            face = ((0 if side_x < 0 else 1), (2 if side_y < 0 else 3))[slot % 4 // 2]
            comp_e, comp_h, sign = CHARS[face][slot % 2]
            for part in (0, 80):
                send_e[64 + diag * 8 + slot, part + row_of(comp_e, *spot)] = 1.0
                send_h[64 + diag * 8 + slot, part + row_of(comp_h, *spot)] = sign
    matrices = np.concatenate([inner, send_e, send_h, lift, corner], axis=0)

    columns = np.zeros((ROWS, 128), np.float32)
    strength = STEP_SIZE * LIFT_HALF
    for comp in range(3):
        for i in range(5):
            for j in range(5):
                row = row_of(comp, i, j)
                columns[row, 0] = root[i] * root[j]
                columns[row, 1] = 1.0 / (root[i] * root[j])
                count = (i in (0, 4)) * (comp != 0) + (j in (0, 4)) * (comp != 1)
                columns[row, 2] = strength * count
                columns[row, 3] = strength * (count + (comp != 2))
                columns[row, 4] = strength * (comp != 2)
    columns[0:64, 5] = (DRIVE_GAIN * STEP_SIZE) ** 2 * slot_weight
    return matrices, columns


def split(value):
    high = value.astype(BF16)
    return high, (value - high.astype(F32)).astype(BF16)


def dot(a, b):
    return jnp.dot(a, b, preferred_element_type=F32)


def dot_nt(a, b):
    return lax.dot_general(a, b, (((1,), (1,)), ((), ())), preferred_element_type=F32)


def lanes(block):
    return slice(block * 128, block * 128 + 128)


def kernel(
    n_gx, n_gy, tags_hbm, data_hbm, cond_hbm, supp_hbm, nodes_hbm, mats_hbm, cols_hbm, est_ref, res_ref,
    tags_ref, data_ref, cond_ref, supp_ref, nodes_ref, mats_ref, cols_ref, mats, order, spread,
    fields, second, rates, rhs, prod, ghost_rhs, corner_rhs, sig, gain, gain_out, pick_row, pick_lane, pick_back,
    left, source, ortho, perm, perm_out, beside_support,
    send_buf, recv_buf, send_next, recv_next, send_diag, recv_diag, red_buf,
    load_sem, send_sem, recv_sem, next_send_sem, next_recv_sem, diag_send_sem, diag_recv_sem, red_send_sem, red_recv_sem,
    supp_send_sem, supp_recv_sem,
):
    loads = []
    pairs = (
        (data_hbm, data_ref), (nodes_hbm, nodes_ref), (mats_hbm, mats_ref), (cols_hbm, cols_ref),
        (cond_hbm, cond_ref), (supp_hbm, supp_ref), (tags_hbm, tags_ref),
    )
    for number, (far, near) in enumerate(pairs):
        load = pltpu.make_async_copy(far, near, load_sem.at[number])
        load.start()
        loads.append(load)

    deriv, root = lobatto_scaled()
    deriv = STEP_SIZE * deriv
    gx, gy = lax.axis_index("gx"), lax.axis_index("gy")
    sizes = (n_gx, n_gy)

    def partner(phase, step):
        if phase == 0:
            return (lax.rem(gx + step, n_gx), gy)
        return (gx, lax.rem(gy + step, n_gy))

    def near_by(step_x, step_y):
        return (lax.rem(gx + n_gx + step_x, n_gx), lax.rem(gy + n_gy + step_y, n_gy))

    beside = (near_by(1, 0), near_by(-1, 0), near_by(0, 1), near_by(0, -1))
    across = tuple(near_by(-side_x, -side_y) for side_x, side_y in DIAGS)
    strength = STEP_SIZE * LIFT_HALF
    has = {(0, -1): gx > 0, (0, 1): gx < n_gx - 1, (1, -1): gy > 0, (1, 1): gy < n_gy - 1}
    open_faces = tuple(
        jnp.where(has[key], strength, 0.0).astype(F32) for key in ((0, -1), (0, 1), (1, -1), (1, 1))
    )
    open_diags = tuple(
        jnp.where(has[(0, side_x)] & has[(1, side_y)], strength, 0.0).astype(F32) for side_x, side_y in DIAGS
    )

    barrier = pltpu.get_barrier_semaphore()
    greeted = 0
    for device in across:
        pl.semaphore_signal(barrier, inc=1, device_id=device, device_id_type=MESH)
        greeted += 1
    for phase in range(2):
        for step in range(1, sizes[phase]):
            pl.semaphore_signal(barrier, inc=1, device_id=partner(phase, step), device_id_type=MESH)
            greeted += 1

    def remote(src, dst, sem_out, sem_in, device):
        copy = pltpu.make_async_remote_copy(
            src_ref=src, dst_ref=dst, send_sem=sem_out, recv_sem=sem_in, device_id=device, device_id_type=MESH
        )
        copy.start()
        return copy

    z_id = lax.broadcasted_iota(jnp.int32, (HALF, 128), 0)
    five = 5 * lax.broadcasted_iota(jnp.int32, (HALF, 128), 1)
    for k in range(5):
        order[:, lanes(k)] = jnp.where(z_id == five + k, 1.0, 0.0).astype(BF16)
    rhs[240:256, :] = jnp.zeros((16, WIDE), BF16)
    left[...] = jnp.zeros_like(left)
    perm[...] = jnp.zeros_like(perm)
    sub8 = lax.broadcasted_iota(jnp.int32, (8, 128), 0)
    lane56 = lax.broadcasted_iota(jnp.int32, (QROWS, 128), 1)
    lane1 = lax.broadcasted_iota(jnp.int32, (1, 128), 1)
    row_id = lax.broadcasted_iota(jnp.int32, (ROWS, 128), 0)
    comp_id = (row_id >= 25).astype(jnp.int32) + (row_id >= 50).astype(jnp.int32) + (row_id >= 75).astype(jnp.int32)
    spot_id = (row_id - 25 * comp_id).astype(F32)

    for load in loads:
        load.wait()
    mats[...] = mats_ref[...].astype(BF16)
    at_e, at_h, at_lift, at_corner = INNER, INNER + SENT, INNER + 2 * SENT, INNER + 2 * SENT + 2 * ROWS
    inner = mats.at[0:INNER]
    send_e, send_h = mats.at[at_e:at_h], mats.at[at_h:at_lift]
    lift = mats.at[at_lift:at_corner, 0:128]
    for number in range(3):
        spread[number] = jnp.broadcast_to(cols_ref[:, 2 + number : 3 + number], (ROWS, 128))

    node = nodes_ref[...].astype(F32)
    pair = jnp.floor((node + 0.5) * (1.0 / HALF))
    depth = node - float(HALF) * pair
    element = jnp.floor((depth + 0.5) * 0.2)
    inside = depth - 5.0 * element
    weight = jnp.zeros_like(node)
    for k in range(5):
        weight = jnp.where(inside == float(k), float(1.0 / root[k]), weight)
    pick_row[...] = jnp.where(spot_id == pair, cols_ref[:, 1:2] * weight, 0.0)
    sub_id = lax.broadcasted_iota(jnp.int32, (128, 128), 0).astype(F32)
    for k in range(5):
        hot = jnp.where((sub_id == element) & (inside == float(k)), 1.0, 0.0)
        pick_lane[lanes(k), :] = hot.astype(BF16)
        flipped = jnp.transpose(hot).astype(BF16)
        pick_back[0:128, lanes(k)] = flipped
        pick_back[128:256, lanes(k)] = flipped
    for comp in range(3):
        for moment in range(2):
            left[0, moment, comp : comp + 1, :] = data_ref[comp, moment : moment + 1, :]

    tag_low = tags_ref[0][:, 0:1].astype(F32)
    tag_high = tags_ref[0][:, 1:2].astype(F32)
    for comp in range(3):
        for i in range(5):
            perm[comp * 25 + i * 5 : comp * 25 + i * 5 + 5, :] = cond_ref[i]
    halves = jnp.concatenate(split(perm[0:ROWS, :]), axis=0)
    for k in range(5):
        both = dot(halves, order[:, lanes(k)])
        sig[:, lanes(k)] = STEP_SIZE * (both[0:ROWS] + both[ROWS : 2 * ROWS]) + spread[1 if k in (0, 4) else 0]
    support = supp_ref[0].astype(F32)
    for k in range(5):
        gain[:, lanes(k)] = (-DRIVE_GAIN * STEP_SIZE * float(root[k])) * support * cols_ref[:, 0:1]
    beside_support[4] = support

    pl.semaphore_wait(barrier, greeted)
    support_copies = [
        remote(
            beside_support.at[4], beside_support.at[face], supp_send_sem.at[face], supp_recv_sem.at[face], beside[face]
        )
        for face in range(FACES)
    ]

    def reduce_send(index, phase, row):
        red_buf[index, phase, 0] = row
        for step in range(1, sizes[phase]):
            remote(
                red_buf.at[index, phase, 0], red_buf.at[index, phase, step], red_send_sem.at[index, phase],
                red_recv_sem.at[index, phase], partner(phase, step),
            )

    def reduce_take(index, phase):
        if sizes[phase] == 1:
            return red_buf[index, phase, 0]
        others = red_buf.at[index, phase, pl.ds(1, sizes[phase] - 1)]
        pltpu.make_async_copy(others, others, red_recv_sem.at[index, phase]).wait()
        pltpu.make_async_copy(others, others, red_send_sem.at[index, phase]).wait()
        terms = [red_buf[index, phase, step] for step in range(sizes[phase])]
        while len(terms) > 1:
            terms = [sum(terms[at + 1 : at + 2], terms[at]) for at in range(0, len(terms), 2)]
        return terms[0]

    def whole(value):
        return jnp.sum(jnp.sum(value, axis=0, keepdims=True), axis=1, keepdims=True)

    def packed_row(values):
        row = jnp.zeros((1, 128), F32)
        for number, value in enumerate(values):
            row = jnp.where(lane1 == number, value, row)
        return row

    def entry(row, number):
        return jnp.sum(jnp.where(lane1 == number, row, 0.0), axis=1, keepdims=True)

    def data_dot(a, b):
        return whole(a[0] * b[0] + a[1] * b[1])

    def source_dot(a, b):
        total = jnp.zeros((ROWS, 128), F32)
        for moment in range(2):
            for k in range(5):
                total = total + a[moment, :, lanes(k)] * b[moment, :, lanes(k)]
        return whole(total)

    def load_rhs(ref, magnetic):
        for block in range(10 if magnetic else 5):
            high, low = split(ref[:, lanes(block)])
            rhs[0:80, lanes(block)] = high
            rhs[80:160, lanes(block)] = low
            rhs[160:240, lanes(block)] = high

    def own_rates(field, result, halves, magnetic):
        if not magnetic:
            prod[:, 0:HALF] = dot(inner[...], rhs[:, 0:HALF])
        elif len(halves) == 1:
            prod[:, HALF:WIDE] = dot(inner[...], rhs[:, HALF:WIDE])
        else:
            prod[...] = dot(inner[...], rhs[...])
        for half in halves:
            own0, other0 = half * 5, (1 - half) * 5
            sign = 1.0 if half == 0 else -1.0
            for k in range(5):
                if half == 0 and not magnetic:
                    change = -sig[:, lanes(k)] * field[:, lanes(k)]
                    upper = change[0:QROWS]
                    if k == 0:
                        inward = pltpu.roll(field[0:QROWS, lanes(4)], 1, 1)
                        edge = -tag_low * field[0:QROWS, lanes(0)]
                        upper = upper + spread[2][0:QROWS] * jnp.where(lane56 == 0, edge, inward)
                    elif k == 4:
                        inward = pltpu.roll(field[0:QROWS, lanes(0)], 127, 1)
                        edge = -tag_high * field[0:QROWS, lanes(4)]
                        upper = upper + spread[2][0:QROWS] * jnp.where(lane56 == 127, edge, inward)
                    result[0:QROWS, lanes(k)] = upper
                    result[QROWS:ROWS, lanes(k)] = change[QROWS:ROWS]
                    continue
                slope = None
                for m in range(5):
                    if m != k and abs(deriv[k, m]) > 1e-12:
                        term = float(deriv[k, m]) * prod[80:136, lanes(other0 + m)]
                        slope = term if slope is None else slope + term
                decay = sig[:, lanes(k)] if half == 0 else spread[1 if k in (0, 4) else 0]
                change = sign * prod[0:80, lanes(other0 + k)] - decay * field[:, lanes(own0 + k)]
                upper = change[0:QROWS] - sign * slope
                if k in (0, 4):
                    own_low, turn_low = field[0:QROWS, lanes(own0)], prod[80:136, lanes(other0)]
                    own_high, turn_high = field[0:QROWS, lanes(own0 + 4)], prod[80:136, lanes(other0 + 4)]
                    if half == 1:
                        turn_low, turn_high = -turn_low, -turn_high
                    if k == 0:
                        inward = pltpu.roll(own_high + turn_high, 1, 1)
                        edge = (tag_low * -sign) * (own_low - turn_low)
                        incoming = jnp.where(lane56 == 0, edge, inward)
                    else:
                        inward = pltpu.roll(own_low - turn_low, 127, 1)
                        edge = (tag_high * -sign) * (own_high + turn_high)
                        incoming = jnp.where(lane56 == 127, edge, inward)
                    upper = upper + spread[2][0:QROWS] * incoming
                result[0:QROWS, lanes(own0 + k)] = upper
                result[QROWS:ROWS, lanes(own0 + k)] = change[QROWS:ROWS]

    def pack_face(out, face, buf):
        base = face * 16
        mixed = jnp.zeros((8, 128), F32)
        for k in range(5):
            buf[8 * k : 8 * k + 8, :] = out[base : base + 8, lanes(k)]
            if k < 4:
                mixed = jnp.where((sub8 >= 2 * k) & (sub8 < 2 * k + 2), out[base + 8 : base + 16, lanes(k)], mixed)
        buf[40:48, :] = mixed
        buf[48:56, :] = out[base + 8 : base + 16, lanes(4)]

    def kept(k):
        start = 2 * k if k < 4 else 0
        return (sub8 >= start) & (sub8 < start + 2)

    def unpack_face(buf, k):
        mixed = buf[40:48, :] if k < 4 else buf[48:56, :]
        return jnp.concatenate([buf[8 * k : 8 * k + 8, :], jnp.where(kept(k), mixed, 0.0)], axis=0)

    def set_ghosts(face, k, piece):
        high, low = split(open_faces[face] * piece)
        ghost_rhs[face * 16 : face * 16 + 16, lanes(k)] = high
        ghost_rhs[64 + face * 16 : 64 + face * 16 + 16, lanes(k)] = low

    def stage(slot, early, make_second, late, merge, halves_1, halves_2, magnetic_1, magnetic_2, share):
        load_rhs(fields, magnetic_1)
        out = dot(send_e[...], rhs[:, 0:HALF])
        if magnetic_1:
            out = out + dot(send_h[...], rhs[:, HALF:WIDE])
        copies = []
        for face in range(FACES):
            pack_face(out, face, send_buf.at[slot, face])
            copies.append(
                remote(
                    send_buf.at[slot, face], recv_buf.at[slot, face], send_sem.at[slot, face], recv_sem.at[slot, face],
                    beside[face],
                )
            )
        corner_copies = []
        for diag in range(4):
            base = 64 + diag * 8
            for tile in range(3):
                piece = out[base : base + 8, lanes(2 * tile)]
                if tile < 2:
                    piece = jnp.where(sub8 < 4, piece, out[base : base + 8, lanes(2 * tile + 1)])
                send_diag[slot, diag, 8 * tile : 8 * tile + 8, :] = piece
            corner_copies.append(
                remote(
                    send_diag.at[slot, diag], recv_diag.at[slot, diag], diag_send_sem.at[slot, diag],
                    diag_recv_sem.at[slot, diag], across[diag],
                )
            )
        early()
        own_rates(fields, rates, halves_1, magnetic_1)
        make_second()
        load_rhs(second, magnetic_2)
        out = dot(send_e[0:64, :], rhs[:, 0:HALF])
        if magnetic_2:
            out = out + dot(send_h[0:64, :], rhs[:, HALF:WIDE])
        next_copies = []
        for face in range(FACES):
            pack_face(out, face, send_next.at[slot, face])
            next_copies.append(
                remote(
                    send_next.at[slot, face], recv_next.at[slot, face], next_send_sem.at[slot, face],
                    next_recv_sem.at[slot, face], beside[face],
                )
            )
        late()

        for copy in copies:
            copy.wait()
        for face in range(FACES):
            for k in range(5):
                set_ghosts(face, k, unpack_face(recv_buf.at[slot, face], k))
        merge(dot(lift[...], ghost_rhs[...]))
        load_rhs(second, magnetic_2)
        own_rates(second, rates, halves_2, magnetic_2)

        for copy in corner_copies:
            copy.wait()
        for two in range(2):
            for k in range(5):
                pieces = []
                for diag in (2 * two, 2 * two + 1):
                    tile = recv_diag[slot, diag, 8 * (k // 2) : 8 * (k // 2) + 8, :]
                    tile = jnp.where(sub8 >= 4 if k % 2 else sub8 < 4, tile, 0.0)
                    pieces.append(open_diags[diag] * tile)
                high, low = split(jnp.concatenate(pieces, axis=0))
                corner_rhs[16 * two : 16 * two + 16, lanes(k)] = high
                corner_rhs[32 + 16 * two : 32 + 16 * two + 16, lanes(k)] = low
        start = at_corner + (0 if magnetic_2 else 64)
        extra = dot(mats[start : start + 64, 0:64], corner_rhs[...])
        for copy in next_copies:
            copy.wait()
        for face in range(FACES):
            for k in range(5):
                piece = extra[face * 16 : face * 16 + 16, lanes(k)]
                piece = jnp.concatenate([piece[0:8], jnp.where(kept(k), piece[8:16], 0.0)], axis=0)
                if not magnetic_2:
                    piece = piece + strength * unpack_face(send_buf.at[slot, face ^ 1], k)
                    piece = piece * gain_out[face * 16 : face * 16 + 16, lanes(k)]
                set_ghosts(face, k, unpack_face(recv_next.at[slot, face], k) + share * piece)
        if len(halves_2) == 2:
            lifted = dot(lift[...], ghost_rhs[...])
            rates[:, 0:HALF] += lifted[0:ROWS]
            rates[:, HALF:WIDE] += lifted[ROWS : 2 * ROWS]
        else:
            rates[:, 0:HALF] += dot(lift[0:ROWS, :], ghost_rhs[...])

    def inject(turn, moment):
        values = jnp.where(
            comp_id == 0,
            left[turn, moment, 0:1, :],
            jnp.where(comp_id == 1, left[turn, moment, 1:2, :], left[turn, moment, 2:3, :]),
        )
        high, low = split(pick_row[...] * values)
        return dot(jnp.concatenate([high, low], axis=1), pick_back[...])

    def gather(halves, turn, moment):
        both = dot(halves, pick_lane[...])
        chosen = (both[0:ROWS] + both[ROWS : 2 * ROWS]) * pick_row[...]
        out = jnp.zeros((8, 128), F32)
        for comp in range(3):
            part = jnp.sum(jnp.where(comp_id == comp, chosen, 0.0), axis=0, keepdims=True)
            out = jnp.where(sub8 == comp, part, out)
        left[turn, moment] = out

    def nothing():
        pass

    def to_output_order(vector, number):
        for moment in range(2):
            both = dot_nt(jnp.concatenate(split(vector[moment]), axis=0), order[...])
            at = (number * 2 + moment) * ROWS
            perm_out[at : at + ROWS, :] = both[0:ROWS] + both[ROWS : 2 * ROWS]

    every, electric = (0, 1), (0,)

    def sweep(turn, carry):
        fields[:, 0:HALF] = inject(turn, 1)
        fields[:, HALF:WIDE] = jnp.zeros((ROWS, HALF), F32)

        def second_1():
            second[...] = rates[...]

        def merge_1(lifted):
            second[:, 0:HALF] += lifted[0:ROWS]
            second[:, HALF:WIDE] += lifted[ROWS : 2 * ROWS]

        def late_1():
            @pl.when(turn == 1)
            def _():
                reduce_send(0, 1, reduce_take(0, 0))
                to_output_order(source.at[0], 0)

        stage(turn * 3, nothing, second_1, late_1, merge_1, every, every, False, True, 1.0)
        for k in range(5):
            source[turn, 1, :, lanes(k)] = gain[:, lanes(k)] * (fields[:, lanes(k)] + 0.5 * second[:, lanes(k)])
        fields[:, 0:HALF] = inject(turn, 0) + fields[:, 0:HALF] + second[:, 0:HALF] + 0.5 * rates[:, 0:HALF]
        fields[:, HALF:WIDE] = second[:, HALF:WIDE] + 0.5 * rates[:, HALF:WIDE]

        def second_2():
            for k in range(5):
                amount = gain[:, lanes(k)] * (fields[:, lanes(k)] + 0.5 * rates[:, lanes(k)])
                source[turn, 0, :, lanes(k)] = amount
                second[:, lanes(k)] = gain[:, lanes(k)] * amount
            second[:, HALF:WIDE] = jnp.zeros((ROWS, HALF), F32)

        def merge_2(lifted):
            for k in range(5):
                amount = source[turn, 0, :, lanes(k)] + 0.5 * gain[:, lanes(k)] * lifted[0:ROWS, lanes(k)]
                source[turn, 0, :, lanes(k)] = amount
                second[:, lanes(k)] = gain[:, lanes(k)] * amount

        def late_2():
            @pl.when(turn == 0)
            def _():
                for copy in support_copies:
                    copy.wait()
                for face in range(FACES):
                    for k in range(5):
                        column = float(root[k] ** 2) * cols_ref[face * 16 : face * 16 + 16, 5:6]
                        gain_out[face * 16 : face * 16 + 16, lanes(k)] = column * beside_support[face]

        stage(turn * 3 + 1, nothing, second_2, late_2, merge_2, electric, every, True, False, 0.5)
        fields[:, 0:HALF] = second[:, 0:HALF] + 0.5 * rates[:, 0:HALF]
        fields[:, HALF:WIDE] = 0.5 * rates[:, HALF:WIDE]

        def early_3():
            gather(rhs[0:160, 0:HALF], turn + 1, 0)

        def second_3():
            for k in range(5):
                drive = gain[:, lanes(k)] * source[turn, 1, :, lanes(k)]
                second[:, lanes(k)] = fields[:, lanes(k)] + 0.5 * (rates[:, lanes(k)] + drive)
                fields[:, lanes(k)] = fields[:, lanes(k)] + drive
            second[:, HALF:WIDE] = fields[:, HALF:WIDE] + 0.5 * rates[:, HALF:WIDE]

        def merge_3(lifted):
            second[:, 0:HALF] += 0.5 * lifted[0:ROWS]
            second[:, HALF:WIDE] += 0.5 * lifted[ROWS : 2 * ROWS]

        def late_3():
            @pl.when(turn == 0)
            def _():
                reduce_send(
                    0, 0, packed_row([data_dot(left[0], left[0]), source_dot(source.at[0], source.at[0])])
                )

            @pl.when(turn == 1)
            def _():
                norms = reduce_take(0, 1)
                red_buf[0, 0, 0] = norms
                ratio = entry(norms, 1) / entry(norms, 0)
                for moment in range(2):
                    for k in range(5):
                        ortho[moment, :, lanes(k)] = (
                            source[1, moment, :, lanes(k)] - ratio * source[0, moment, :, lanes(k)]
                        )
                to_output_order(ortho, 1)

        stage(turn * 3 + 2, early_3, second_3, late_3, merge_3, every, electric, True, True, 0.5)
        halves = split(fields[:, 0:HALF] + rates[:, 0:HALF])
        gather(jnp.concatenate(halves, axis=0), turn + 1, 1)
        return carry

    lax.fori_loop(0, 2, sweep, 0)

    norms = red_buf[0, 0, 0]
    sq_b, sq_g = entry(norms, 0), entry(norms, 1)
    ratio = sq_g / sq_b
    for moment in range(2):
        left[0, moment] = left[1, moment] - ratio * left[0, moment]
        left[2, moment] = left[2, moment] - ratio * left[1, moment]
    p, f, h = left[0], left[1], left[2]
    products = [
        data_dot(p, p), source_dot(ortho, ortho), source_dot(ortho, source.at[0]), data_dot(h, h), data_dot(h, f),
        data_dot(f, f), data_dot(h, p), data_dot(f, p),
    ]
    reduce_send(1, 0, packed_row(products))
    reduce_send(1, 1, reduce_take(1, 0))
    total = reduce_take(1, 1)
    pp, oo, og, hh, hf, ff, hp, fp = (entry(total, number) for number in range(8))
    take = pp / sq_g
    sq_q = jnp.maximum(oo - 2.0 * take * og + take * take * sq_g, 0.0)
    beta_1 = jnp.sqrt(sq_b)
    alpha_1 = jnp.sqrt(ratio)
    beta_2 = jnp.sqrt(take)
    alpha_2 = jnp.sqrt(sq_q / pp)
    sq_w = hh - 2.0 * take * hf + take * take * ff
    sq_beta_3 = jnp.maximum(sq_w / sq_q - 2.0 * (hp - take * fp) / pp + sq_q / pp, 0.0)
    rho_1 = jnp.sqrt(alpha_1 * alpha_1 + beta_2 * beta_2)
    cosine, sine = alpha_1 / rho_1, beta_2 / rho_1
    step_1 = cosine * beta_1 / rho_1
    phi_bar = sine * beta_1
    theta = sine * alpha_2
    rho_bar = -cosine * alpha_2
    rho_2 = jnp.sqrt(rho_bar * rho_bar + sq_beta_3)
    step_2 = rho_bar / rho_2 * phi_bar / rho_2
    on_ortho = step_2 / jnp.sqrt(sq_q)
    on_first = (step_1 - step_2 * theta / rho_1) / jnp.sqrt(sq_g) - on_ortho * take
    on_h = phi_bar / rho_2 / jnp.sqrt(sq_q)
    on_p = phi_bar / rho_2 * jnp.sqrt(sq_q) / pp
    for moment in range(2):
        res_ref[moment] = (on_h * (h[moment] - take * f[moment]) - on_p * p[moment])[0:3, :]
        for comp in range(3):
            for i in range(5):
                at = comp * 25 + i * 5
                one = perm_out[moment * ROWS + at : moment * ROWS + at + 5, :]
                two = perm_out[(2 + moment) * ROWS + at : (2 + moment) * ROWS + at + 5, :]
                est_ref[moment, comp, i] = on_first * one + on_ortho * two


def solution(mesh):
    n_gx, n_gy = mesh.shape["gx"], mesh.shape["gy"]
    matrices, columns = tables()

    def shards(probe_data, conductivity, support, face_tags, probe_nodes):
        vmem = pl.BlockSpec(memory_space=pltpu.VMEM)
        anywhere = pl.BlockSpec(memory_space=pl.ANY)
        return pl.pallas_call(
            functools.partial(kernel, n_gx, n_gy),
            out_shape=(
                jax.ShapeDtypeStruct((2, 3, 5, 5, HALF), F32),
                jax.ShapeDtypeStruct((2, 3, 128), F32),
            ),
            in_specs=[anywhere] * 7,
            out_specs=(vmem, vmem),
            scratch_shapes=[
                pltpu.VMEM((1, 1, 2), jnp.int32),
                pltpu.VMEM((3, 2, 128), F32),
                pltpu.VMEM((5, 5, HALF), F32),
                pltpu.VMEM((1, 1, 128), jnp.int32),
                pltpu.VMEM((1, 128), jnp.int32),
                pltpu.VMEM(matrices.shape, F32),
                pltpu.VMEM(columns.shape, F32),
                pltpu.VMEM(matrices.shape, BF16),
                pltpu.VMEM((HALF, HALF), BF16),
                pltpu.VMEM((3, ROWS, 128), F32),
                pltpu.VMEM((ROWS, WIDE), F32),
                pltpu.VMEM((ROWS, WIDE), F32),
                pltpu.VMEM((ROWS, WIDE), F32),
                pltpu.VMEM((256, WIDE), BF16),
                pltpu.VMEM((INNER, WIDE), F32),
                pltpu.VMEM((128, HALF), BF16),
                pltpu.VMEM((64, HALF), BF16),
                pltpu.VMEM((ROWS, HALF), F32),
                pltpu.VMEM((ROWS, HALF), F32),
                pltpu.VMEM((64, HALF), F32),
                pltpu.VMEM((ROWS, 128), F32),
                pltpu.VMEM((HALF, 128), BF16),
                pltpu.VMEM((256, HALF), BF16),
                pltpu.VMEM((3, 2, 8, 128), F32),
                pltpu.VMEM((2, 2, ROWS, HALF), F32),
                pltpu.VMEM((2, ROWS, HALF), F32),
                pltpu.VMEM((ROWS, HALF), F32),
                pltpu.VMEM((4 * ROWS, HALF), F32),
                pltpu.VMEM((5, 1, 128), F32),
                pltpu.VMEM((6, FACES, QROWS, 128), F32),
                pltpu.VMEM((6, FACES, QROWS, 128), F32),
                pltpu.VMEM((6, FACES, QROWS, 128), F32),
                pltpu.VMEM((6, FACES, QROWS, 128), F32),
                pltpu.VMEM((6, 4, 24, 128), F32),
                pltpu.VMEM((6, 4, 24, 128), F32),
                pltpu.VMEM((2, 2, max(n_gx, n_gy), 1, 128), F32),
                pltpu.SemaphoreType.DMA((7,)),
                pltpu.SemaphoreType.DMA((6, FACES)),
                pltpu.SemaphoreType.DMA((6, FACES)),
                pltpu.SemaphoreType.DMA((6, FACES)),
                pltpu.SemaphoreType.DMA((6, FACES)),
                pltpu.SemaphoreType.DMA((6, 4)),
                pltpu.SemaphoreType.DMA((6, 4)),
                pltpu.SemaphoreType.DMA((2, 2)),
                pltpu.SemaphoreType.DMA((2, 2)),
                pltpu.SemaphoreType.DMA((FACES,)),
                pltpu.SemaphoreType.DMA((FACES,)),
            ],
            compiler_params=pltpu.CompilerParams(
                collective_id=0, has_side_effects=True, vmem_limit_bytes=22 * 1024 * 1024
            ),
        )(
            jnp.transpose(face_tags, (1, 2, 0)), jnp.transpose(probe_data, (1, 0, 2)), conductivity, support,
            probe_nodes.reshape(1, 128), jnp.asarray(matrices), jnp.asarray(columns),
        )

    return jax.shard_map(
        shards,
        mesh=mesh,
        in_specs=(
            P(None, None, ("gx", "gy")),
            P("gx", "gy", None),
            P("gx", "gy", None),
            P(None, "gx", "gy"),
            P(("gx", "gy")),
        ),
        out_specs=(P(None, None, "gx", "gy", None), P(None, None, ("gx", "gy"))),
        check_vma=False,
    )
```

```python
import functools
import math

import jax
import jax.numpy as jnp
import numpy as np
from jax import lax
from jax.experimental import pallas as pl
from jax.experimental.pallas import tpu as pltpu
from jax.sharding import PartitionSpec as P

MESH = pl.DeviceIdType.MESH
F32 = jnp.float32
BF16 = jnp.bfloat16

STEP_SIZE = 0.02
LIFT_HALF = 5.0
DRIVE_GAIN = 50.0
ROWS = 80
QROWS = 56
HALF = 640
WIDE = 1280
INNER = 144
SENT = 96
FACES = 4
DIAGS = ((-1, -1), (-1, 1), (1, -1), (1, 1))
CHARS = (
    ((1, 2, 1.0), (2, 1, -1.0)),
    ((1, 2, -1.0), (2, 1, 1.0)),
    ((0, 2, -1.0), (2, 0, 1.0)),
    ((0, 2, 1.0), (2, 0, -1.0)),
)
SIDES = ((0, 4, 0), (0, 0, 4), (1, 4, 0), (1, 0, 4))


def lobatto_scaled():
    radical = math.sqrt(3.0 / 7.0)
    points = np.array([-1.0, -radical, 0.0, radical, 1.0])
    legendre = (35.0 * points**4 - 30.0 * points**2 + 3.0) / 8.0
    weights = 0.1 / legendre**2
    matrix = np.zeros((5, 5))
    for i in range(5):
        for j in range(5):
            if i != j:
                matrix[i, j] = legendre[i] / (legendre[j] * (points[i] - points[j]))
    root = np.sqrt(weights)
    return matrix * root[:, None] / root[None, :], root


def row_of(comp, i, j):
    return comp * 25 + 5 * i + j


def split_np(matrix):
    high = np.asarray(matrix, np.float32).astype(jnp.bfloat16)
    low = (np.asarray(matrix, np.float32) - high.astype(np.float32)).astype(jnp.bfloat16)
    return high, low


def tables():
    deriv, root = lobatto_scaled()
    deriv = STEP_SIZE * deriv
    curl = np.zeros((ROWS, ROWS))
    turn = np.zeros((QROWS, ROWS))
    for i in range(5):
        for j in range(5):
            for k in range(5):
                curl[row_of(0, i, j), row_of(2, i, k)] += deriv[j, k]
                curl[row_of(1, i, j), row_of(2, k, j)] -= deriv[i, k]
                curl[row_of(2, i, j), row_of(1, k, j)] += deriv[i, k]
                curl[row_of(2, i, j), row_of(0, i, k)] -= deriv[j, k]
            turn[row_of(0, i, j), row_of(1, i, j)] = 1.0
            turn[row_of(1, i, j), row_of(0, i, j)] = -1.0
    high, low = split_np(curl)
    inner = np.zeros((INNER, 256), np.float32)
    inner[:ROWS, 0:80] = high
    inner[:ROWS, 80:160] = high
    inner[:ROWS, 160:240] = low
    inner[ROWS : ROWS + QROWS, 0:80] = turn
    inner[ROWS : ROWS + QROWS, 80:160] = turn

    send_e = np.zeros((SENT, 256), np.float32)
    send_h = np.zeros((SENT, 256), np.float32)
    lift = np.zeros((2 * ROWS, 256), np.float32)
    corner = np.zeros((128, 256), np.float32)
    slot_weight = np.zeros(64)
    for face in range(FACES):
        axis, node_out, node_in = SIDES[face]
        for slot in range(16):
            char = slot if slot < 8 else 8 + slot % 2
            which, along = char // 5, char % 5
            comp_e, comp_h, sign = CHARS[face][which]
            spot_out = (node_out, along) if axis == 0 else (along, node_out)
            spot_in = (node_in, along) if axis == 0 else (along, node_in)
            at = face * 16 + slot
            slot_weight[at] = root[0] ** 2 * root[along] ** 2
            for part in (0, 80):
                send_e[at, part + row_of(comp_e, *spot_out)] = 1.0
                send_h[at, part + row_of(comp_h, *spot_out)] = sign
            for part in (0, 64):
                lift[row_of(comp_e, *spot_in), part + at] = 1.0
                lift[ROWS + row_of(comp_h, *spot_in), part + at] = sign
            for diag, (side_x, side_y) in enumerate(DIAGS):
                if axis == 0:
                    if side_x != (-1 if face == 0 else 1):
                        continue
                    other, first = (2 if side_y < 0 else 3), 2
                else:
                    if side_y != (-1 if face == 2 else 1):
                        continue
                    other, first = (0 if side_x < 0 else 1), 0
                if along != SIDES[other][2]:
                    continue
                for number, (other_e, other_h, other_sign) in enumerate(CHARS[other]):
                    only_e = float(comp_e == other_e)
                    both = only_e + sign * other_sign * float(comp_h == other_h)
                    for part in (0, 4, 32, 36):
                        column = diag * 8 + first + number + part
                        corner[at, column] = both
                        corner[64 + at, column] = only_e
    for diag, (side_x, side_y) in enumerate(DIAGS):
        spot = (4 if side_x < 0 else 0, 4 if side_y < 0 else 0)
        for slot in range(8):
            face = ((0 if side_x < 0 else 1), (2 if side_y < 0 else 3))[slot % 4 // 2]
            comp_e, comp_h, sign = CHARS[face][slot % 2]
            for part in (0, 80):
                send_e[64 + diag * 8 + slot, part + row_of(comp_e, *spot)] = 1.0
                send_h[64 + diag * 8 + slot, part + row_of(comp_h, *spot)] = sign
    matrices = np.concatenate([inner, send_e, send_h, lift, corner], axis=0)

    columns = np.zeros((ROWS, 128), np.float32)
    strength = STEP_SIZE * LIFT_HALF
    for comp in range(3):
        for i in range(5):
            for j in range(5):
                row = row_of(comp, i, j)
                columns[row, 0] = root[i] * root[j]
                columns[row, 1] = 1.0 / (root[i] * root[j])
                count = (i in (0, 4)) * (comp != 0) + (j in (0, 4)) * (comp != 1)
                columns[row, 2] = strength * count
                columns[row, 3] = strength * (count + (comp != 2))
                columns[row, 4] = strength * (comp != 2)
    columns[0:64, 5] = (DRIVE_GAIN * STEP_SIZE) ** 2 * slot_weight
    return matrices, columns


def split(value):
    high = value.astype(BF16)
    return high, (value - high.astype(F32)).astype(BF16)


def dot(a, b):
    return jnp.dot(a, b, preferred_element_type=F32)


def dot_nt(a, b):
    return lax.dot_general(a, b, (((1,), (1,)), ((), ())), preferred_element_type=F32)


def lanes(block):
    return slice(block * 128, block * 128 + 128)


def kernel(
    n_gx, n_gy, tags_hbm, data_hbm, cond_hbm, supp_hbm, nodes_hbm, mats_hbm, cols_hbm, est_ref, res_ref,
    tags_ref, data_ref, cond_ref, supp_ref, nodes_ref, mats_ref, cols_ref, mats, order, spread,
    fields, second, rates, rhs, prod, ghost_rhs, corner_rhs, sig, gain, gain_out, pick_row, pick_lane, pick_back,
    left, source, ortho, perm, perm_out, beside_support,
    send_buf, recv_buf, send_next, recv_next, send_diag, recv_diag, red_buf,
    load_sem, send_sem, recv_sem, next_send_sem, next_recv_sem, diag_send_sem, diag_recv_sem, red_send_sem, red_recv_sem,
    supp_send_sem, supp_recv_sem,
):
    loads = []
    pairs = (
        (data_hbm, data_ref), (nodes_hbm, nodes_ref), (mats_hbm, mats_ref), (cols_hbm, cols_ref),
        (cond_hbm, cond_ref), (supp_hbm, supp_ref), (tags_hbm, tags_ref),
    )
    for number, (far, near) in enumerate(pairs):
        load = pltpu.make_async_copy(far, near, load_sem.at[number])
        load.start()
        loads.append(load)

    deriv, root = lobatto_scaled()
    deriv = STEP_SIZE * deriv
    gx, gy = lax.axis_index("gx"), lax.axis_index("gy")
    sizes = (n_gx, n_gy)

    def partner(phase, step):
        if phase == 0:
            return (lax.rem(gx + step, n_gx), gy)
        return (gx, lax.rem(gy + step, n_gy))

    def near_by(step_x, step_y):
        return (lax.rem(gx + n_gx + step_x, n_gx), lax.rem(gy + n_gy + step_y, n_gy))

    beside = (near_by(1, 0), near_by(-1, 0), near_by(0, 1), near_by(0, -1))
    across = tuple(near_by(-side_x, -side_y) for side_x, side_y in DIAGS)
    strength = STEP_SIZE * LIFT_HALF
    has = {(0, -1): gx > 0, (0, 1): gx < n_gx - 1, (1, -1): gy > 0, (1, 1): gy < n_gy - 1}
    open_faces = tuple(
        jnp.where(has[key], strength, 0.0).astype(F32) for key in ((0, -1), (0, 1), (1, -1), (1, 1))
    )
    open_diags = tuple(
        jnp.where(has[(0, side_x)] & has[(1, side_y)], strength, 0.0).astype(F32) for side_x, side_y in DIAGS
    )

    barrier = pltpu.get_barrier_semaphore()
    greeted = 0
    for device in across:
        pl.semaphore_signal(barrier, inc=1, device_id=device, device_id_type=MESH)
        greeted += 1
    for phase in range(2):
        for step in range(1, sizes[phase]):
            pl.semaphore_signal(barrier, inc=1, device_id=partner(phase, step), device_id_type=MESH)
            greeted += 1

    def remote(src, dst, sem_out, sem_in, device):
        copy = pltpu.make_async_remote_copy(
            src_ref=src, dst_ref=dst, send_sem=sem_out, recv_sem=sem_in, device_id=device, device_id_type=MESH
        )
        copy.start()
        return copy

    z_id = lax.broadcasted_iota(jnp.int32, (HALF, 128), 0)
    five = 5 * lax.broadcasted_iota(jnp.int32, (HALF, 128), 1)
    for k in range(5):
        order[:, lanes(k)] = jnp.where(z_id == five + k, 1.0, 0.0).astype(BF16)
    rhs[240:256, :] = jnp.zeros((16, WIDE), BF16)
    left[...] = jnp.zeros_like(left)
    perm[...] = jnp.zeros_like(perm)
    sub8 = lax.broadcasted_iota(jnp.int32, (8, 128), 0)
    lane56 = lax.broadcasted_iota(jnp.int32, (QROWS, 128), 1)
    lane1 = lax.broadcasted_iota(jnp.int32, (1, 128), 1)
    row_id = lax.broadcasted_iota(jnp.int32, (ROWS, 128), 0)
    comp_id = (row_id >= 25).astype(jnp.int32) + (row_id >= 50).astype(jnp.int32) + (row_id >= 75).astype(jnp.int32)
    spot_id = (row_id - 25 * comp_id).astype(F32)

    for load in loads:
        load.wait()
    mats[...] = mats_ref[...].astype(BF16)
    at_e, at_h, at_lift, at_corner = INNER, INNER + SENT, INNER + 2 * SENT, INNER + 2 * SENT + 2 * ROWS
    inner = mats.at[0:INNER]
    send_e, send_h = mats.at[at_e:at_h], mats.at[at_h:at_lift]
    lift = mats.at[at_lift:at_corner, 0:128]
    for number in range(3):
        spread[number] = jnp.broadcast_to(cols_ref[:, 2 + number : 3 + number], (ROWS, 128))

    node = nodes_ref[...].astype(F32)
    pair = jnp.floor((node + 0.5) * (1.0 / HALF))
    depth = node - float(HALF) * pair
    element = jnp.floor((depth + 0.5) * 0.2)
    inside = depth - 5.0 * element
    weight = jnp.zeros_like(node)
    for k in range(5):
        weight = jnp.where(inside == float(k), float(1.0 / root[k]), weight)
    pick_row[...] = jnp.where(spot_id == pair, cols_ref[:, 1:2] * weight, 0.0)
    sub_id = lax.broadcasted_iota(jnp.int32, (128, 128), 0).astype(F32)
    for k in range(5):
        hot = jnp.where((sub_id == element) & (inside == float(k)), 1.0, 0.0)
        pick_lane[lanes(k), :] = hot.astype(BF16)
        flipped = jnp.transpose(hot).astype(BF16)
        pick_back[0:128, lanes(k)] = flipped
        pick_back[128:256, lanes(k)] = flipped
    for comp in range(3):
        for moment in range(2):
            left[0, moment, comp : comp + 1, :] = data_ref[comp, moment : moment + 1, :]

    tag_low = tags_ref[0][:, 0:1].astype(F32)
    tag_high = tags_ref[0][:, 1:2].astype(F32)
    for comp in range(3):
        for i in range(5):
            perm[comp * 25 + i * 5 : comp * 25 + i * 5 + 5, :] = cond_ref[i]
    halves = jnp.concatenate(split(perm[0:ROWS, :]), axis=0)
    for k in range(5):
        both = dot(halves, order[:, lanes(k)])
        sig[:, lanes(k)] = STEP_SIZE * (both[0:ROWS] + both[ROWS : 2 * ROWS]) + spread[1 if k in (0, 4) else 0]
    support = supp_ref[0].astype(F32)
    for k in range(5):
        gain[:, lanes(k)] = (-DRIVE_GAIN * STEP_SIZE * float(root[k])) * support * cols_ref[:, 0:1]
    beside_support[4] = support

    pl.semaphore_wait(barrier, greeted)
    support_copies = [
        remote(
            beside_support.at[4], beside_support.at[face], supp_send_sem.at[face], supp_recv_sem.at[face], beside[face]
        )
        for face in range(FACES)
    ]

    def reduce_send(index, phase, row):
        red_buf[index, phase, 0] = row
        for step in range(1, sizes[phase]):
            remote(
                red_buf.at[index, phase, 0], red_buf.at[index, phase, step], red_send_sem.at[index, phase],
                red_recv_sem.at[index, phase], partner(phase, step),
            )

    def reduce_take(index, phase):
        if sizes[phase] == 1:
            return red_buf[index, phase, 0]
        others = red_buf.at[index, phase, pl.ds(1, sizes[phase] - 1)]
        pltpu.make_async_copy(others, others, red_recv_sem.at[index, phase]).wait()
        pltpu.make_async_copy(others, others, red_send_sem.at[index, phase]).wait()
        terms = [red_buf[index, phase, step] for step in range(sizes[phase])]
        while len(terms) > 1:
            terms = [sum(terms[at + 1 : at + 2], terms[at]) for at in range(0, len(terms), 2)]
        return terms[0]

    def whole(value):
        return jnp.sum(jnp.sum(value, axis=0, keepdims=True), axis=1, keepdims=True)

    def packed_row(values):
        row = jnp.zeros((1, 128), F32)
        for number, value in enumerate(values):
            row = jnp.where(lane1 == number, value, row)
        return row

    def entry(row, number):
        return jnp.sum(jnp.where(lane1 == number, row, 0.0), axis=1, keepdims=True)

    def data_dot(a, b):
        return whole(a[0] * b[0] + a[1] * b[1])

    def source_dot(a, b):
        total = jnp.zeros((ROWS, 128), F32)
        for moment in range(2):
            for k in range(5):
                total = total + a[moment, :, lanes(k)] * b[moment, :, lanes(k)]
        return whole(total)

    def load_rhs(ref, magnetic):
        for block in range(10 if magnetic else 5):
            high, low = split(ref[:, lanes(block)])
            rhs[0:80, lanes(block)] = high
            rhs[80:160, lanes(block)] = low
            rhs[160:240, lanes(block)] = high

    def own_rates(field, result, halves, magnetic):
        if not magnetic:
            prod[:, 0:HALF] = dot(inner[...], rhs[:, 0:HALF])
        elif len(halves) == 1:
            prod[:, HALF:WIDE] = dot(inner[...], rhs[:, HALF:WIDE])
        else:
            prod[...] = dot(inner[...], rhs[...])
        for half in halves:
            own0, other0 = half * 5, (1 - half) * 5
            sign = 1.0 if half == 0 else -1.0
            for k in range(5):
                if half == 0 and not magnetic:
                    change = -sig[:, lanes(k)] * field[:, lanes(k)]
                    upper = change[0:QROWS]
                    if k == 0:
                        inward = pltpu.roll(field[0:QROWS, lanes(4)], 1, 1)
                        edge = -tag_low * field[0:QROWS, lanes(0)]
                        upper = upper + spread[2][0:QROWS] * jnp.where(lane56 == 0, edge, inward)
                    elif k == 4:
                        inward = pltpu.roll(field[0:QROWS, lanes(0)], 127, 1)
                        edge = -tag_high * field[0:QROWS, lanes(4)]
                        upper = upper + spread[2][0:QROWS] * jnp.where(lane56 == 127, edge, inward)
                    result[0:QROWS, lanes(k)] = upper
                    result[QROWS:ROWS, lanes(k)] = change[QROWS:ROWS]
                    continue
                slope = None
                for m in range(5):
                    if m != k and abs(deriv[k, m]) > 1e-12:
                        term = float(deriv[k, m]) * prod[80:136, lanes(other0 + m)]
                        slope = term if slope is None else slope + term
                decay = sig[:, lanes(k)] if half == 0 else spread[1 if k in (0, 4) else 0]
                change = sign * prod[0:80, lanes(other0 + k)] - decay * field[:, lanes(own0 + k)]
                upper = change[0:QROWS] - sign * slope
                if k in (0, 4):
                    own_low, turn_low = field[0:QROWS, lanes(own0)], prod[80:136, lanes(other0)]
                    own_high, turn_high = field[0:QROWS, lanes(own0 + 4)], prod[80:136, lanes(other0 + 4)]
                    if half == 1:
                        turn_low, turn_high = -turn_low, -turn_high
                    if k == 0:
                        inward = pltpu.roll(own_high + turn_high, 1, 1)
                        edge = (tag_low * -sign) * (own_low - turn_low)
                        incoming = jnp.where(lane56 == 0, edge, inward)
                    else:
                        inward = pltpu.roll(own_low - turn_low, 127, 1)
                        edge = (tag_high * -sign) * (own_high + turn_high)
                        incoming = jnp.where(lane56 == 127, edge, inward)
                    upper = upper + spread[2][0:QROWS] * incoming
                result[0:QROWS, lanes(own0 + k)] = upper
                result[QROWS:ROWS, lanes(own0 + k)] = change[QROWS:ROWS]

    def pack_face(out, face, buf):
        base = face * 16
        mixed = jnp.zeros((8, 128), F32)
        for k in range(5):
            buf[8 * k : 8 * k + 8, :] = out[base : base + 8, lanes(k)]
            if k < 4:
                mixed = jnp.where((sub8 >= 2 * k) & (sub8 < 2 * k + 2), out[base + 8 : base + 16, lanes(k)], mixed)
        buf[40:48, :] = mixed
        buf[48:56, :] = out[base + 8 : base + 16, lanes(4)]

    def kept(k):
        start = 2 * k if k < 4 else 0
        return (sub8 >= start) & (sub8 < start + 2)

    def unpack_face(buf, k):
        mixed = buf[40:48, :] if k < 4 else buf[48:56, :]
        return jnp.concatenate([buf[8 * k : 8 * k + 8, :], jnp.where(kept(k), mixed, 0.0)], axis=0)

    def set_ghosts(face, k, piece):
        high, low = split(open_faces[face] * piece)
        ghost_rhs[face * 16 : face * 16 + 16, lanes(k)] = high
        ghost_rhs[64 + face * 16 : 64 + face * 16 + 16, lanes(k)] = low

    def stage(slot, early, make_second, late, merge, halves_1, halves_2, magnetic_1, magnetic_2, share):
        load_rhs(fields, magnetic_1)
        out = dot(send_e[...], rhs[:, 0:HALF])
        if magnetic_1:
            out = out + dot(send_h[...], rhs[:, HALF:WIDE])
        copies = []
        for face in range(FACES):
            pack_face(out, face, send_buf.at[slot, face])
            copies.append(
                remote(
                    send_buf.at[slot, face], recv_buf.at[slot, face], send_sem.at[slot, face], recv_sem.at[slot, face],
                    beside[face],
                )
            )
        corner_copies = []
        for diag in range(4):
            base = 64 + diag * 8
            for tile in range(3):
                piece = out[base : base + 8, lanes(2 * tile)]
                if tile < 2:
                    piece = jnp.where(sub8 < 4, piece, out[base : base + 8, lanes(2 * tile + 1)])
                send_diag[slot, diag, 8 * tile : 8 * tile + 8, :] = piece
            corner_copies.append(
                remote(
                    send_diag.at[slot, diag], recv_diag.at[slot, diag], diag_send_sem.at[slot, diag],
                    diag_recv_sem.at[slot, diag], across[diag],
                )
            )
        early()
        own_rates(fields, rates, halves_1, magnetic_1)
        make_second()
        load_rhs(second, magnetic_2)
        out = dot(send_e[0:64, :], rhs[:, 0:HALF])
        if magnetic_2:
            out = out + dot(send_h[0:64, :], rhs[:, HALF:WIDE])
        next_copies = []
        for face in range(FACES):
            pack_face(out, face, send_next.at[slot, face])
            next_copies.append(
                remote(
                    send_next.at[slot, face], recv_next.at[slot, face], next_send_sem.at[slot, face],
                    next_recv_sem.at[slot, face], beside[face],
                )
            )
        late()

        for copy in copies:
            copy.wait()
        for face in range(FACES):
            for k in range(5):
                set_ghosts(face, k, unpack_face(recv_buf.at[slot, face], k))
        merge(dot(lift[...], ghost_rhs[...]))
        load_rhs(second, magnetic_2)
        own_rates(second, rates, halves_2, magnetic_2)

        for copy in corner_copies:
            copy.wait()
        for two in range(2):
            for k in range(5):
                pieces = []
                for diag in (2 * two, 2 * two + 1):
                    tile = recv_diag[slot, diag, 8 * (k // 2) : 8 * (k // 2) + 8, :]
                    tile = jnp.where(sub8 >= 4 if k % 2 else sub8 < 4, tile, 0.0)
                    pieces.append(open_diags[diag] * tile)
                high, low = split(jnp.concatenate(pieces, axis=0))
                corner_rhs[16 * two : 16 * two + 16, lanes(k)] = high
                corner_rhs[32 + 16 * two : 32 + 16 * two + 16, lanes(k)] = low
        start = at_corner + (0 if magnetic_2 else 64)
        extra = dot(mats[start : start + 64, 0:64], corner_rhs[...])
        for copy in next_copies:
            copy.wait()
        for face in range(FACES):
            for k in range(5):
                piece = extra[face * 16 : face * 16 + 16, lanes(k)]
                piece = jnp.concatenate([piece[0:8], jnp.where(kept(k), piece[8:16], 0.0)], axis=0)
                if not magnetic_2:
                    piece = piece + strength * unpack_face(send_buf.at[slot, face ^ 1], k)
                    piece = piece * gain_out[face * 16 : face * 16 + 16, lanes(k)]
                set_ghosts(face, k, unpack_face(recv_next.at[slot, face], k) + share * piece)
        if len(halves_2) == 2:
            lifted = dot(lift[...], ghost_rhs[...])
            rates[:, 0:HALF] += lifted[0:ROWS]
            rates[:, HALF:WIDE] += lifted[ROWS : 2 * ROWS]
        else:
            rates[:, 0:HALF] += dot(lift[0:ROWS, :], ghost_rhs[...])

    def inject(turn, moment):
        values = jnp.where(
            comp_id == 0,
            left[turn, moment, 0:1, :],
            jnp.where(comp_id == 1, left[turn, moment, 1:2, :], left[turn, moment, 2:3, :]),
        )
        high, low = split(pick_row[...] * values)
        return dot(jnp.concatenate([high, low], axis=1), pick_back[...])

    def gather(halves, turn, moment):
        both = dot(halves, pick_lane[...])
        chosen = (both[0:ROWS] + both[ROWS : 2 * ROWS]) * pick_row[...]
        out = jnp.zeros((8, 128), F32)
        for comp in range(3):
            part = jnp.sum(jnp.where(comp_id == comp, chosen, 0.0), axis=0, keepdims=True)
            out = jnp.where(sub8 == comp, part, out)
        left[turn, moment] = out

    def nothing():
        pass

    def to_output_order(vector, number):
        for moment in range(2):
            both = dot_nt(jnp.concatenate(split(vector[moment]), axis=0), order[...])
            at = (number * 2 + moment) * ROWS
            perm_out[at : at + ROWS, :] = both[0:ROWS] + both[ROWS : 2 * ROWS]

    every, electric = (0, 1), (0,)

    def sweep(turn, carry):
        fields[:, 0:HALF] = inject(turn, 1)
        fields[:, HALF:WIDE] = jnp.zeros((ROWS, HALF), F32)

        def second_1():
            second[...] = rates[...]

        def merge_1(lifted):
            second[:, 0:HALF] += lifted[0:ROWS]
            second[:, HALF:WIDE] += lifted[ROWS : 2 * ROWS]

        def late_1():
            @pl.when(turn == 1)
            def _():
                reduce_send(0, 1, reduce_take(0, 0))
                to_output_order(source.at[0], 0)

        stage(turn * 3, nothing, second_1, late_1, merge_1, every, every, False, True, 1.0)
        for k in range(5):
            source[turn, 1, :, lanes(k)] = gain[:, lanes(k)] * (fields[:, lanes(k)] + 0.5 * second[:, lanes(k)])
        fields[:, 0:HALF] = inject(turn, 0) + fields[:, 0:HALF] + second[:, 0:HALF] + 0.5 * rates[:, 0:HALF]
        fields[:, HALF:WIDE] = second[:, HALF:WIDE] + 0.5 * rates[:, HALF:WIDE]

        def second_2():
            for k in range(5):
                amount = gain[:, lanes(k)] * (fields[:, lanes(k)] + 0.5 * rates[:, lanes(k)])
                source[turn, 0, :, lanes(k)] = amount
                second[:, lanes(k)] = gain[:, lanes(k)] * amount
            second[:, HALF:WIDE] = jnp.zeros((ROWS, HALF), F32)

        def merge_2(lifted):
            for k in range(5):
                amount = source[turn, 0, :, lanes(k)] + 0.5 * gain[:, lanes(k)] * lifted[0:ROWS, lanes(k)]
                source[turn, 0, :, lanes(k)] = amount
                second[:, lanes(k)] = gain[:, lanes(k)] * amount

        def late_2():
            @pl.when(turn == 0)
            def _():
                for copy in support_copies:
                    copy.wait()
                for face in range(FACES):
                    for k in range(5):
                        column = float(root[k] ** 2) * cols_ref[face * 16 : face * 16 + 16, 5:6]
                        gain_out[face * 16 : face * 16 + 16, lanes(k)] = column * beside_support[face]

        stage(turn * 3 + 1, nothing, second_2, late_2, merge_2, electric, every, True, False, 0.5)
        fields[:, 0:HALF] = second[:, 0:HALF] + 0.5 * rates[:, 0:HALF]
        fields[:, HALF:WIDE] = 0.5 * rates[:, HALF:WIDE]

        def early_3():
            gather(rhs[0:160, 0:HALF], turn + 1, 0)

        def second_3():
            for k in range(5):
                drive = gain[:, lanes(k)] * source[turn, 1, :, lanes(k)]
                second[:, lanes(k)] = fields[:, lanes(k)] + 0.5 * (rates[:, lanes(k)] + drive)
                fields[:, lanes(k)] = fields[:, lanes(k)] + drive
            second[:, HALF:WIDE] = fields[:, HALF:WIDE] + 0.5 * rates[:, HALF:WIDE]

        def merge_3(lifted):
            second[:, 0:HALF] += 0.5 * lifted[0:ROWS]
            second[:, HALF:WIDE] += 0.5 * lifted[ROWS : 2 * ROWS]

        def late_3():
            @pl.when(turn == 0)
            def _():
                reduce_send(
                    0, 0, packed_row([data_dot(left[0], left[0]), source_dot(source.at[0], source.at[0])])
                )

            @pl.when(turn == 1)
            def _():
                norms = reduce_take(0, 1)
                red_buf[0, 0, 0] = norms
                ratio = entry(norms, 1) / entry(norms, 0)
                for moment in range(2):
                    for k in range(5):
                        ortho[moment, :, lanes(k)] = (
                            source[1, moment, :, lanes(k)] - ratio * source[0, moment, :, lanes(k)]
                        )
                to_output_order(ortho, 1)

        stage(turn * 3 + 2, early_3, second_3, late_3, merge_3, every, electric, True, True, 0.5)
        halves = split(fields[:, 0:HALF] + rates[:, 0:HALF])
        gather(jnp.concatenate(halves, axis=0), turn + 1, 1)
        return carry

    lax.fori_loop(0, 2, sweep, 0)

    norms = red_buf[0, 0, 0]
    sq_b, sq_g = entry(norms, 0), entry(norms, 1)
    ratio = sq_g / sq_b
    for moment in range(2):
        left[0, moment] = left[1, moment] - ratio * left[0, moment]
        left[2, moment] = left[2, moment] - ratio * left[1, moment]
    p, f, h = left[0], left[1], left[2]
    products = [
        data_dot(p, p), source_dot(ortho, ortho), source_dot(ortho, source.at[0]), data_dot(h, h), data_dot(h, f),
        data_dot(f, f), data_dot(h, p), data_dot(f, p),
    ]
    reduce_send(1, 0, packed_row(products))
    reduce_send(1, 1, reduce_take(1, 0))
    total = reduce_take(1, 1)
    pp, oo, og, hh, hf, ff, hp, fp = (entry(total, number) for number in range(8))
    take = pp / sq_g
    sq_q = jnp.maximum(oo - 2.0 * take * og + take * take * sq_g, 0.0)
    beta_1 = jnp.sqrt(sq_b)
    alpha_1 = jnp.sqrt(ratio)
    beta_2 = jnp.sqrt(take)
    alpha_2 = jnp.sqrt(sq_q / pp)
    sq_w = hh - 2.0 * take * hf + take * take * ff
    sq_beta_3 = jnp.maximum(sq_w / sq_q - 2.0 * (hp - take * fp) / pp + sq_q / pp, 0.0)
    rho_1 = jnp.sqrt(alpha_1 * alpha_1 + beta_2 * beta_2)
    cosine, sine = alpha_1 / rho_1, beta_2 / rho_1
    step_1 = cosine * beta_1 / rho_1
    phi_bar = sine * beta_1
    theta = sine * alpha_2
    rho_bar = -cosine * alpha_2
    rho_2 = jnp.sqrt(rho_bar * rho_bar + sq_beta_3)
    step_2 = rho_bar / rho_2 * phi_bar / rho_2
    on_ortho = step_2 / jnp.sqrt(sq_q)
    on_first = (step_1 - step_2 * theta / rho_1) / jnp.sqrt(sq_g) - on_ortho * take
    on_h = phi_bar / rho_2 / jnp.sqrt(sq_q)
    on_p = phi_bar / rho_2 * jnp.sqrt(sq_q) / pp
    for moment in range(2):
        res_ref[moment] = (on_h * (h[moment] - take * f[moment]) - on_p * p[moment])[0:3, :]
        for comp in range(3):
            for i in range(5):
                at = comp * 25 + i * 5
                one = perm_out[moment * ROWS + at : moment * ROWS + at + 5, :]
                two = perm_out[(2 + moment) * ROWS + at : (2 + moment) * ROWS + at + 5, :]
                est_ref[moment, comp, i] = on_first * one + on_ortho * two


def solution(mesh):
    n_gx, n_gy = mesh.shape["gx"], mesh.shape["gy"]
    matrices, columns = tables()

    def shards(probe_data, conductivity, support, face_tags, probe_nodes):
        vmem = pl.BlockSpec(memory_space=pltpu.VMEM)
        anywhere = pl.BlockSpec(memory_space=pl.ANY)
        return pl.pallas_call(
            functools.partial(kernel, n_gx, n_gy),
            out_shape=(
                jax.ShapeDtypeStruct((2, 3, 5, 5, HALF), F32),
                jax.ShapeDtypeStruct((2, 3, 128), F32),
            ),
            in_specs=[anywhere] * 7,
            out_specs=(vmem, vmem),
            scratch_shapes=[
                pltpu.VMEM((1, 1, 2), jnp.int32),
                pltpu.VMEM((3, 2, 128), F32),
                pltpu.VMEM((5, 5, HALF), F32),
                pltpu.VMEM((1, 1, 128), jnp.int32),
                pltpu.VMEM((1, 128), jnp.int32),
                pltpu.VMEM(matrices.shape, F32),
                pltpu.VMEM(columns.shape, F32),
                pltpu.VMEM(matrices.shape, BF16),
                pltpu.VMEM((HALF, HALF), BF16),
                pltpu.VMEM((3, ROWS, 128), F32),
                pltpu.VMEM((ROWS, WIDE), F32),
                pltpu.VMEM((ROWS, WIDE), F32),
                pltpu.VMEM((ROWS, WIDE), F32),
                pltpu.VMEM((256, WIDE), BF16),
                pltpu.VMEM((INNER, WIDE), F32),
                pltpu.VMEM((128, HALF), BF16),
                pltpu.VMEM((64, HALF), BF16),
                pltpu.VMEM((ROWS, HALF), F32),
                pltpu.VMEM((ROWS, HALF), F32),
                pltpu.VMEM((64, HALF), F32),
                pltpu.VMEM((ROWS, 128), F32),
                pltpu.VMEM((HALF, 128), BF16),
                pltpu.VMEM((256, HALF), BF16),
                pltpu.VMEM((3, 2, 8, 128), F32),
                pltpu.VMEM((2, 2, ROWS, HALF), F32),
                pltpu.VMEM((2, ROWS, HALF), F32),
                pltpu.VMEM((ROWS, HALF), F32),
                pltpu.VMEM((4 * ROWS, HALF), F32),
                pltpu.VMEM((5, 1, 128), F32),
                pltpu.VMEM((6, FACES, QROWS, 128), F32),
                pltpu.VMEM((6, FACES, QROWS, 128), F32),
                pltpu.VMEM((6, FACES, QROWS, 128), F32),
                pltpu.VMEM((6, FACES, QROWS, 128), F32),
                pltpu.VMEM((6, 4, 24, 128), F32),
                pltpu.VMEM((6, 4, 24, 128), F32),
                pltpu.VMEM((2, 2, max(n_gx, n_gy), 1, 128), F32),
                pltpu.SemaphoreType.DMA((7,)),
                pltpu.SemaphoreType.DMA((6, FACES)),
                pltpu.SemaphoreType.DMA((6, FACES)),
                pltpu.SemaphoreType.DMA((6, FACES)),
                pltpu.SemaphoreType.DMA((6, FACES)),
                pltpu.SemaphoreType.DMA((6, 4)),
                pltpu.SemaphoreType.DMA((6, 4)),
                pltpu.SemaphoreType.DMA((2, 2)),
                pltpu.SemaphoreType.DMA((2, 2)),
                pltpu.SemaphoreType.DMA((FACES,)),
                pltpu.SemaphoreType.DMA((FACES,)),
            ],
            compiler_params=pltpu.CompilerParams(
                collective_id=0, has_side_effects=True, vmem_limit_bytes=22 * 1024 * 1024
            ),
        )(
            *(
                pltpu.with_memory_space_constraint(array, pltpu.HBM)
                for array in (
                    jnp.transpose(face_tags, (1, 2, 0)), jnp.transpose(probe_data, (1, 0, 2)), conductivity, support,
                    probe_nodes.reshape(1, 128), jnp.asarray(matrices), jnp.asarray(columns),
                )
            )
        )

    return jax.shard_map(
        shards,
        mesh=mesh,
        in_specs=(
            P(None, None, ("gx", "gy")),
            P("gx", "gy", None),
            P("gx", "gy", None),
            P(None, "gx", "gy"),
            P(("gx", "gy")),
        ),
        out_specs=(P(None, None, "gx", "gy", None), P(None, None, ("gx", "gy"))),
        check_vma=False,
    )
```

```python
import functools
import math

import jax
import jax.numpy as jnp
import numpy as np
from jax import lax
from jax.experimental import pallas as pl
from jax.experimental.pallas import tpu as pltpu
from jax.sharding import PartitionSpec as P

MESH = pl.DeviceIdType.MESH
F32 = jnp.float32
BF16 = jnp.bfloat16

STEP_SIZE = 0.02
LIFT_HALF = 5.0
DRIVE_GAIN = 50.0
ROWS = 80
QROWS = 56
HALF = 640
WIDE = 1280
INNER = 144
SENT = 96
FACES = 4
DIAGS = ((-1, -1), (-1, 1), (1, -1), (1, 1))
CHARS = (
    ((1, 2, 1.0), (2, 1, -1.0)),
    ((1, 2, -1.0), (2, 1, 1.0)),
    ((0, 2, -1.0), (2, 0, 1.0)),
    ((0, 2, 1.0), (2, 0, -1.0)),
)
SIDES = ((0, 4, 0), (0, 0, 4), (1, 4, 0), (1, 0, 4))


def lobatto_scaled():
    radical = math.sqrt(3.0 / 7.0)
    points = np.array([-1.0, -radical, 0.0, radical, 1.0])
    legendre = (35.0 * points**4 - 30.0 * points**2 + 3.0) / 8.0
    weights = 0.1 / legendre**2
    matrix = np.zeros((5, 5))
    for i in range(5):
        for j in range(5):
            if i != j:
                matrix[i, j] = legendre[i] / (legendre[j] * (points[i] - points[j]))
    root = np.sqrt(weights)
    return matrix * root[:, None] / root[None, :], root


def row_of(comp, i, j):
    return comp * 25 + 5 * i + j


def split_np(matrix):
    high = np.asarray(matrix, np.float32).astype(jnp.bfloat16)
    low = (np.asarray(matrix, np.float32) - high.astype(np.float32)).astype(jnp.bfloat16)
    return high, low


def tables():
    deriv, root = lobatto_scaled()
    deriv = STEP_SIZE * deriv
    curl = np.zeros((ROWS, ROWS))
    turn = np.zeros((QROWS, ROWS))
    for i in range(5):
        for j in range(5):
            for k in range(5):
                curl[row_of(0, i, j), row_of(2, i, k)] += deriv[j, k]
                curl[row_of(1, i, j), row_of(2, k, j)] -= deriv[i, k]
                curl[row_of(2, i, j), row_of(1, k, j)] += deriv[i, k]
                curl[row_of(2, i, j), row_of(0, i, k)] -= deriv[j, k]
            turn[row_of(0, i, j), row_of(1, i, j)] = 1.0
            turn[row_of(1, i, j), row_of(0, i, j)] = -1.0
    high, low = split_np(curl)
    inner = np.zeros((INNER, 256), np.float32)
    inner[:ROWS, 0:80] = high
    inner[:ROWS, 80:160] = high
    inner[:ROWS, 160:240] = low
    inner[ROWS : ROWS + QROWS, 0:80] = turn
    inner[ROWS : ROWS + QROWS, 80:160] = turn

    send_e = np.zeros((SENT, 256), np.float32)
    send_h = np.zeros((SENT, 256), np.float32)
    lift = np.zeros((2 * ROWS, 256), np.float32)
    corner = np.zeros((128, 256), np.float32)
    slot_weight = np.zeros(64)
    for face in range(FACES):
        axis, node_out, node_in = SIDES[face]
        for slot in range(16):
            char = slot if slot < 8 else 8 + slot % 2
            which, along = char // 5, char % 5
            comp_e, comp_h, sign = CHARS[face][which]
            spot_out = (node_out, along) if axis == 0 else (along, node_out)
            spot_in = (node_in, along) if axis == 0 else (along, node_in)
            at = face * 16 + slot
            slot_weight[at] = root[0] ** 2 * root[along] ** 2
            for part in (0, 80):
                send_e[at, part + row_of(comp_e, *spot_out)] = 1.0
                send_h[at, part + row_of(comp_h, *spot_out)] = sign
            for part in (0, 64):
                lift[row_of(comp_e, *spot_in), part + at] = 1.0
                lift[ROWS + row_of(comp_h, *spot_in), part + at] = sign
            for diag, (side_x, side_y) in enumerate(DIAGS):
                if axis == 0:
                    if side_x != (-1 if face == 0 else 1):
                        continue
                    other, first = (2 if side_y < 0 else 3), 2
                else:
                    if side_y != (-1 if face == 2 else 1):
                        continue
                    other, first = (0 if side_x < 0 else 1), 0
                if along != SIDES[other][2]:
                    continue
                for number, (other_e, other_h, other_sign) in enumerate(CHARS[other]):
                    only_e = float(comp_e == other_e)
                    both = only_e + sign * other_sign * float(comp_h == other_h)
                    for part in (0, 4, 32, 36):
                        column = diag * 8 + first + number + part
                        corner[at, column] = both
                        corner[64 + at, column] = only_e
    for diag, (side_x, side_y) in enumerate(DIAGS):
        spot = (4 if side_x < 0 else 0, 4 if side_y < 0 else 0)
        for slot in range(8):
            face = ((0 if side_x < 0 else 1), (2 if side_y < 0 else 3))[slot % 4 // 2]
            comp_e, comp_h, sign = CHARS[face][slot % 2]
            for part in (0, 80):
                send_e[64 + diag * 8 + slot, part + row_of(comp_e, *spot)] = 1.0
                send_h[64 + diag * 8 + slot, part + row_of(comp_h, *spot)] = sign
    matrices = np.concatenate([inner, send_e, send_h, lift, corner], axis=0)

    columns = np.zeros((ROWS, 128), np.float32)
    strength = STEP_SIZE * LIFT_HALF
    for comp in range(3):
        for i in range(5):
            for j in range(5):
                row = row_of(comp, i, j)
                columns[row, 0] = root[i] * root[j]
                columns[row, 1] = 1.0 / (root[i] * root[j])
                count = (i in (0, 4)) * (comp != 0) + (j in (0, 4)) * (comp != 1)
                columns[row, 2] = strength * count
                columns[row, 3] = strength * (count + (comp != 2))
                columns[row, 4] = strength * (comp != 2)
    columns[0:64, 5] = (DRIVE_GAIN * STEP_SIZE) ** 2 * slot_weight
    return matrices, columns


def split(value):
    high = value.astype(BF16)
    return high, (value - high.astype(F32)).astype(BF16)


def dot(a, b):
    return jnp.dot(a, b, preferred_element_type=F32)


def dot_nt(a, b):
    return lax.dot_general(a, b, (((1,), (1,)), ((), ())), preferred_element_type=F32)


def lanes(block):
    return slice(block * 128, block * 128 + 128)


def kernel(
    n_gx, n_gy, tags_hbm, data_hbm, cond_hbm, supp_hbm, nodes_hbm, mats_hbm, cols_hbm, est_ref, res_ref,
    tags_ref, data_ref, cond_ref, supp_ref, nodes_ref, mats_ref, cols_ref, mats, order, spread,
    fields, second, rates, rhs, prod, ghost_rhs, corner_rhs, sig, gain, gain_out, pick_row, pick_lane, pick_back,
    left, source, ortho, perm, perm_out, beside_support, own_support,
    send_buf, recv_buf, send_next, recv_next, send_diag, recv_diag, red_buf,
    load_sem, send_sem, recv_sem, next_send_sem, next_recv_sem, diag_send_sem, diag_recv_sem, red_send_sem, red_recv_sem,
    supp_send_sem, supp_recv_sem, meet_sem,
):
    loads = []
    pairs = (
        (data_hbm, data_ref), (nodes_hbm, nodes_ref), (mats_hbm, mats_ref), (cols_hbm, cols_ref),
        (cond_hbm, cond_ref), (supp_hbm, supp_ref), (tags_hbm, tags_ref),
    )
    for number, (far, near) in enumerate(pairs):
        load = pltpu.make_async_copy(far, near, load_sem.at[number])
        load.start()
        loads.append(load)

    deriv, root = lobatto_scaled()
    deriv = STEP_SIZE * deriv
    gx, gy = lax.axis_index("gx"), lax.axis_index("gy")
    sizes = (n_gx, n_gy)

    def partner(phase, step):
        if phase == 0:
            return (lax.rem(gx + step, n_gx), gy)
        return (gx, lax.rem(gy + step, n_gy))

    def near_by(step_x, step_y):
        return (lax.rem(gx + n_gx + step_x, n_gx), lax.rem(gy + n_gy + step_y, n_gy))

    beside = (near_by(1, 0), near_by(-1, 0), near_by(0, 1), near_by(0, -1))
    across = tuple(near_by(-side_x, -side_y) for side_x, side_y in DIAGS)
    strength = STEP_SIZE * LIFT_HALF
    has = {(0, -1): gx > 0, (0, 1): gx < n_gx - 1, (1, -1): gy > 0, (1, 1): gy < n_gy - 1}
    to_face = tuple(has[key] for key in ((0, 1), (0, -1), (1, 1), (1, -1)))
    to_diag = tuple(has[(0, -side_x)] & has[(1, -side_y)] for side_x, side_y in DIAGS)

    for face in range(FACES):

        @pl.when(jnp.logical_not(to_face[face ^ 1]))
        def _():
            for slot in range(6):
                recv_buf[slot, face] = jnp.zeros((QROWS, 128), F32)
                recv_next[slot, face] = jnp.zeros((QROWS, 128), F32)
            beside_support[face] = jnp.zeros((1, 128), F32)

    for diag in range(4):

        @pl.when(jnp.logical_not(to_diag[3 - diag]))
        def _():
            for slot in range(6):
                recv_diag[slot, diag] = jnp.zeros((24, 128), F32)

    barrier = pltpu.get_barrier_semaphore()
    greeted = jnp.int32(0)
    for device, exists in zip(beside + across, to_face + to_diag):

        @pl.when(exists)
        def _():
            pl.semaphore_signal(barrier, inc=1, device_id=device, device_id_type=MESH)

        greeted = greeted + exists.astype(jnp.int32)

    def remote(src, dst, sem_out, sem_in, device):
        copy = pltpu.make_async_remote_copy(
            src_ref=src, dst_ref=dst, send_sem=sem_out, recv_sem=sem_in, device_id=device, device_id_type=MESH
        )
        return copy

    def start(copy, exists):
        @pl.when(exists)
        def _():
            copy.start()

    def wait_all(copies, exist, flip):
        for number, exists in enumerate(exist):
            back = number ^ flip

            @pl.when(exists)
            def _():
                copies[number].wait_send()
                copies[back].wait_recv()

    z_id = lax.broadcasted_iota(jnp.int32, (HALF, 128), 0)
    five = 5 * lax.broadcasted_iota(jnp.int32, (HALF, 128), 1)
    for k in range(5):
        order[:, lanes(k)] = jnp.where(z_id == five + k, 1.0, 0.0).astype(BF16)
    rhs[240:256, :] = jnp.zeros((16, WIDE), BF16)
    left[...] = jnp.zeros_like(left)
    perm[...] = jnp.zeros_like(perm)
    sub8 = lax.broadcasted_iota(jnp.int32, (8, 128), 0)
    lane56 = lax.broadcasted_iota(jnp.int32, (QROWS, 128), 1)
    lane1 = lax.broadcasted_iota(jnp.int32, (1, 128), 1)
    row_id = lax.broadcasted_iota(jnp.int32, (ROWS, 128), 0)
    comp_id = (row_id >= 25).astype(jnp.int32) + (row_id >= 50).astype(jnp.int32) + (row_id >= 75).astype(jnp.int32)
    spot_id = (row_id - 25 * comp_id).astype(F32)

    for load in loads:
        load.wait()
    mats[...] = mats_ref[...].astype(BF16)
    at_e, at_h, at_lift, at_corner = INNER, INNER + SENT, INNER + 2 * SENT, INNER + 2 * SENT + 2 * ROWS
    inner = mats.at[0:INNER]
    send_e, send_h = mats.at[at_e:at_h], mats.at[at_h:at_lift]
    lift = mats.at[at_lift:at_corner, 0:128]
    for number in range(3):
        spread[number] = jnp.broadcast_to(cols_ref[:, 2 + number : 3 + number], (ROWS, 128))

    node = nodes_ref[...].astype(F32)
    pair = jnp.floor((node + 0.5) * (1.0 / HALF))
    depth = node - float(HALF) * pair
    element = jnp.floor((depth + 0.5) * 0.2)
    inside = depth - 5.0 * element
    weight = jnp.zeros_like(node)
    for k in range(5):
        weight = jnp.where(inside == float(k), float(1.0 / root[k]), weight)
    pick_row[...] = jnp.where(spot_id == pair, cols_ref[:, 1:2] * weight, 0.0)
    sub_id = lax.broadcasted_iota(jnp.int32, (128, 128), 0).astype(F32)
    for k in range(5):
        hot = jnp.where((sub_id == element) & (inside == float(k)), 1.0, 0.0)
        pick_lane[lanes(k), :] = hot.astype(BF16)
        flipped = jnp.transpose(hot).astype(BF16)
        pick_back[0:128, lanes(k)] = flipped
        pick_back[128:256, lanes(k)] = flipped
    for comp in range(3):
        for moment in range(2):
            left[0, moment, comp : comp + 1, :] = data_ref[comp, moment : moment + 1, :]

    tag_low = tags_ref[0][:, 0:1].astype(F32)
    tag_high = tags_ref[0][:, 1:2].astype(F32)
    for comp in range(3):
        for i in range(5):
            perm[comp * 25 + i * 5 : comp * 25 + i * 5 + 5, :] = cond_ref[i]
    halves = jnp.concatenate(split(perm[0:ROWS, :]), axis=0)
    for k in range(5):
        both = dot(halves, order[:, lanes(k)])
        sig[:, lanes(k)] = STEP_SIZE * (both[0:ROWS] + both[ROWS : 2 * ROWS]) + spread[1 if k in (0, 4) else 0]
    support = supp_ref[0].astype(F32)
    for k in range(5):
        gain[:, lanes(k)] = (-DRIVE_GAIN * STEP_SIZE * float(root[k])) * support * cols_ref[:, 0:1]
    own_support[...] = support

    pl.semaphore_wait(barrier, greeted)
    support_copies = [
        remote(
            own_support, beside_support.at[face], supp_send_sem.at[face], supp_recv_sem.at[face], beside[face]
        )
        for face in range(FACES)
    ]
    for copy, exists in zip(support_copies, to_face):
        start(copy, exists)

    rounds = 0
    while 2**rounds < max(n_gx, n_gy):
        rounds += 1

    def meet(turn, when, taken, sent):
        def beyond(number):
            for at, size, along_x in ((gx, n_gx, True), (gy, n_gy, False)):
                distance = 2**number
                if distance < size:
                    yield at >= distance, ((gx - distance, gy) if along_x else (gx, gy - distance))
                    yield at < size - distance, ((gx + distance, gy) if along_x else (gx, gy + distance))

        @pl.when(turn == when)
        def _():
            if 0 <= taken < rounds:
                count = jnp.int32(0)
                for exists, _ in beyond(taken):
                    count = count + exists.astype(jnp.int32)
                pl.semaphore_wait(meet_sem.at[taken], count)
            if sent < rounds:
                for exists, device in beyond(sent):

                    @pl.when(exists)
                    def _():
                        pl.semaphore_signal(meet_sem.at[sent], inc=1, device_id=device, device_id_type=MESH)

    def reduce_send(index, phase, row):
        red_buf[index, phase, 0] = row
        for step in range(1, sizes[phase]):
            remote(
                red_buf.at[index, phase, 0], red_buf.at[index, phase, step], red_send_sem.at[index, phase],
                red_recv_sem.at[index, phase], partner(phase, step),
            ).start()

    def reduce_take(index, phase):
        if sizes[phase] == 1:
            return red_buf[index, phase, 0]
        others = red_buf.at[index, phase, pl.ds(1, sizes[phase] - 1)]
        pltpu.make_async_copy(others, others, red_recv_sem.at[index, phase]).wait()
        pltpu.make_async_copy(others, others, red_send_sem.at[index, phase]).wait()
        terms = [red_buf[index, phase, step] for step in range(sizes[phase])]
        while len(terms) > 1:
            terms = [sum(terms[at + 1 : at + 2], terms[at]) for at in range(0, len(terms), 2)]
        return terms[0]

    def whole(value):
        return jnp.sum(jnp.sum(value, axis=0, keepdims=True), axis=1, keepdims=True)

    def packed_row(values):
        row = jnp.zeros((1, 128), F32)
        for number, value in enumerate(values):
            row = jnp.where(lane1 == number, value, row)
        return row

    def entry(row, number):
        return jnp.sum(jnp.where(lane1 == number, row, 0.0), axis=1, keepdims=True)

    def data_dot(a, b):
        return whole(a[0] * b[0] + a[1] * b[1])

    def source_dot(a, b):
        total = jnp.zeros((ROWS, 128), F32)
        for moment in range(2):
            for k in range(5):
                total = total + a[moment, :, lanes(k)] * b[moment, :, lanes(k)]
        return whole(total)

    def load_rhs(ref, magnetic):
        for block in range(10 if magnetic else 5):
            high, low = split(ref[:, lanes(block)])
            rhs[0:80, lanes(block)] = high
            rhs[80:160, lanes(block)] = low
            rhs[160:240, lanes(block)] = high

    def own_rates(field, result, halves, magnetic):
        if not magnetic:
            prod[:, 0:HALF] = dot(inner[...], rhs[:, 0:HALF])
        elif len(halves) == 1:
            prod[:, HALF:WIDE] = dot(inner[...], rhs[:, HALF:WIDE])
        else:
            prod[...] = dot(inner[...], rhs[...])
        for half in halves:
            own0, other0 = half * 5, (1 - half) * 5
            sign = 1.0 if half == 0 else -1.0
            for k in range(5):
                if half == 0 and not magnetic:
                    change = -sig[:, lanes(k)] * field[:, lanes(k)]
                    upper = change[0:QROWS]
                    if k == 0:
                        inward = pltpu.roll(field[0:QROWS, lanes(4)], 1, 1)
                        edge = -tag_low * field[0:QROWS, lanes(0)]
                        upper = upper + spread[2][0:QROWS] * jnp.where(lane56 == 0, edge, inward)
                    elif k == 4:
                        inward = pltpu.roll(field[0:QROWS, lanes(0)], 127, 1)
                        edge = -tag_high * field[0:QROWS, lanes(4)]
                        upper = upper + spread[2][0:QROWS] * jnp.where(lane56 == 127, edge, inward)
                    result[0:QROWS, lanes(k)] = upper
                    result[QROWS:ROWS, lanes(k)] = change[QROWS:ROWS]
                    continue
                slope = None
                for m in range(5):
                    if m != k and abs(deriv[k, m]) > 1e-12:
                        term = float(deriv[k, m]) * prod[80:136, lanes(other0 + m)]
                        slope = term if slope is None else slope + term
                decay = sig[:, lanes(k)] if half == 0 else spread[1 if k in (0, 4) else 0]
                change = sign * prod[0:80, lanes(other0 + k)] - decay * field[:, lanes(own0 + k)]
                upper = change[0:QROWS] - sign * slope
                if k in (0, 4):
                    own_low, turn_low = field[0:QROWS, lanes(own0)], prod[80:136, lanes(other0)]
                    own_high, turn_high = field[0:QROWS, lanes(own0 + 4)], prod[80:136, lanes(other0 + 4)]
                    if half == 1:
                        turn_low, turn_high = -turn_low, -turn_high
                    if k == 0:
                        inward = pltpu.roll(own_high + turn_high, 1, 1)
                        edge = (tag_low * -sign) * (own_low - turn_low)
                        incoming = jnp.where(lane56 == 0, edge, inward)
                    else:
                        inward = pltpu.roll(own_low - turn_low, 127, 1)
                        edge = (tag_high * -sign) * (own_high + turn_high)
                        incoming = jnp.where(lane56 == 127, edge, inward)
                    upper = upper + spread[2][0:QROWS] * incoming
                result[0:QROWS, lanes(own0 + k)] = upper
                result[QROWS:ROWS, lanes(own0 + k)] = change[QROWS:ROWS]

    def pack_face(out, face, buf):
        base = face * 16
        mixed = jnp.zeros((8, 128), F32)
        for k in range(5):
            buf[8 * k : 8 * k + 8, :] = out[base : base + 8, lanes(k)]
            if k < 4:
                mixed = jnp.where((sub8 >= 2 * k) & (sub8 < 2 * k + 2), out[base + 8 : base + 16, lanes(k)], mixed)
        buf[40:48, :] = mixed
        buf[48:56, :] = out[base + 8 : base + 16, lanes(4)]

    def kept(k):
        start = 2 * k if k < 4 else 0
        return (sub8 >= start) & (sub8 < start + 2)

    def unpack_face(buf, k):
        mixed = buf[40:48, :] if k < 4 else buf[48:56, :]
        return jnp.concatenate([buf[8 * k : 8 * k + 8, :], jnp.where(kept(k), mixed, 0.0)], axis=0)

    def set_ghosts(face, k, piece):
        high, low = split(strength * piece)
        ghost_rhs[face * 16 : face * 16 + 16, lanes(k)] = high
        ghost_rhs[64 + face * 16 : 64 + face * 16 + 16, lanes(k)] = low

    def stage(slot, early, make_second, late, merge, halves_1, halves_2, magnetic_1, magnetic_2, share):
        load_rhs(fields, magnetic_1)
        out = dot(send_e[...], rhs[:, 0:HALF])
        if magnetic_1:
            out = out + dot(send_h[...], rhs[:, HALF:WIDE])
        copies = []
        for face in range(FACES):
            pack_face(out, face, send_buf.at[slot, face])
            copies.append(
                remote(
                    send_buf.at[slot, face], recv_buf.at[slot, face], send_sem.at[slot, face], recv_sem.at[slot, face],
                    beside[face],
                )
            )
            start(copies[face], to_face[face])
        corner_copies = []
        for diag in range(4):
            base = 64 + diag * 8
            for tile in range(3):
                piece = out[base : base + 8, lanes(2 * tile)]
                if tile < 2:
                    piece = jnp.where(sub8 < 4, piece, out[base : base + 8, lanes(2 * tile + 1)])
                send_diag[slot, diag, 8 * tile : 8 * tile + 8, :] = piece
            corner_copies.append(
                remote(
                    send_diag.at[slot, diag], recv_diag.at[slot, diag], diag_send_sem.at[slot, diag],
                    diag_recv_sem.at[slot, diag], across[diag],
                )
            )
            start(corner_copies[diag], to_diag[diag])
        early()
        own_rates(fields, rates, halves_1, magnetic_1)
        make_second()
        load_rhs(second, magnetic_2)
        out = dot(send_e[0:64, :], rhs[:, 0:HALF])
        if magnetic_2:
            out = out + dot(send_h[0:64, :], rhs[:, HALF:WIDE])
        next_copies = []
        for face in range(FACES):
            pack_face(out, face, send_next.at[slot, face])
            next_copies.append(
                remote(
                    send_next.at[slot, face], recv_next.at[slot, face], next_send_sem.at[slot, face],
                    next_recv_sem.at[slot, face], beside[face],
                )
            )
            start(next_copies[face], to_face[face])
        late()

        wait_all(copies, to_face, 1)
        for face in range(FACES):
            for k in range(5):
                set_ghosts(face, k, unpack_face(recv_buf.at[slot, face], k))
        merge(dot(lift[...], ghost_rhs[...]))
        load_rhs(second, magnetic_2)
        own_rates(second, rates, halves_2, magnetic_2)

        wait_all(corner_copies, to_diag, 3)
        for two in range(2):
            for k in range(5):
                pieces = []
                for diag in (2 * two, 2 * two + 1):
                    tile = recv_diag[slot, diag, 8 * (k // 2) : 8 * (k // 2) + 8, :]
                    tile = jnp.where(sub8 >= 4 if k % 2 else sub8 < 4, tile, 0.0)
                    pieces.append(strength * tile)
                high, low = split(jnp.concatenate(pieces, axis=0))
                corner_rhs[16 * two : 16 * two + 16, lanes(k)] = high
                corner_rhs[32 + 16 * two : 32 + 16 * two + 16, lanes(k)] = low
        begin = at_corner + (0 if magnetic_2 else 64)
        extra = dot(mats[begin : begin + 64, 0:64], corner_rhs[...])
        wait_all(next_copies, to_face, 1)
        for face in range(FACES):
            for k in range(5):
                piece = extra[face * 16 : face * 16 + 16, lanes(k)]
                piece = jnp.concatenate([piece[0:8], jnp.where(kept(k), piece[8:16], 0.0)], axis=0)
                if not magnetic_2:
                    piece = piece + strength * unpack_face(send_buf.at[slot, face ^ 1], k)
                    piece = piece * gain_out[face * 16 : face * 16 + 16, lanes(k)]
                set_ghosts(face, k, unpack_face(recv_next.at[slot, face], k) + share * piece)
        if len(halves_2) == 2:
            lifted = dot(lift[...], ghost_rhs[...])
            rates[:, 0:HALF] += lifted[0:ROWS]
            rates[:, HALF:WIDE] += lifted[ROWS : 2 * ROWS]
        else:
            rates[:, 0:HALF] += dot(lift[0:ROWS, :], ghost_rhs[...])

    def inject(turn, moment):
        values = jnp.where(
            comp_id == 0,
            left[turn, moment, 0:1, :],
            jnp.where(comp_id == 1, left[turn, moment, 1:2, :], left[turn, moment, 2:3, :]),
        )
        high, low = split(pick_row[...] * values)
        return dot(jnp.concatenate([high, low], axis=1), pick_back[...])

    def gather(halves, turn, moment):
        both = dot(halves, pick_lane[...])
        chosen = (both[0:ROWS] + both[ROWS : 2 * ROWS]) * pick_row[...]
        out = jnp.zeros((8, 128), F32)
        for comp in range(3):
            part = jnp.sum(jnp.where(comp_id == comp, chosen, 0.0), axis=0, keepdims=True)
            out = jnp.where(sub8 == comp, part, out)
        left[turn, moment] = out

    def to_output_order(vector, number):
        for moment in range(2):
            both = dot_nt(jnp.concatenate(split(vector[moment]), axis=0), order[...])
            at = (number * 2 + moment) * ROWS
            perm_out[at : at + ROWS, :] = both[0:ROWS] + both[ROWS : 2 * ROWS]

    every, electric = (0, 1), (0,)

    def sweep(turn, carry):
        fields[:, 0:HALF] = inject(turn, 1)
        fields[:, HALF:WIDE] = jnp.zeros((ROWS, HALF), F32)

        def second_1():
            second[...] = rates[...]

        def merge_1(lifted):
            second[:, 0:HALF] += lifted[0:ROWS]
            second[:, HALF:WIDE] += lifted[ROWS : 2 * ROWS]

        def late_1():
            meet(turn, 0, -1, 0)

            @pl.when(turn == 1)
            def _():
                reduce_send(
                    0, 0, packed_row([data_dot(left[0], left[0]), source_dot(source.at[0], source.at[0])])
                )
                to_output_order(source.at[0], 0)

        stage(turn * 3, lambda: meet(turn, 1, 4, 5), second_1, late_1, merge_1, every, every, False, True, 1.0)
        for k in range(5):
            source[turn, 1, :, lanes(k)] = gain[:, lanes(k)] * (fields[:, lanes(k)] + 0.5 * second[:, lanes(k)])
        fields[:, 0:HALF] = inject(turn, 0) + fields[:, 0:HALF] + second[:, 0:HALF] + 0.5 * rates[:, 0:HALF]
        fields[:, HALF:WIDE] = second[:, HALF:WIDE] + 0.5 * rates[:, HALF:WIDE]

        def second_2():
            for k in range(5):
                amount = gain[:, lanes(k)] * (fields[:, lanes(k)] + 0.5 * rates[:, lanes(k)])
                source[turn, 0, :, lanes(k)] = amount
                second[:, lanes(k)] = gain[:, lanes(k)] * amount
            second[:, HALF:WIDE] = jnp.zeros((ROWS, HALF), F32)

        def merge_2(lifted):
            for k in range(5):
                amount = source[turn, 0, :, lanes(k)] + 0.5 * gain[:, lanes(k)] * lifted[0:ROWS, lanes(k)]
                source[turn, 0, :, lanes(k)] = amount
                second[:, lanes(k)] = gain[:, lanes(k)] * amount

        def late_2():
            meet(turn, 0, 1, 2)

            @pl.when(turn == 1)
            def _():
                reduce_send(0, 1, reduce_take(0, 0))

            @pl.when(turn == 0)
            def _():
                wait_all(support_copies, to_face, 1)
                for face in range(FACES):
                    for k in range(5):
                        column = float(root[k] ** 2) * cols_ref[face * 16 : face * 16 + 16, 5:6]
                        gain_out[face * 16 : face * 16 + 16, lanes(k)] = column * beside_support[face]

        stage(turn * 3 + 1, lambda: meet(turn, 0, 0, 1), second_2, late_2, merge_2, electric, every, True, False, 0.5)
        fields[:, 0:HALF] = second[:, 0:HALF] + 0.5 * rates[:, 0:HALF]
        fields[:, HALF:WIDE] = 0.5 * rates[:, HALF:WIDE]

        def early_3():
            gather(rhs[0:160, 0:HALF], turn + 1, 0)
            meet(turn, 0, 2, 3)

        def second_3():
            for k in range(5):
                drive = gain[:, lanes(k)] * source[turn, 1, :, lanes(k)]
                second[:, lanes(k)] = fields[:, lanes(k)] + 0.5 * (rates[:, lanes(k)] + drive)
                fields[:, lanes(k)] = fields[:, lanes(k)] + drive
            second[:, HALF:WIDE] = fields[:, HALF:WIDE] + 0.5 * rates[:, HALF:WIDE]

        def merge_3(lifted):
            second[:, 0:HALF] += 0.5 * lifted[0:ROWS]
            second[:, HALF:WIDE] += 0.5 * lifted[ROWS : 2 * ROWS]

        def late_3():
            meet(turn, 0, 3, 4)

            @pl.when(turn == 1)
            def _():
                norms = reduce_take(0, 1)
                red_buf[0, 0, 0] = norms
                ratio = entry(norms, 1) / entry(norms, 0)
                for moment in range(2):
                    for k in range(5):
                        ortho[moment, :, lanes(k)] = (
                            source[1, moment, :, lanes(k)] - ratio * source[0, moment, :, lanes(k)]
                        )
                to_output_order(ortho, 1)

        stage(turn * 3 + 2, early_3, second_3, late_3, merge_3, every, electric, True, True, 0.5)
        halves = split(fields[:, 0:HALF] + rates[:, 0:HALF])
        gather(jnp.concatenate(halves, axis=0), turn + 1, 1)
        return carry

    lax.fori_loop(0, 2, sweep, 0)

    norms = red_buf[0, 0, 0]
    sq_b, sq_g = entry(norms, 0), entry(norms, 1)
    ratio = sq_g / sq_b
    for moment in range(2):
        left[0, moment] = left[1, moment] - ratio * left[0, moment]
        left[2, moment] = left[2, moment] - ratio * left[1, moment]
    p, f, h = left[0], left[1], left[2]
    products = [
        data_dot(p, p), source_dot(ortho, ortho), source_dot(ortho, source.at[0]), data_dot(h, h), data_dot(h, f),
        data_dot(f, f), data_dot(h, p), data_dot(f, p),
    ]
    reduce_send(1, 0, packed_row(products))
    reduce_send(1, 1, reduce_take(1, 0))
    total = reduce_take(1, 1)
    pp, oo, og, hh, hf, ff, hp, fp = (entry(total, number) for number in range(8))
    take = pp / sq_g
    sq_q = jnp.maximum(oo - 2.0 * take * og + take * take * sq_g, 0.0)
    beta_1 = jnp.sqrt(sq_b)
    alpha_1 = jnp.sqrt(ratio)
    beta_2 = jnp.sqrt(take)
    alpha_2 = jnp.sqrt(sq_q / pp)
    sq_w = hh - 2.0 * take * hf + take * take * ff
    sq_beta_3 = jnp.maximum(sq_w / sq_q - 2.0 * (hp - take * fp) / pp + sq_q / pp, 0.0)
    rho_1 = jnp.sqrt(alpha_1 * alpha_1 + beta_2 * beta_2)
    cosine, sine = alpha_1 / rho_1, beta_2 / rho_1
    step_1 = cosine * beta_1 / rho_1
    phi_bar = sine * beta_1
    theta = sine * alpha_2
    rho_bar = -cosine * alpha_2
    rho_2 = jnp.sqrt(rho_bar * rho_bar + sq_beta_3)
    step_2 = rho_bar / rho_2 * phi_bar / rho_2
    on_ortho = step_2 / jnp.sqrt(sq_q)
    on_first = (step_1 - step_2 * theta / rho_1) / jnp.sqrt(sq_g) - on_ortho * take
    on_h = phi_bar / rho_2 / jnp.sqrt(sq_q)
    on_p = phi_bar / rho_2 * jnp.sqrt(sq_q) / pp
    for moment in range(2):
        res_ref[moment] = (on_h * (h[moment] - take * f[moment]) - on_p * p[moment])[0:3, :]
        for comp in range(3):
            for i in range(5):
                at = comp * 25 + i * 5
                one = perm_out[moment * ROWS + at : moment * ROWS + at + 5, :]
                two = perm_out[(2 + moment) * ROWS + at : (2 + moment) * ROWS + at + 5, :]
                est_ref[moment, comp, i] = on_first * one + on_ortho * two


def solution(mesh):
    n_gx, n_gy = mesh.shape["gx"], mesh.shape["gy"]
    matrices, columns = tables()

    def shards(probe_data, conductivity, support, face_tags, probe_nodes):
        vmem = pl.BlockSpec(memory_space=pltpu.VMEM)
        anywhere = pl.BlockSpec(memory_space=pl.ANY)
        return pl.pallas_call(
            functools.partial(kernel, n_gx, n_gy),
            out_shape=(
                jax.ShapeDtypeStruct((2, 3, 5, 5, HALF), F32),
                jax.ShapeDtypeStruct((2, 3, 128), F32),
            ),
            in_specs=[anywhere] * 7,
            out_specs=(vmem, vmem),
            scratch_shapes=[
                pltpu.VMEM((1, 1, 2), jnp.int32),
                pltpu.VMEM((3, 2, 128), F32),
                pltpu.VMEM((5, 5, HALF), F32),
                pltpu.VMEM((1, 1, 128), jnp.int32),
                pltpu.VMEM((1, 128), jnp.int32),
                pltpu.VMEM(matrices.shape, F32),
                pltpu.VMEM(columns.shape, F32),
                pltpu.VMEM(matrices.shape, BF16),
                pltpu.VMEM((HALF, HALF), BF16),
                pltpu.VMEM((3, ROWS, 128), F32),
                pltpu.VMEM((ROWS, WIDE), F32),
                pltpu.VMEM((ROWS, WIDE), F32),
                pltpu.VMEM((ROWS, WIDE), F32),
                pltpu.VMEM((256, WIDE), BF16),
                pltpu.VMEM((INNER, WIDE), F32),
                pltpu.VMEM((128, HALF), BF16),
                pltpu.VMEM((64, HALF), BF16),
                pltpu.VMEM((ROWS, HALF), F32),
                pltpu.VMEM((ROWS, HALF), F32),
                pltpu.VMEM((64, HALF), F32),
                pltpu.VMEM((ROWS, 128), F32),
                pltpu.VMEM((HALF, 128), BF16),
                pltpu.VMEM((256, HALF), BF16),
                pltpu.VMEM((3, 2, 8, 128), F32),
                pltpu.VMEM((2, 2, ROWS, HALF), F32),
                pltpu.VMEM((2, ROWS, HALF), F32),
                pltpu.VMEM((ROWS, HALF), F32),
                pltpu.VMEM((4 * ROWS, HALF), F32),
                pltpu.VMEM((FACES, 1, 128), F32),
                pltpu.VMEM((1, 128), F32),
                pltpu.VMEM((6, FACES, QROWS, 128), F32),
                pltpu.VMEM((6, FACES, QROWS, 128), F32),
                pltpu.VMEM((6, FACES, QROWS, 128), F32),
                pltpu.VMEM((6, FACES, QROWS, 128), F32),
                pltpu.VMEM((6, 4, 24, 128), F32),
                pltpu.VMEM((6, 4, 24, 128), F32),
                pltpu.VMEM((2, 2, max(n_gx, n_gy), 1, 128), F32),
                pltpu.SemaphoreType.DMA((7,)),
                pltpu.SemaphoreType.DMA((6, FACES)),
                pltpu.SemaphoreType.DMA((6, FACES)),
                pltpu.SemaphoreType.DMA((6, FACES)),
                pltpu.SemaphoreType.DMA((6, FACES)),
                pltpu.SemaphoreType.DMA((6, 4)),
                pltpu.SemaphoreType.DMA((6, 4)),
                pltpu.SemaphoreType.DMA((2, 2)),
                pltpu.SemaphoreType.DMA((2, 2)),
                pltpu.SemaphoreType.DMA((FACES,)),
                pltpu.SemaphoreType.DMA((FACES,)),
                pltpu.SemaphoreType.REGULAR((5,)),
            ],
            compiler_params=pltpu.CompilerParams(
                collective_id=0, has_side_effects=True, vmem_limit_bytes=22 * 1024 * 1024
            ),
        )(
            *(
                pltpu.with_memory_space_constraint(array, pltpu.HBM)
                for array in (
                    jnp.transpose(face_tags, (1, 2, 0)), jnp.transpose(probe_data, (1, 0, 2)), conductivity, support,
                    probe_nodes.reshape(1, 128), jnp.asarray(matrices), jnp.asarray(columns),
                )
            )
        )

    return jax.shard_map(
        shards,
        mesh=mesh,
        in_specs=(
            P(None, None, ("gx", "gy")),
            P("gx", "gy", None),
            P("gx", "gy", None),
            P(None, "gx", "gy"),
            P(("gx", "gy")),
        ),
        out_specs=(P(None, None, "gx", "gy", None), P(None, None, ("gx", "gy"))),
        check_vma=False,
    )
```

```python
import functools
import math

import jax
import jax.numpy as jnp
import numpy as np
from jax import lax
from jax.experimental import pallas as pl
from jax.experimental.pallas import tpu as pltpu
from jax.sharding import PartitionSpec as P

MESH = pl.DeviceIdType.MESH
F32 = jnp.float32
BF16 = jnp.bfloat16

STEP_SIZE = 0.02
LIFT_HALF = 5.0
DRIVE_GAIN = 50.0
ROWS = 80
QROWS = 56
HALF = 640
WIDE = 1280
INNER = 144
SENT = 96
FACES = 4
DIAGS = ((-1, -1), (-1, 1), (1, -1), (1, 1))
CHARS = (
    ((1, 2, 1.0), (2, 1, -1.0)),
    ((1, 2, -1.0), (2, 1, 1.0)),
    ((0, 2, -1.0), (2, 0, 1.0)),
    ((0, 2, 1.0), (2, 0, -1.0)),
)
SIDES = ((0, 4, 0), (0, 0, 4), (1, 4, 0), (1, 0, 4))


def lobatto_scaled():
    radical = math.sqrt(3.0 / 7.0)
    points = np.array([-1.0, -radical, 0.0, radical, 1.0])
    legendre = (35.0 * points**4 - 30.0 * points**2 + 3.0) / 8.0
    weights = 0.1 / legendre**2
    matrix = np.zeros((5, 5))
    for i in range(5):
        for j in range(5):
            if i != j:
                matrix[i, j] = legendre[i] / (legendre[j] * (points[i] - points[j]))
    root = np.sqrt(weights)
    return matrix * root[:, None] / root[None, :], root


def row_of(comp, i, j):
    return comp * 25 + 5 * i + j


def split_np(matrix):
    high = np.asarray(matrix, np.float32).astype(jnp.bfloat16)
    low = (np.asarray(matrix, np.float32) - high.astype(np.float32)).astype(jnp.bfloat16)
    return high, low


def tables():
    deriv, root = lobatto_scaled()
    deriv = STEP_SIZE * deriv
    curl = np.zeros((ROWS, ROWS))
    turn = np.zeros((QROWS, ROWS))
    for i in range(5):
        for j in range(5):
            for k in range(5):
                curl[row_of(0, i, j), row_of(2, i, k)] += deriv[j, k]
                curl[row_of(1, i, j), row_of(2, k, j)] -= deriv[i, k]
                curl[row_of(2, i, j), row_of(1, k, j)] += deriv[i, k]
                curl[row_of(2, i, j), row_of(0, i, k)] -= deriv[j, k]
            turn[row_of(0, i, j), row_of(1, i, j)] = 1.0
            turn[row_of(1, i, j), row_of(0, i, j)] = -1.0
    high, low = split_np(curl)
    inner = np.zeros((INNER, 256), np.float32)
    inner[:ROWS, 0:80] = high
    inner[:ROWS, 80:160] = high
    inner[:ROWS, 160:240] = low
    inner[ROWS : ROWS + QROWS, 0:80] = turn
    inner[ROWS : ROWS + QROWS, 80:160] = turn

    send_e = np.zeros((SENT, 256), np.float32)
    send_h = np.zeros((SENT, 256), np.float32)
    lift = np.zeros((2 * ROWS, 256), np.float32)
    corner = np.zeros((128, 256), np.float32)
    slot_weight = np.zeros(64)
    for face in range(FACES):
        axis, node_out, node_in = SIDES[face]
        for slot in range(16):
            char = slot if slot < 8 else 8 + slot % 2
            which, along = char // 5, char % 5
            comp_e, comp_h, sign = CHARS[face][which]
            spot_out = (node_out, along) if axis == 0 else (along, node_out)
            spot_in = (node_in, along) if axis == 0 else (along, node_in)
            at = face * 16 + slot
            slot_weight[at] = root[0] ** 2 * root[along] ** 2
            for part in (0, 80):
                send_e[at, part + row_of(comp_e, *spot_out)] = 1.0
                send_h[at, part + row_of(comp_h, *spot_out)] = sign
            for part in (0, 64):
                lift[row_of(comp_e, *spot_in), part + at] = 1.0
                lift[ROWS + row_of(comp_h, *spot_in), part + at] = sign
            for diag, (side_x, side_y) in enumerate(DIAGS):
                if axis == 0:
                    if side_x != (-1 if face == 0 else 1):
                        continue
                    other, first = (2 if side_y < 0 else 3), 2
                else:
                    if side_y != (-1 if face == 2 else 1):
                        continue
                    other, first = (0 if side_x < 0 else 1), 0
                if along != SIDES[other][2]:
                    continue
                for number, (other_e, other_h, other_sign) in enumerate(CHARS[other]):
                    only_e = float(comp_e == other_e)
                    both = only_e + sign * other_sign * float(comp_h == other_h)
                    for part in (0, 4, 32, 36):
                        column = diag * 8 + first + number + part
                        corner[at, column] = both
                        corner[64 + at, column] = only_e
    for diag, (side_x, side_y) in enumerate(DIAGS):
        spot = (4 if side_x < 0 else 0, 4 if side_y < 0 else 0)
        for slot in range(8):
            face = ((0 if side_x < 0 else 1), (2 if side_y < 0 else 3))[slot % 4 // 2]
            comp_e, comp_h, sign = CHARS[face][slot % 2]
            for part in (0, 80):
                send_e[64 + diag * 8 + slot, part + row_of(comp_e, *spot)] = 1.0
                send_h[64 + diag * 8 + slot, part + row_of(comp_h, *spot)] = sign
    matrices = np.concatenate([inner, send_e, send_h, lift, corner], axis=0)

    columns = np.zeros((ROWS, 128), np.float32)
    strength = STEP_SIZE * LIFT_HALF
    for comp in range(3):
        for i in range(5):
            for j in range(5):
                row = row_of(comp, i, j)
                columns[row, 0] = root[i] * root[j]
                columns[row, 1] = 1.0 / (root[i] * root[j])
                count = (i in (0, 4)) * (comp != 0) + (j in (0, 4)) * (comp != 1)
                columns[row, 2] = strength * count
                columns[row, 3] = strength * (count + (comp != 2))
                columns[row, 4] = strength * (comp != 2)
    columns[0:64, 5] = (DRIVE_GAIN * STEP_SIZE) ** 2 * slot_weight
    return matrices, columns


def split(value):
    high = value.astype(BF16)
    return high, (value - high.astype(F32)).astype(BF16)


def dot(a, b):
    return jnp.dot(a, b, preferred_element_type=F32)


def dot_nt(a, b):
    return lax.dot_general(a, b, (((1,), (1,)), ((), ())), preferred_element_type=F32)


def lanes(block):
    return slice(block * 128, block * 128 + 128)


def kernel(
    n_gx, n_gy, tags_hbm, data_hbm, cond_hbm, supp_hbm, nodes_hbm, mats_hbm, cols_hbm, est_ref, res_ref,
    tags_ref, data_ref, cond_ref, supp_ref, nodes_ref, mats_ref, cols_ref, mats, order, spread,
    fields, second, rates, saved, held, multiple, rhs, prod, ghost_rhs, corner_rhs, sig, gain, gain_out, pick_row, pick_lane, pick_back,
    left, source, ortho, perm, perm_out, beside_support, own_support,
    send_buf, recv_buf, send_next, recv_next, send_diag, recv_diag, red_buf,
    load_sem, send_sem, recv_sem, next_send_sem, next_recv_sem, diag_send_sem, diag_recv_sem, red_send_sem, red_recv_sem,
    supp_send_sem, supp_recv_sem, meet_sem,
):
    loads = []
    pairs = (
        (data_hbm, data_ref), (nodes_hbm, nodes_ref), (mats_hbm, mats_ref), (cols_hbm, cols_ref),
        (cond_hbm, cond_ref), (supp_hbm, supp_ref), (tags_hbm, tags_ref),
    )
    for number, (far, near) in enumerate(pairs):
        load = pltpu.make_async_copy(far, near, load_sem.at[number])
        load.start()
        loads.append(load)

    deriv, root = lobatto_scaled()
    deriv = STEP_SIZE * deriv
    gx, gy = lax.axis_index("gx"), lax.axis_index("gy")
    sizes = (n_gx, n_gy)

    def partner(phase, step):
        if phase == 0:
            return (lax.rem(gx + step, n_gx), gy)
        return (gx, lax.rem(gy + step, n_gy))

    def near_by(step_x, step_y):
        return (lax.rem(gx + n_gx + step_x, n_gx), lax.rem(gy + n_gy + step_y, n_gy))

    beside = (near_by(1, 0), near_by(-1, 0), near_by(0, 1), near_by(0, -1))
    across = tuple(near_by(-side_x, -side_y) for side_x, side_y in DIAGS)
    strength = STEP_SIZE * LIFT_HALF
    has = {(0, -1): gx > 0, (0, 1): gx < n_gx - 1, (1, -1): gy > 0, (1, 1): gy < n_gy - 1}
    to_face = tuple(has[key] for key in ((0, 1), (0, -1), (1, 1), (1, -1)))
    to_diag = tuple(has[(0, -side_x)] & has[(1, -side_y)] for side_x, side_y in DIAGS)

    for face in range(FACES):

        @pl.when(jnp.logical_not(to_face[face ^ 1]))
        def _():
            for slot in range(6):
                recv_buf[slot, face] = jnp.zeros((QROWS, 128), F32)
                recv_next[slot, face] = jnp.zeros((QROWS, 128), F32)
            beside_support[face] = jnp.zeros((1, 128), F32)

    for diag in range(4):

        @pl.when(jnp.logical_not(to_diag[3 - diag]))
        def _():
            for slot in range(6):
                recv_diag[slot, diag] = jnp.zeros((24, 128), F32)

    barrier = pltpu.get_barrier_semaphore()
    greeted = jnp.int32(0)
    for device, exists in zip(beside + across, to_face + to_diag):

        @pl.when(exists)
        def _():
            pl.semaphore_signal(barrier, inc=1, device_id=device, device_id_type=MESH)

        greeted = greeted + exists.astype(jnp.int32)

    def remote(src, dst, sem_out, sem_in, device):
        copy = pltpu.make_async_remote_copy(
            src_ref=src, dst_ref=dst, send_sem=sem_out, recv_sem=sem_in, device_id=device, device_id_type=MESH
        )
        return copy

    def start(copy, exists):
        @pl.when(exists)
        def _():
            copy.start()

    def wait_all(copies, exist, flip):
        for number, exists in enumerate(exist):
            back = number ^ flip

            @pl.when(exists)
            def _():
                copies[number].wait_send()
                copies[back].wait_recv()

    z_id = lax.broadcasted_iota(jnp.int32, (HALF, 128), 0)
    five = 5 * lax.broadcasted_iota(jnp.int32, (HALF, 128), 1)
    for k in range(5):
        order[:, lanes(k)] = jnp.where(z_id == five + k, 1.0, 0.0).astype(BF16)
    rhs[240:256, :] = jnp.zeros((16, WIDE), BF16)
    left[...] = jnp.zeros_like(left)
    perm[...] = jnp.zeros_like(perm)
    sub8 = lax.broadcasted_iota(jnp.int32, (8, 128), 0)
    lane56 = lax.broadcasted_iota(jnp.int32, (QROWS, 128), 1)
    lane1 = lax.broadcasted_iota(jnp.int32, (1, 128), 1)
    row_id = lax.broadcasted_iota(jnp.int32, (ROWS, 128), 0)
    comp_id = (row_id >= 25).astype(jnp.int32) + (row_id >= 50).astype(jnp.int32) + (row_id >= 75).astype(jnp.int32)
    spot_id = (row_id - 25 * comp_id).astype(F32)

    for load in loads:
        load.wait()
    mats[...] = mats_ref[...].astype(BF16)
    at_e, at_h, at_lift, at_corner = INNER, INNER + SENT, INNER + 2 * SENT, INNER + 2 * SENT + 2 * ROWS
    inner = mats.at[0:INNER]
    send_e, send_h = mats.at[at_e:at_h], mats.at[at_h:at_lift]
    lift = mats.at[at_lift:at_corner, 0:128]
    for number in range(3):
        spread[number] = jnp.broadcast_to(cols_ref[:, 2 + number : 3 + number], (ROWS, 128))

    node = nodes_ref[...].astype(F32)
    pair = jnp.floor((node + 0.5) * (1.0 / HALF))
    depth = node - float(HALF) * pair
    element = jnp.floor((depth + 0.5) * 0.2)
    inside = depth - 5.0 * element
    weight = jnp.zeros_like(node)
    for k in range(5):
        weight = jnp.where(inside == float(k), float(1.0 / root[k]), weight)
    pick_row[...] = jnp.where(spot_id == pair, cols_ref[:, 1:2] * weight, 0.0)
    sub_id = lax.broadcasted_iota(jnp.int32, (128, 128), 0).astype(F32)
    for k in range(5):
        hot = jnp.where((sub_id == element) & (inside == float(k)), 1.0, 0.0)
        pick_lane[lanes(k), :] = hot.astype(BF16)
        flipped = jnp.transpose(hot).astype(BF16)
        pick_back[0:128, lanes(k)] = flipped
        pick_back[128:256, lanes(k)] = flipped
    high, low = split(pick_row[...] * pick_row[...])
    multiple[...] = dot(jnp.concatenate([high, low], axis=1), pick_back[...])
    for comp in range(3):
        for moment in range(2):
            left[0, moment, comp : comp + 1, :] = data_ref[comp, moment : moment + 1, :]

    tag_low = tags_ref[0][:, 0:1].astype(F32)
    tag_high = tags_ref[0][:, 1:2].astype(F32)
    for comp in range(3):
        for i in range(5):
            perm[comp * 25 + i * 5 : comp * 25 + i * 5 + 5, :] = cond_ref[i]
    halves = jnp.concatenate(split(perm[0:ROWS, :]), axis=0)
    for k in range(5):
        both = dot(halves, order[:, lanes(k)])
        sig[:, lanes(k)] = STEP_SIZE * (both[0:ROWS] + both[ROWS : 2 * ROWS]) + spread[1 if k in (0, 4) else 0]
    support = supp_ref[0].astype(F32)
    for k in range(5):
        gain[:, lanes(k)] = (-DRIVE_GAIN * STEP_SIZE * float(root[k])) * support * cols_ref[:, 0:1]
    own_support[...] = support

    support_copies = [
        remote(
            own_support, beside_support.at[face], supp_send_sem.at[face], supp_recv_sem.at[face], beside[face]
        )
        for face in range(FACES)
    ]

    rounds = 0
    while 2**rounds < max(n_gx, n_gy):
        rounds += 1

    def meet(turn, when, taken, sent):
        def beyond(number):
            for at, size, along_x in ((gx, n_gx, True), (gy, n_gy, False)):
                distance = 2**number
                if distance < size:
                    yield at >= distance, ((gx - distance, gy) if along_x else (gx, gy - distance))
                    yield at < size - distance, ((gx + distance, gy) if along_x else (gx, gy + distance))

        @pl.when(turn == when)
        def _():
            if 0 <= taken < rounds:
                count = jnp.int32(0)
                for exists, _ in beyond(taken):
                    count = count + exists.astype(jnp.int32)
                pl.semaphore_wait(meet_sem.at[taken], count)
            if sent < rounds:
                for exists, device in beyond(sent):

                    @pl.when(exists)
                    def _():
                        pl.semaphore_signal(meet_sem.at[sent], inc=1, device_id=device, device_id_type=MESH)

    def reduce_send(index, phase, row):
        red_buf[index, phase, 0] = row
        size = sizes[phase]
        for step in range(1, size):
            remote(
                red_buf.at[index, phase, 0], red_buf.at[index, phase, step], red_send_sem.at[index, phase],
                red_recv_sem.at[index, phase], partner(phase, step),
            ).start()

    def reduce_take(index, phase):
        if sizes[phase] == 1:
            return red_buf[index, phase, 0]
        others = red_buf.at[index, phase, pl.ds(1, sizes[phase] - 1)]
        pltpu.make_async_copy(others, others, red_recv_sem.at[index, phase]).wait()
        pltpu.make_async_copy(others, others, red_send_sem.at[index, phase]).wait()
        terms = [red_buf[index, phase, step] for step in range(sizes[phase])]
        while len(terms) > 1:
            terms = [sum(terms[at + 1 : at + 2], terms[at]) for at in range(0, len(terms), 2)]
        return terms[0]

    def whole(value):
        return jnp.sum(jnp.sum(value, axis=0, keepdims=True), axis=1, keepdims=True)

    def packed_row(values):
        row = jnp.zeros((1, 128), F32)
        for number, value in enumerate(values):
            row = jnp.where(lane1 == number, value, row)
        return row

    def entry(row, number):
        return jnp.sum(jnp.where(lane1 == number, row, 0.0), axis=1, keepdims=True)

    def data_dot(a, b):
        return whole(a[0] * b[0] + a[1] * b[1])

    def source_dot(a, b):
        total = jnp.zeros((ROWS, 128), F32)
        for moment in range(2):
            for k in range(5):
                total = total + a[moment, :, lanes(k)] * b[moment, :, lanes(k)]
        return whole(total)

    def load_rhs(ref, magnetic):
        for block in range(10 if magnetic else 5):
            high, low = split(ref[:, lanes(block)])
            rhs[0:80, lanes(block)] = high
            rhs[80:160, lanes(block)] = low
            rhs[160:240, lanes(block)] = high

    def own_rates(field, result, halves, magnetic):
        if not magnetic:
            prod[:, 0:HALF] = dot(inner[...], rhs[:, 0:HALF])
        elif len(halves) == 1:
            prod[:, HALF:WIDE] = dot(inner[...], rhs[:, HALF:WIDE])
        else:
            prod[...] = dot(inner[...], rhs[...])
        for half in halves:
            own0, other0 = half * 5, (1 - half) * 5
            sign = 1.0 if half == 0 else -1.0
            for k in range(5):
                if half == 0 and not magnetic:
                    change = -sig[:, lanes(k)] * field[:, lanes(k)]
                    upper = change[0:QROWS]
                    if k == 0:
                        inward = pltpu.roll(field[0:QROWS, lanes(4)], 1, 1)
                        edge = -tag_low * field[0:QROWS, lanes(0)]
                        upper = upper + spread[2][0:QROWS] * jnp.where(lane56 == 0, edge, inward)
                    elif k == 4:
                        inward = pltpu.roll(field[0:QROWS, lanes(0)], 127, 1)
                        edge = -tag_high * field[0:QROWS, lanes(4)]
                        upper = upper + spread[2][0:QROWS] * jnp.where(lane56 == 127, edge, inward)
                    result[0:QROWS, lanes(k)] = upper
                    result[QROWS:ROWS, lanes(k)] = change[QROWS:ROWS]
                    continue
                slope = None
                for m in range(5):
                    if m != k and abs(deriv[k, m]) > 1e-12:
                        term = float(deriv[k, m]) * prod[80:136, lanes(other0 + m)]
                        slope = term if slope is None else slope + term
                decay = sig[:, lanes(k)] if half == 0 else spread[1 if k in (0, 4) else 0]
                change = sign * prod[0:80, lanes(other0 + k)] - decay * field[:, lanes(own0 + k)]
                upper = change[0:QROWS] - sign * slope
                if k in (0, 4):
                    own_low, turn_low = field[0:QROWS, lanes(own0)], prod[80:136, lanes(other0)]
                    own_high, turn_high = field[0:QROWS, lanes(own0 + 4)], prod[80:136, lanes(other0 + 4)]
                    if half == 1:
                        turn_low, turn_high = -turn_low, -turn_high
                    if k == 0:
                        inward = pltpu.roll(own_high + turn_high, 1, 1)
                        edge = (tag_low * -sign) * (own_low - turn_low)
                        incoming = jnp.where(lane56 == 0, edge, inward)
                    else:
                        inward = pltpu.roll(own_low - turn_low, 127, 1)
                        edge = (tag_high * -sign) * (own_high + turn_high)
                        incoming = jnp.where(lane56 == 127, edge, inward)
                    upper = upper + spread[2][0:QROWS] * incoming
                result[0:QROWS, lanes(own0 + k)] = upper
                result[QROWS:ROWS, lanes(own0 + k)] = change[QROWS:ROWS]

    def pack_face(out, face, buf):
        base = face * 16
        mixed = jnp.zeros((8, 128), F32)
        for k in range(5):
            buf[8 * k : 8 * k + 8, :] = out[base : base + 8, lanes(k)]
            if k < 4:
                mixed = jnp.where((sub8 >= 2 * k) & (sub8 < 2 * k + 2), out[base + 8 : base + 16, lanes(k)], mixed)
        buf[40:48, :] = mixed
        buf[48:56, :] = out[base + 8 : base + 16, lanes(4)]

    def kept(k):
        start = 2 * k if k < 4 else 0
        return (sub8 >= start) & (sub8 < start + 2)

    def unpack_face(buf, k):
        mixed = buf[40:48, :] if k < 4 else buf[48:56, :]
        return jnp.concatenate([buf[8 * k : 8 * k + 8, :], jnp.where(kept(k), mixed, 0.0)], axis=0)

    def set_ghosts(face, k, piece):
        high, low = split(strength * piece)
        ghost_rhs[face * 16 : face * 16 + 16, lanes(k)] = high
        ghost_rhs[64 + face * 16 : 64 + face * 16 + 16, lanes(k)] = low

    def prepare(slot, magnetic):
        load_rhs(fields, magnetic)
        out = dot(send_e[...], rhs[:, 0:HALF])
        if magnetic:
            out = out + dot(send_h[...], rhs[:, HALF:WIDE])
        for face in range(FACES):
            pack_face(out, face, send_buf.at[slot, face])
        for diag in range(4):
            base = 64 + diag * 8
            for tile in range(3):
                piece = out[base : base + 8, lanes(2 * tile)]
                if tile < 2:
                    piece = jnp.where(sub8 < 4, piece, out[base : base + 8, lanes(2 * tile + 1)])
                send_diag[slot, diag, 8 * tile : 8 * tile + 8, :] = piece

    def stage(slot, prepared, first_rates, early, make_second, late, merge, halves_1, halves_2, magnetic_1, magnetic_2, share):
        if not prepared:
            prepare(slot, magnetic_1)
        copies = [
            remote(
                send_buf.at[slot, face], recv_buf.at[slot, face], send_sem.at[slot, face], recv_sem.at[slot, face],
                beside[face],
            )
            for face in range(FACES)
        ]
        for copy, exists in zip(copies, to_face):
            start(copy, exists)
        corner_copies = [
            remote(
                send_diag.at[slot, diag], recv_diag.at[slot, diag], diag_send_sem.at[slot, diag],
                diag_recv_sem.at[slot, diag], across[diag],
            )
            for diag in range(4)
        ]
        for copy, exists in zip(corner_copies, to_diag):
            start(copy, exists)
        early()
        own_rates(fields, first_rates, halves_1, magnetic_1)
        make_second()
        load_rhs(second, magnetic_2)
        out = dot(send_e[0:64, :], rhs[:, 0:HALF])
        if magnetic_2:
            out = out + dot(send_h[0:64, :], rhs[:, HALF:WIDE])
        next_copies = []
        for face in range(FACES):
            pack_face(out, face, send_next.at[slot, face])
            next_copies.append(
                remote(
                    send_next.at[slot, face], recv_next.at[slot, face], next_send_sem.at[slot, face],
                    next_recv_sem.at[slot, face], beside[face],
                )
            )
            start(next_copies[face], to_face[face])
        late()

        wait_all(copies, to_face, 1)
        for face in range(FACES):
            for k in range(5):
                set_ghosts(face, k, unpack_face(recv_buf.at[slot, face], k))
        merge(dot(lift[...], ghost_rhs[...]))
        load_rhs(second, magnetic_2)
        own_rates(second, rates, halves_2, magnetic_2)

        wait_all(corner_copies, to_diag, 3)
        for two in range(2):
            for k in range(5):
                pieces = []
                for diag in (2 * two, 2 * two + 1):
                    tile = recv_diag[slot, diag, 8 * (k // 2) : 8 * (k // 2) + 8, :]
                    tile = jnp.where(sub8 >= 4 if k % 2 else sub8 < 4, tile, 0.0)
                    pieces.append(strength * tile)
                high, low = split(jnp.concatenate(pieces, axis=0))
                corner_rhs[16 * two : 16 * two + 16, lanes(k)] = high
                corner_rhs[32 + 16 * two : 32 + 16 * two + 16, lanes(k)] = low
        begin = at_corner + (0 if magnetic_2 else 64)
        extra = dot(mats[begin : begin + 64, 0:64], corner_rhs[...])
        wait_all(next_copies, to_face, 1)
        for face in range(FACES):
            for k in range(5):
                piece = extra[face * 16 : face * 16 + 16, lanes(k)]
                piece = jnp.concatenate([piece[0:8], jnp.where(kept(k), piece[8:16], 0.0)], axis=0)
                if not magnetic_2:
                    piece = piece + strength * unpack_face(send_buf.at[slot, face ^ 1], k)
                    piece = piece * gain_out[face * 16 : face * 16 + 16, lanes(k)]
                set_ghosts(face, k, unpack_face(recv_next.at[slot, face], k) + share * piece)
        if len(halves_2) == 2:
            lifted = dot(lift[...], ghost_rhs[...])
            rates[:, 0:HALF] += lifted[0:ROWS]
            rates[:, HALF:WIDE] += lifted[ROWS : 2 * ROWS]
        else:
            rates[:, 0:HALF] += dot(lift[0:ROWS, :], ghost_rhs[...])

    def inject(turn, moment):
        values = jnp.where(
            comp_id == 0,
            left[turn, moment, 0:1, :],
            jnp.where(comp_id == 1, left[turn, moment, 1:2, :], left[turn, moment, 2:3, :]),
        )
        high, low = split(pick_row[...] * values)
        return dot(jnp.concatenate([high, low], axis=1), pick_back[...])

    def gather(halves, turn, moment):
        both = dot(halves, pick_lane[...])
        chosen = (both[0:ROWS] + both[ROWS : 2 * ROWS]) * pick_row[...]
        out = jnp.zeros((8, 128), F32)
        for comp in range(3):
            part = jnp.sum(jnp.where(comp_id == comp, chosen, 0.0), axis=0, keepdims=True)
            out = jnp.where(sub8 == comp, part, out)
        left[turn, moment] = out

    def to_output_order(vector, number):
        for moment in range(2):
            both = dot_nt(jnp.concatenate(split(vector[moment]), axis=0), order[...])
            both = both[0:ROWS] + both[ROWS : 2 * ROWS]
            for block in range(5):
                perm_out[number, block, pl.ds(moment, ROWS, stride=2), :] = both[:, lanes(block)]

    every, electric = (0, 1), (0,)

    def sweep(turn, carry):
        def second_1():
            pass

        def merge_1(lifted):
            second[:, 0:HALF] += lifted[0:ROWS]
            second[:, HALF:WIDE] += lifted[ROWS : 2 * ROWS]

        def late_1():
            meet(turn, 0, -1, 0)
            held[...] = inject(turn, 0)

            @pl.when(turn == 1)
            def _():
                gather(jnp.concatenate(split(saved[...]), axis=0), 1, 1)
                reduce_send(
                    0, 0, packed_row([data_dot(left[0], left[0]), source_dot(source.at[0], source.at[0])])
                )
                to_output_order(source.at[0], 0)

        stage(turn * 3, True, second, lambda: meet(turn, 1, 4, 5), second_1, late_1, merge_1, every, every, False, True, 1.0)
        for k in range(5):
            source[turn, 1, :, lanes(k)] = gain[:, lanes(k)] * (fields[:, lanes(k)] + 0.5 * second[:, lanes(k)])
        fields[:, 0:HALF] = held[...] + fields[:, 0:HALF] + second[:, 0:HALF] + 0.5 * rates[:, 0:HALF]
        fields[:, HALF:WIDE] = second[:, HALF:WIDE] + 0.5 * rates[:, HALF:WIDE]

        def second_2():
            for k in range(5):
                amount = gain[:, lanes(k)] * (fields[:, lanes(k)] + 0.5 * rates[:, lanes(k)])
                source[turn, 0, :, lanes(k)] = amount
                second[:, lanes(k)] = gain[:, lanes(k)] * amount
            second[:, HALF:WIDE] = jnp.zeros((ROWS, HALF), F32)

        def merge_2(lifted):
            for k in range(5):
                amount = source[turn, 0, :, lanes(k)] + 0.5 * gain[:, lanes(k)] * lifted[0:ROWS, lanes(k)]
                source[turn, 0, :, lanes(k)] = amount
                second[:, lanes(k)] = gain[:, lanes(k)] * amount

        def late_2():
            meet(turn, 0, 1, 2)

            @pl.when(turn == 1)
            def _():
                reduce_send(0, 1, reduce_take(0, 0))

            @pl.when(turn == 0)
            def _():
                wait_all(support_copies, to_face, 1)
                for face in range(FACES):
                    for k in range(5):
                        column = float(root[k] ** 2) * cols_ref[face * 16 : face * 16 + 16, 5:6]
                        gain_out[face * 16 : face * 16 + 16, lanes(k)] = column * beside_support[face]

        stage(turn * 3 + 1, False, rates, lambda: meet(turn, 0, 0, 1), second_2, late_2, merge_2, electric, every, True, False, 0.5)
        for k in range(5):
            first = second[:, lanes(k)] + 0.5 * rates[:, lanes(k)]
            fields[:, lanes(k)] = first
            held[:, lanes(k)] = first
        fields[:, HALF:WIDE] = 0.5 * rates[:, HALF:WIDE]

        def early_3():
            meet(turn, 0, 2, 3)

        def second_3():
            for k in range(5):
                drive = gain[:, lanes(k)] * source[turn, 1, :, lanes(k)]
                second[:, lanes(k)] = fields[:, lanes(k)] + 0.5 * (rates[:, lanes(k)] + drive)
                fields[:, lanes(k)] = fields[:, lanes(k)] + drive
            second[:, HALF:WIDE] = fields[:, HALF:WIDE] + 0.5 * rates[:, HALF:WIDE]

        def merge_3(lifted):
            second[:, 0:HALF] += 0.5 * lifted[0:ROWS]
            second[:, HALF:WIDE] += 0.5 * lifted[ROWS : 2 * ROWS]

        def late_3():
            meet(turn, 0, 3, 4)
            gather(jnp.concatenate(split(held[...]), axis=0), turn + 1, 0)

            @pl.when(turn == 1)
            def _():
                norms = reduce_take(0, 1)
                red_buf[0, 0, 0] = norms
                ratio = entry(norms, 1) / entry(norms, 0)
                for moment in range(2):
                    for k in range(5):
                        ortho[moment, :, lanes(k)] = (
                            source[1, moment, :, lanes(k)] - ratio * source[0, moment, :, lanes(k)]
                        )
                dots = [
                    source_dot(ortho, ortho), source_dot(ortho, source.at[0]), data_dot(left[1], left[1]),
                ]
                for moment in range(2):
                    left[0, moment] = left[1, moment] - ratio * left[0, moment]
                dots += [data_dot(left[0], left[0]), data_dot(left[1], left[0])]
                red_buf[0, 1, 0] = packed_row(dots)
                to_output_order(ortho, 1)

        stage(turn * 3 + 2, False, rates, early_3, second_3, late_3, merge_3, every, electric, True, True, 0.5)

        @pl.when(turn == 0)
        def _():
            for k in range(5):
                last = fields[:, lanes(k)] + rates[:, lanes(k)]
                saved[:, lanes(k)] = last
                fields[:, lanes(k)] = multiple[:, lanes(k)] * last
            fields[:, HALF:WIDE] = jnp.zeros((ROWS, HALF), F32)
            prepare(3, False)

        return carry

    fields[:, 0:HALF] = inject(0, 1)
    fields[:, HALF:WIDE] = jnp.zeros((ROWS, HALF), F32)
    prepare(0, False)
    pl.semaphore_wait(barrier, greeted)
    for copy, exists in zip(support_copies, to_face):
        start(copy, exists)
    lax.fori_loop(0, 2, sweep, 0)
    gather(jnp.concatenate(split(fields[:, 0:HALF] + rates[:, 0:HALF]), axis=0), 2, 1)

    norms = red_buf[0, 0, 0]
    sq_b, sq_g = entry(norms, 0), entry(norms, 1)
    ratio = sq_g / sq_b
    for moment in range(2):
        left[2, moment] = left[2, moment] - ratio * left[1, moment]
    p, f, h = left[0], left[1], left[2]
    row = red_buf[0, 1, 0]
    for number, value in ((5, data_dot(h, h)), (6, data_dot(h, f)), (7, data_dot(h, p))):
        row = jnp.where(lane1 == number, value, row)
    reduce_send(1, 0, row)
    reduce_send(1, 1, reduce_take(1, 0))
    total = reduce_take(1, 1)
    oo, og, ff, pp, fp, hh, hf, hp = (entry(total, number) for number in range(8))
    take = pp / sq_g
    sq_q = jnp.maximum(oo - 2.0 * take * og + take * take * sq_g, 0.0)
    beta_1 = jnp.sqrt(sq_b)
    alpha_1 = jnp.sqrt(ratio)
    beta_2 = jnp.sqrt(take)
    alpha_2 = jnp.sqrt(sq_q / pp)
    sq_w = hh - 2.0 * take * hf + take * take * ff
    sq_beta_3 = jnp.maximum(sq_w / sq_q - 2.0 * (hp - take * fp) / pp + sq_q / pp, 0.0)
    rho_1 = jnp.sqrt(alpha_1 * alpha_1 + beta_2 * beta_2)
    cosine, sine = alpha_1 / rho_1, beta_2 / rho_1
    step_1 = cosine * beta_1 / rho_1
    phi_bar = sine * beta_1
    theta = sine * alpha_2
    rho_bar = -cosine * alpha_2
    rho_2 = jnp.sqrt(rho_bar * rho_bar + sq_beta_3)
    step_2 = rho_bar / rho_2 * phi_bar / rho_2
    on_ortho = step_2 / jnp.sqrt(sq_q)
    on_first = (step_1 - step_2 * theta / rho_1) / jnp.sqrt(sq_g) - on_ortho * take
    on_h = phi_bar / rho_2 / jnp.sqrt(sq_q)
    on_p = phi_bar / rho_2 * jnp.sqrt(sq_q) / pp
    for moment in range(2):
        out = on_h * (h[moment] - take * f[moment]) - on_p * p[moment]
        for comp in range(3):
            res_ref[comp, moment : moment + 1, :] = out[comp : comp + 1, :]
    for tile in range(19):
        rows = slice(8 * tile, 8 * tile + 8)
        for block in range(5):
            value = on_first * perm_out[0, block, rows, :] + on_ortho * perm_out[1, block, rows, :]
            for part in range(4):
                node = 4 * tile + part
                if node < 75:
                    est_ref[node // 25, node // 5 % 5, node % 5, :, lanes(block)] = value[2 * part : 2 * part + 2, :]


def solution(mesh):
    n_gx, n_gy = mesh.shape["gx"], mesh.shape["gy"]
    matrices, columns = tables()

    def shards(probe_data, conductivity, support, face_tags, probe_nodes):
        vmem = pl.BlockSpec(memory_space=pltpu.VMEM)
        anywhere = pl.BlockSpec(memory_space=pl.ANY)
        estimate, residual = pl.pallas_call(
            functools.partial(kernel, n_gx, n_gy),
            out_shape=(
                jax.ShapeDtypeStruct((3, 5, 5, 2, HALF), F32),
                jax.ShapeDtypeStruct((3, 2, 128), F32),
            ),
            in_specs=[anywhere] * 7,
            out_specs=(vmem, vmem),
            scratch_shapes=[
                pltpu.VMEM((1, 1, 2), jnp.int32),
                pltpu.VMEM((3, 2, 128), F32),
                pltpu.VMEM((5, 5, HALF), F32),
                pltpu.VMEM((1, 1, 128), jnp.int32),
                pltpu.VMEM((1, 128), jnp.int32),
                pltpu.VMEM(matrices.shape, F32),
                pltpu.VMEM(columns.shape, F32),
                pltpu.VMEM(matrices.shape, BF16),
                pltpu.VMEM((HALF, HALF), BF16),
                pltpu.VMEM((3, ROWS, 128), F32),
                pltpu.VMEM((ROWS, WIDE), F32),
                pltpu.VMEM((ROWS, WIDE), F32),
                pltpu.VMEM((ROWS, WIDE), F32),
                pltpu.VMEM((ROWS, HALF), F32),
                pltpu.VMEM((ROWS, HALF), F32),
                pltpu.VMEM((ROWS, HALF), F32),
                pltpu.VMEM((256, WIDE), BF16),
                pltpu.VMEM((INNER, WIDE), F32),
                pltpu.VMEM((128, HALF), BF16),
                pltpu.VMEM((64, HALF), BF16),
                pltpu.VMEM((ROWS, HALF), F32),
                pltpu.VMEM((ROWS, HALF), F32),
                pltpu.VMEM((64, HALF), F32),
                pltpu.VMEM((ROWS, 128), F32),
                pltpu.VMEM((HALF, 128), BF16),
                pltpu.VMEM((256, HALF), BF16),
                pltpu.VMEM((3, 2, 8, 128), F32),
                pltpu.VMEM((2, 2, ROWS, HALF), F32),
                pltpu.VMEM((2, ROWS, HALF), F32),
                pltpu.VMEM((ROWS, HALF), F32),
                pltpu.VMEM((2, 5, 2 * ROWS, 128), F32),
                pltpu.VMEM((FACES, 1, 128), F32),
                pltpu.VMEM((1, 128), F32),
                pltpu.VMEM((6, FACES, QROWS, 128), F32),
                pltpu.VMEM((6, FACES, QROWS, 128), F32),
                pltpu.VMEM((6, FACES, QROWS, 128), F32),
                pltpu.VMEM((6, FACES, QROWS, 128), F32),
                pltpu.VMEM((6, 4, 24, 128), F32),
                pltpu.VMEM((6, 4, 24, 128), F32),
                pltpu.VMEM((2, 2, max(n_gx, n_gy), 1, 128), F32),
                pltpu.SemaphoreType.DMA((7,)),
                pltpu.SemaphoreType.DMA((6, FACES)),
                pltpu.SemaphoreType.DMA((6, FACES)),
                pltpu.SemaphoreType.DMA((6, FACES)),
                pltpu.SemaphoreType.DMA((6, FACES)),
                pltpu.SemaphoreType.DMA((6, 4)),
                pltpu.SemaphoreType.DMA((6, 4)),
                pltpu.SemaphoreType.DMA((2, 2)),
                pltpu.SemaphoreType.DMA((2, 2)),
                pltpu.SemaphoreType.DMA((FACES,)),
                pltpu.SemaphoreType.DMA((FACES,)),
                pltpu.SemaphoreType.REGULAR((5,)),
            ],
            compiler_params=pltpu.CompilerParams(
                collective_id=0, has_side_effects=True, vmem_limit_bytes=22 * 1024 * 1024
            ),
        )(
            *(
                pltpu.with_memory_space_constraint(array, pltpu.HBM)
                for array in (
                    jnp.transpose(face_tags, (1, 2, 0)), jnp.transpose(probe_data, (1, 0, 2)), conductivity, support,
                    probe_nodes.reshape(1, 128), jnp.asarray(matrices), jnp.asarray(columns),
                )
            )
        )
        return jnp.transpose(estimate, (3, 0, 1, 2, 4)), jnp.transpose(residual, (1, 0, 2))

    return jax.shard_map(
        shards,
        mesh=mesh,
        in_specs=(
            P(None, None, ("gx", "gy")),
            P("gx", "gy", None),
            P("gx", "gy", None),
            P(None, "gx", "gy"),
            P(("gx", "gy")),
        ),
        out_specs=(P(None, None, "gx", "gy", None), P(None, None, ("gx", "gy"))),
        check_vma=False,
    )
```

```python
import functools
import math

import jax
import jax.numpy as jnp
import numpy as np
from jax import lax
from jax.experimental import pallas as pl
from jax.experimental.pallas import tpu as pltpu
from jax.sharding import PartitionSpec as P

MESH = pl.DeviceIdType.MESH
F32 = jnp.float32
BF16 = jnp.bfloat16

STEP_SIZE = 0.02
LIFT_HALF = 5.0
DRIVE_GAIN = 50.0
ROWS = 80
QROWS = 56
HALF = 640
WIDE = 1280
INNER = 144
SENT = 96
FACES = 4
DIAGS = ((-1, -1), (-1, 1), (1, -1), (1, 1))
CHARS = (
    ((1, 2, 1.0), (2, 1, -1.0)),
    ((1, 2, -1.0), (2, 1, 1.0)),
    ((0, 2, -1.0), (2, 0, 1.0)),
    ((0, 2, 1.0), (2, 0, -1.0)),
)
SIDES = ((0, 4, 0), (0, 0, 4), (1, 4, 0), (1, 0, 4))


def lobatto_scaled():
    radical = math.sqrt(3.0 / 7.0)
    points = np.array([-1.0, -radical, 0.0, radical, 1.0])
    legendre = (35.0 * points**4 - 30.0 * points**2 + 3.0) / 8.0
    weights = 0.1 / legendre**2
    matrix = np.zeros((5, 5))
    for i in range(5):
        for j in range(5):
            if i != j:
                matrix[i, j] = legendre[i] / (legendre[j] * (points[i] - points[j]))
    root = np.sqrt(weights)
    return matrix * root[:, None] / root[None, :], root


def row_of(comp, i, j):
    return comp * 25 + 5 * i + j


def split_np(matrix):
    high = np.asarray(matrix, np.float32).astype(jnp.bfloat16)
    low = (np.asarray(matrix, np.float32) - high.astype(np.float32)).astype(jnp.bfloat16)
    return high, low


def tables():
    deriv, root = lobatto_scaled()
    deriv = STEP_SIZE * deriv
    curl = np.zeros((ROWS, ROWS))
    turn = np.zeros((QROWS, ROWS))
    for i in range(5):
        for j in range(5):
            for k in range(5):
                curl[row_of(0, i, j), row_of(2, i, k)] += deriv[j, k]
                curl[row_of(1, i, j), row_of(2, k, j)] -= deriv[i, k]
                curl[row_of(2, i, j), row_of(1, k, j)] += deriv[i, k]
                curl[row_of(2, i, j), row_of(0, i, k)] -= deriv[j, k]
            turn[row_of(0, i, j), row_of(1, i, j)] = 1.0
            turn[row_of(1, i, j), row_of(0, i, j)] = -1.0
    high, low = split_np(curl)
    inner = np.zeros((INNER, 256), np.float32)
    inner[:ROWS, 0:80] = high
    inner[:ROWS, 80:160] = high
    inner[:ROWS, 160:240] = low
    inner[ROWS : ROWS + QROWS, 0:80] = turn
    inner[ROWS : ROWS + QROWS, 80:160] = turn

    send_e = np.zeros((SENT, 256), np.float32)
    send_h = np.zeros((SENT, 256), np.float32)
    lift = np.zeros((2 * ROWS, 256), np.float32)
    corner = np.zeros((128, 256), np.float32)
    slot_weight = np.zeros(64)
    for face in range(FACES):
        axis, node_out, node_in = SIDES[face]
        for slot in range(16):
            char = slot if slot < 8 else 8 + slot % 2
            which, along = char // 5, char % 5
            comp_e, comp_h, sign = CHARS[face][which]
            spot_out = (node_out, along) if axis == 0 else (along, node_out)
            spot_in = (node_in, along) if axis == 0 else (along, node_in)
            at = face * 16 + slot
            slot_weight[at] = root[0] ** 2 * root[along] ** 2
            for part in (0, 80):
                send_e[at, part + row_of(comp_e, *spot_out)] = 1.0
                send_h[at, part + row_of(comp_h, *spot_out)] = sign
            for part in (0, 64):
                lift[row_of(comp_e, *spot_in), part + at] = 1.0
                lift[ROWS + row_of(comp_h, *spot_in), part + at] = sign
            for diag, (side_x, side_y) in enumerate(DIAGS):
                if axis == 0:
                    if side_x != (-1 if face == 0 else 1):
                        continue
                    other, first = (2 if side_y < 0 else 3), 2
                else:
                    if side_y != (-1 if face == 2 else 1):
                        continue
                    other, first = (0 if side_x < 0 else 1), 0
                if along != SIDES[other][2]:
                    continue
                for number, (other_e, other_h, other_sign) in enumerate(CHARS[other]):
                    only_e = float(comp_e == other_e)
                    both = only_e + sign * other_sign * float(comp_h == other_h)
                    for part in (0, 4, 32, 36):
                        column = diag * 8 + first + number + part
                        corner[at, column] = both
                        corner[64 + at, column] = only_e
    for diag, (side_x, side_y) in enumerate(DIAGS):
        spot = (4 if side_x < 0 else 0, 4 if side_y < 0 else 0)
        for slot in range(8):
            face = ((0 if side_x < 0 else 1), (2 if side_y < 0 else 3))[slot % 4 // 2]
            comp_e, comp_h, sign = CHARS[face][slot % 2]
            for part in (0, 80):
                send_e[64 + diag * 8 + slot, part + row_of(comp_e, *spot)] = 1.0
                send_h[64 + diag * 8 + slot, part + row_of(comp_h, *spot)] = sign
    matrices = np.concatenate([inner, send_e, send_h, lift, corner], axis=0)

    columns = np.zeros((ROWS, 128), np.float32)
    strength = STEP_SIZE * LIFT_HALF
    for comp in range(3):
        for i in range(5):
            for j in range(5):
                row = row_of(comp, i, j)
                columns[row, 0] = root[i] * root[j]
                columns[row, 1] = 1.0 / (root[i] * root[j])
                count = (i in (0, 4)) * (comp != 0) + (j in (0, 4)) * (comp != 1)
                columns[row, 2] = strength * count
                columns[row, 3] = strength * (count + (comp != 2))
                columns[row, 4] = strength * (comp != 2)
    columns[0:64, 5] = (DRIVE_GAIN * STEP_SIZE) ** 2 * slot_weight
    return matrices, columns


def split(value):
    high = value.astype(BF16)
    return high, (value - high.astype(F32)).astype(BF16)


def dot(a, b):
    return jnp.dot(a, b, preferred_element_type=F32)


def dot_nt(a, b):
    return lax.dot_general(a, b, (((1,), (1,)), ((), ())), preferred_element_type=F32)


def lanes(block):
    return slice(block * 128, block * 128 + 128)


def kernel(
    n_gx, n_gy, tags_hbm, data_hbm, cond_hbm, supp_hbm, nodes_hbm, mats_hbm, cols_hbm, est_ref, res_ref,
    tags_ref, data_ref, cond_ref, supp_ref, nodes_ref, mats_ref, cols_ref, mats, order, spread,
    fields, second, rates, saved, held, multiple, rhs, prod, ghost_rhs, corner_rhs, sig, gain, gain_out, pick_row, pick_lane, pick_back,
    left, source, ortho, perm, perm_out, beside_support, own_support,
    send_buf, recv_buf, send_next, recv_next, send_diag, recv_diag, red_buf,
    load_sem, send_sem, recv_sem, next_send_sem, next_recv_sem, diag_send_sem, diag_recv_sem, red_send_sem, red_recv_sem,
    supp_send_sem, supp_recv_sem, meet_sem,
):
    loads = []
    pairs = (
        (data_hbm, data_ref), (nodes_hbm, nodes_ref), (mats_hbm, mats_ref), (cols_hbm, cols_ref),
        (cond_hbm, cond_ref), (supp_hbm, supp_ref), (tags_hbm, tags_ref),
    )
    for number, (far, near) in enumerate(pairs):
        load = pltpu.make_async_copy(far, near, load_sem.at[number])
        load.start()
        loads.append(load)

    deriv, root = lobatto_scaled()
    deriv = STEP_SIZE * deriv
    gx, gy = lax.axis_index("gx"), lax.axis_index("gy")
    sizes = (n_gx, n_gy)

    def partner(phase, step):
        if phase == 0:
            return (lax.rem(gx + step, n_gx), gy)
        return (gx, lax.rem(gy + step, n_gy))

    def near_by(step_x, step_y):
        return (lax.rem(gx + n_gx + step_x, n_gx), lax.rem(gy + n_gy + step_y, n_gy))

    beside = (near_by(1, 0), near_by(-1, 0), near_by(0, 1), near_by(0, -1))
    across = tuple(near_by(-side_x, -side_y) for side_x, side_y in DIAGS)
    strength = STEP_SIZE * LIFT_HALF
    has = {(0, -1): gx > 0, (0, 1): gx < n_gx - 1, (1, -1): gy > 0, (1, 1): gy < n_gy - 1}
    to_face = tuple(has[key] for key in ((0, 1), (0, -1), (1, 1), (1, -1)))
    to_diag = tuple(has[(0, -side_x)] & has[(1, -side_y)] for side_x, side_y in DIAGS)

    for face in range(FACES):

        @pl.when(jnp.logical_not(to_face[face ^ 1]))
        def _():
            for slot in range(6):
                recv_buf[slot, face] = jnp.zeros((QROWS, 128), F32)
                recv_next[slot, face] = jnp.zeros((QROWS, 128), F32)
            beside_support[face] = jnp.zeros((1, 128), F32)

    for diag in range(4):

        @pl.when(jnp.logical_not(to_diag[3 - diag]))
        def _():
            for slot in range(6):
                recv_diag[slot, diag] = jnp.zeros((24, 128), F32)

    barrier = pltpu.get_barrier_semaphore()
    greeted = jnp.int32(0)
    for device, exists in zip(beside + across, to_face + to_diag):

        @pl.when(exists)
        def _():
            pl.semaphore_signal(barrier, inc=1, device_id=device, device_id_type=MESH)

        greeted = greeted + exists.astype(jnp.int32)

    def remote(src, dst, sem_out, sem_in, device):
        copy = pltpu.make_async_remote_copy(
            src_ref=src, dst_ref=dst, send_sem=sem_out, recv_sem=sem_in, device_id=device, device_id_type=MESH
        )
        return copy

    def start(copy, exists):
        @pl.when(exists)
        def _():
            copy.start()

    def wait_all(copies, exist, flip):
        for number, exists in enumerate(exist):
            back = number ^ flip

            @pl.when(exists)
            def _():
                copies[number].wait_send()
                copies[back].wait_recv()

    z_id = lax.broadcasted_iota(jnp.int32, (HALF, 128), 0)
    five = 5 * lax.broadcasted_iota(jnp.int32, (HALF, 128), 1)
    for k in range(5):
        order[:, lanes(k)] = jnp.where(z_id == five + k, 1.0, 0.0).astype(BF16)
    rhs[240:256, :] = jnp.zeros((16, WIDE), BF16)
    left[...] = jnp.zeros_like(left)
    perm[...] = jnp.zeros_like(perm)
    sub8 = lax.broadcasted_iota(jnp.int32, (8, 128), 0)
    lane56 = lax.broadcasted_iota(jnp.int32, (QROWS, 128), 1)
    lane1 = lax.broadcasted_iota(jnp.int32, (1, 128), 1)
    row_id = lax.broadcasted_iota(jnp.int32, (ROWS, 128), 0)
    comp_id = (row_id >= 25).astype(jnp.int32) + (row_id >= 50).astype(jnp.int32) + (row_id >= 75).astype(jnp.int32)
    spot_id = (row_id - 25 * comp_id).astype(F32)

    for load in loads:
        load.wait()
    mats[...] = mats_ref[...].astype(BF16)
    at_e, at_h, at_lift, at_corner = INNER, INNER + SENT, INNER + 2 * SENT, INNER + 2 * SENT + 2 * ROWS
    inner = mats.at[0:INNER]
    send_e, send_h = mats.at[at_e:at_h], mats.at[at_h:at_lift]
    lift = mats.at[at_lift:at_corner, 0:128]
    for number in range(3):
        spread[number] = jnp.broadcast_to(cols_ref[:, 2 + number : 3 + number], (ROWS, 128))

    node = nodes_ref[...].astype(F32)
    pair = jnp.floor((node + 0.5) * (1.0 / HALF))
    depth = node - float(HALF) * pair
    element = jnp.floor((depth + 0.5) * 0.2)
    inside = depth - 5.0 * element
    weight = jnp.zeros_like(node)
    for k in range(5):
        weight = jnp.where(inside == float(k), float(1.0 / root[k]), weight)
    pick_row[...] = jnp.where(spot_id == pair, cols_ref[:, 1:2] * weight, 0.0)
    sub_id = lax.broadcasted_iota(jnp.int32, (128, 128), 0).astype(F32)
    for k in range(5):
        hot = jnp.where((sub_id == element) & (inside == float(k)), 1.0, 0.0)
        pick_lane[lanes(k), :] = hot.astype(BF16)
        flipped = jnp.transpose(hot).astype(BF16)
        pick_back[0:128, lanes(k)] = flipped
        pick_back[128:256, lanes(k)] = flipped
    high, low = split(pick_row[...] * pick_row[...])
    multiple[...] = dot(jnp.concatenate([high, low], axis=1), pick_back[...])
    for comp in range(3):
        for moment in range(2):
            left[0, moment, comp : comp + 1, :] = data_ref[comp, moment : moment + 1, :]

    tag_low = tags_ref[0][:, 0:1].astype(F32)
    tag_high = tags_ref[0][:, 1:2].astype(F32)
    for comp in range(3):
        for i in range(5):
            perm[comp * 25 + i * 5 : comp * 25 + i * 5 + 5, :] = cond_ref[i]
    halves = jnp.concatenate(split(perm[0:ROWS, :]), axis=0)
    for k in range(5):
        both = dot(halves, order[:, lanes(k)])
        sig[:, lanes(k)] = STEP_SIZE * (both[0:ROWS] + both[ROWS : 2 * ROWS]) + spread[1 if k in (0, 4) else 0]
    support = supp_ref[0].astype(F32)
    for k in range(5):
        gain[:, lanes(k)] = (-DRIVE_GAIN * STEP_SIZE * float(root[k])) * support * cols_ref[:, 0:1]
    own_support[...] = support

    support_copies = [
        remote(
            own_support, beside_support.at[face], supp_send_sem.at[face], supp_recv_sem.at[face], beside[face]
        )
        for face in range(FACES)
    ]

    rounds = 0
    while 2**rounds < max(n_gx, n_gy):
        rounds += 1

    def meet(turn, when, taken, sent):
        def beyond(number):
            for at, size, along_x in ((gx, n_gx, True), (gy, n_gy, False)):
                distance = 2**number
                if distance < size:
                    yield at >= distance, ((gx - distance, gy) if along_x else (gx, gy - distance))
                    yield at < size - distance, ((gx + distance, gy) if along_x else (gx, gy + distance))

        @pl.when(turn == when)
        def _():
            if 0 <= taken < rounds:
                count = jnp.int32(0)
                for exists, _ in beyond(taken):
                    count = count + exists.astype(jnp.int32)
                pl.semaphore_wait(meet_sem.at[taken], count)
            if sent < rounds:
                for exists, device in beyond(sent):

                    @pl.when(exists)
                    def _():
                        pl.semaphore_signal(meet_sem.at[sent], inc=1, device_id=device, device_id_type=MESH)

    def reduce_send(index, phase, row):
        red_buf[index, phase, 0] = row
        size = sizes[phase]
        for step in range(1, size):
            remote(
                red_buf.at[index, phase, 0], red_buf.at[index, phase, step], red_send_sem.at[index, phase],
                red_recv_sem.at[index, phase], partner(phase, step),
            ).start()

    def reduce_take(index, phase):
        if sizes[phase] == 1:
            return red_buf[index, phase, 0]
        others = red_buf.at[index, phase, pl.ds(1, sizes[phase] - 1)]
        pltpu.make_async_copy(others, others, red_recv_sem.at[index, phase]).wait()
        pltpu.make_async_copy(others, others, red_send_sem.at[index, phase]).wait()
        terms = [red_buf[index, phase, step] for step in range(sizes[phase])]
        while len(terms) > 1:
            terms = [sum(terms[at + 1 : at + 2], terms[at]) for at in range(0, len(terms), 2)]
        return terms[0]

    def whole(value):
        return jnp.sum(jnp.sum(value, axis=0, keepdims=True), axis=1, keepdims=True)

    def packed_row(values):
        row = jnp.zeros((1, 128), F32)
        for number, value in enumerate(values):
            row = jnp.where(lane1 == number, value, row)
        return row

    def entry(row, number):
        return jnp.sum(jnp.where(lane1 == number, row, 0.0), axis=1, keepdims=True)

    def data_dot(a, b):
        return whole(a[0] * b[0] + a[1] * b[1])

    def source_dot(a, b):
        total = jnp.zeros((ROWS, 128), F32)
        for moment in range(2):
            for k in range(5):
                total = total + a[moment, :, lanes(k)] * b[moment, :, lanes(k)]
        return whole(total)

    def put_rhs(block, value):
        high, low = split(value)
        rhs[0:80, lanes(block)] = high
        rhs[80:160, lanes(block)] = low
        rhs[160:240, lanes(block)] = high

    def own_rates(field, halves, magnetic, emit):
        if not magnetic:
            prod[:, 0:HALF] = dot(inner[...], rhs[:, 0:HALF])
        elif len(halves) == 1:
            prod[:, HALF:WIDE] = dot(inner[...], rhs[:, HALF:WIDE])
        else:
            prod[...] = dot(inner[...], rhs[...])
        for half in halves:
            own0, other0 = half * 5, (1 - half) * 5
            sign = 1.0 if half == 0 else -1.0
            for k in range(5):
                if half == 0 and not magnetic:
                    change = -sig[:, lanes(k)] * field[:, lanes(k)]
                    upper = change[0:QROWS]
                    if k == 0:
                        inward = pltpu.roll(field[0:QROWS, lanes(4)], 1, 1)
                        edge = -tag_low * field[0:QROWS, lanes(0)]
                        upper = upper + spread[2][0:QROWS] * jnp.where(lane56 == 0, edge, inward)
                    elif k == 4:
                        inward = pltpu.roll(field[0:QROWS, lanes(0)], 127, 1)
                        edge = -tag_high * field[0:QROWS, lanes(4)]
                        upper = upper + spread[2][0:QROWS] * jnp.where(lane56 == 127, edge, inward)
                    emit(k, jnp.concatenate([upper, change[QROWS:ROWS]], axis=0))
                    continue
                slope = None
                for m in range(5):
                    if m != k and abs(deriv[k, m]) > 1e-12:
                        term = float(deriv[k, m]) * prod[80:136, lanes(other0 + m)]
                        slope = term if slope is None else slope + term
                decay = sig[:, lanes(k)] if half == 0 else spread[1 if k in (0, 4) else 0]
                change = sign * prod[0:80, lanes(other0 + k)] - decay * field[:, lanes(own0 + k)]
                upper = change[0:QROWS] - sign * slope
                if k in (0, 4):
                    own_low, turn_low = field[0:QROWS, lanes(own0)], prod[80:136, lanes(other0)]
                    own_high, turn_high = field[0:QROWS, lanes(own0 + 4)], prod[80:136, lanes(other0 + 4)]
                    if half == 1:
                        turn_low, turn_high = -turn_low, -turn_high
                    if k == 0:
                        inward = pltpu.roll(own_high + turn_high, 1, 1)
                        edge = (tag_low * -sign) * (own_low - turn_low)
                        incoming = jnp.where(lane56 == 0, edge, inward)
                    else:
                        inward = pltpu.roll(own_low - turn_low, 127, 1)
                        edge = (tag_high * -sign) * (own_high + turn_high)
                        incoming = jnp.where(lane56 == 127, edge, inward)
                    upper = upper + spread[2][0:QROWS] * incoming
                emit(own0 + k, jnp.concatenate([upper, change[QROWS:ROWS]], axis=0))

    def pack_face(out, face, buf):
        base = face * 16
        mixed = jnp.zeros((8, 128), F32)
        for k in range(5):
            buf[8 * k : 8 * k + 8, :] = out[base : base + 8, lanes(k)]
            if k < 4:
                mixed = jnp.where((sub8 >= 2 * k) & (sub8 < 2 * k + 2), out[base + 8 : base + 16, lanes(k)], mixed)
        buf[40:48, :] = mixed
        buf[48:56, :] = out[base + 8 : base + 16, lanes(4)]

    def kept(k):
        start = 2 * k if k < 4 else 0
        return (sub8 >= start) & (sub8 < start + 2)

    def unpack_face(buf, k):
        mixed = buf[40:48, :] if k < 4 else buf[48:56, :]
        return jnp.concatenate([buf[8 * k : 8 * k + 8, :], jnp.where(kept(k), mixed, 0.0)], axis=0)

    def set_ghosts(face, k, piece):
        high, low = split(strength * piece)
        ghost_rhs[face * 16 : face * 16 + 16, lanes(k)] = high
        ghost_rhs[64 + face * 16 : 64 + face * 16 + 16, lanes(k)] = low

    def prepare(slot, magnetic):
        out = dot(send_e[...], rhs[:, 0:HALF])
        if magnetic:
            out = out + dot(send_h[...], rhs[:, HALF:WIDE])
        for face in range(FACES):
            pack_face(out, face, send_buf.at[slot, face])
        for diag in range(4):
            base = 64 + diag * 8
            for tile in range(3):
                piece = out[base : base + 8, lanes(2 * tile)]
                if tile < 2:
                    piece = jnp.where(sub8 < 4, piece, out[base : base + 8, lanes(2 * tile + 1)])
                send_diag[slot, diag, 8 * tile : 8 * tile + 8, :] = piece

    def stage(slot, early, first_block, late, merge, finish, halves_1, halves_2, magnetic_1, magnetic_2, share):
        copies = [
            remote(
                send_buf.at[slot, face], recv_buf.at[slot, face], send_sem.at[slot, face], recv_sem.at[slot, face],
                beside[face],
            )
            for face in range(FACES)
        ]
        for copy, exists in zip(copies, to_face):
            start(copy, exists)
        corner_copies = [
            remote(
                send_diag.at[slot, diag], recv_diag.at[slot, diag], diag_send_sem.at[slot, diag],
                diag_recv_sem.at[slot, diag], across[diag],
            )
            for diag in range(4)
        ]
        for copy, exists in zip(corner_copies, to_diag):
            start(copy, exists)
        early()
        own_rates(fields, halves_1, magnetic_1, first_block)
        out = dot(send_e[0:64, :], rhs[:, 0:HALF])
        if magnetic_2:
            out = out + dot(send_h[0:64, :], rhs[:, HALF:WIDE])
        next_copies = []
        for face in range(FACES):
            pack_face(out, face, send_next.at[slot, face])
            next_copies.append(
                remote(
                    send_next.at[slot, face], recv_next.at[slot, face], next_send_sem.at[slot, face],
                    next_recv_sem.at[slot, face], beside[face],
                )
            )
            start(next_copies[face], to_face[face])
        late()

        wait_all(copies, to_face, 1)
        for face in range(FACES):
            for k in range(5):
                set_ghosts(face, k, unpack_face(recv_buf.at[slot, face], k))
        merge(dot(lift[...], ghost_rhs[...]))

        def store(block, value):
            rates[:, lanes(block)] = value

        own_rates(second, halves_2, magnetic_2, store)

        wait_all(corner_copies, to_diag, 3)
        for two in range(2):
            for k in range(5):
                pieces = []
                for diag in (2 * two, 2 * two + 1):
                    tile = recv_diag[slot, diag, 8 * (k // 2) : 8 * (k // 2) + 8, :]
                    tile = jnp.where(sub8 >= 4 if k % 2 else sub8 < 4, tile, 0.0)
                    pieces.append(strength * tile)
                high, low = split(jnp.concatenate(pieces, axis=0))
                corner_rhs[16 * two : 16 * two + 16, lanes(k)] = high
                corner_rhs[32 + 16 * two : 32 + 16 * two + 16, lanes(k)] = low
        begin = at_corner + (0 if magnetic_2 else 64)
        extra = dot(mats[begin : begin + 64, 0:64], corner_rhs[...])
        wait_all(next_copies, to_face, 1)
        for face in range(FACES):
            for k in range(5):
                piece = extra[face * 16 : face * 16 + 16, lanes(k)]
                piece = jnp.concatenate([piece[0:8], jnp.where(kept(k), piece[8:16], 0.0)], axis=0)
                if not magnetic_2:
                    piece = piece + strength * unpack_face(send_buf.at[slot, face ^ 1], k)
                    piece = piece * gain_out[face * 16 : face * 16 + 16, lanes(k)]
                set_ghosts(face, k, unpack_face(recv_next.at[slot, face], k) + share * piece)
        finish(dot(lift[...] if len(halves_2) == 2 else lift[0:ROWS, :], ghost_rhs[...]))

    def inject(turn, moment):
        values = jnp.where(
            comp_id == 0,
            left[turn, moment, 0:1, :],
            jnp.where(comp_id == 1, left[turn, moment, 1:2, :], left[turn, moment, 2:3, :]),
        )
        high, low = split(pick_row[...] * values)
        return dot(jnp.concatenate([high, low], axis=1), pick_back[...])

    def gather(halves, turn, moment):
        both = dot(halves, pick_lane[...])
        chosen = (both[0:ROWS] + both[ROWS : 2 * ROWS]) * pick_row[...]
        out = jnp.zeros((8, 128), F32)
        for comp in range(3):
            part = jnp.sum(jnp.where(comp_id == comp, chosen, 0.0), axis=0, keepdims=True)
            out = jnp.where(sub8 == comp, part, out)
        left[turn, moment] = out

    def to_output_order(vector, number):
        for moment in range(2):
            both = dot_nt(jnp.concatenate(split(vector[moment]), axis=0), order[...])
            both = both[0:ROWS] + both[ROWS : 2 * ROWS]
            for block in range(5):
                perm_out[number, block, pl.ds(moment, ROWS, stride=2), :] = both[:, lanes(block)]

    every, electric = (0, 1), (0,)

    def sweep(turn, carry):
        def set_second(block, value):
            second[:, lanes(block)] = value
            put_rhs(block, value)

        def set_fields(block, value):
            fields[:, lanes(block)] = value
            put_rhs(block, value)

        def lifted_block(lifted, block):
            return lifted[block // 5 * ROWS : (block // 5 + 1) * ROWS, lanes(block % 5)]

        def merge_1(lifted):
            for block in range(10):
                set_second(block, second[:, lanes(block)] + lifted_block(lifted, block))

        def finish_1(lifted):
            for block in range(10):
                slope = second[:, lanes(block)]
                value = slope + 0.5 * (rates[:, lanes(block)] + lifted_block(lifted, block))
                if block < 5:
                    start = fields[:, lanes(block)]
                    source[turn, 1, :, lanes(block)] = gain[:, lanes(block)] * (start + 0.5 * slope)
                    value = value + start + held[:, lanes(block)]
                set_fields(block, value)
            prepare(turn * 3 + 1, True)

        def late_1():
            meet(turn, 0, -1, 0)
            held[...] = inject(turn, 0)

            @pl.when(turn == 1)
            def _():
                gather(jnp.concatenate(split(saved[...]), axis=0), 1, 1)
                reduce_send(
                    0, 0, packed_row([data_dot(left[0], left[0]), source_dot(source.at[0], source.at[0])])
                )
                to_output_order(source.at[0], 0)

        stage(
            turn * 3, lambda: meet(turn, 1, 4, 5), set_second, late_1, merge_1, finish_1, every, every, False, True, 1.0
        )

        def block_2(k, value):
            amount = gain[:, lanes(k)] * (fields[:, lanes(k)] + 0.5 * value)
            source[turn, 0, :, lanes(k)] = amount
            set_second(k, gain[:, lanes(k)] * amount)

        def merge_2(lifted):
            for k in range(5):
                amount = source[turn, 0, :, lanes(k)] + 0.5 * gain[:, lanes(k)] * lifted[0:ROWS, lanes(k)]
                source[turn, 0, :, lanes(k)] = amount
                set_second(k, gain[:, lanes(k)] * amount)

        def finish_2(lifted):
            for block in range(10):
                value = 0.5 * (rates[:, lanes(block)] + lifted_block(lifted, block))
                if block < 5:
                    value = value + second[:, lanes(block)]
                    held[:, lanes(block)] = value
                set_fields(block, value)
            prepare(turn * 3 + 2, True)

        def late_2():
            meet(turn, 0, 1, 2)
            second[:, HALF:WIDE] = jnp.zeros((ROWS, HALF), F32)

            @pl.when(turn == 1)
            def _():
                reduce_send(0, 1, reduce_take(0, 0))

            @pl.when(turn == 0)
            def _():
                wait_all(support_copies, to_face, 1)
                for face in range(FACES):
                    for k in range(5):
                        column = float(root[k] ** 2) * cols_ref[face * 16 : face * 16 + 16, 5:6]
                        gain_out[face * 16 : face * 16 + 16, lanes(k)] = column * beside_support[face]

        stage(
            turn * 3 + 1, lambda: meet(turn, 0, 0, 1), block_2, late_2, merge_2, finish_2, electric, every, True, False, 0.5
        )

        def early_3():
            meet(turn, 0, 2, 3)

        def block_3(block, value):
            if block < 5:
                value = value + gain[:, lanes(block)] * source[turn, 1, :, lanes(block)]
            set_second(block, fields[:, lanes(block)] + 0.5 * value)

        def merge_3(lifted):
            for block in range(10):
                set_second(block, second[:, lanes(block)] + 0.5 * lifted_block(lifted, block))

        def finish_3(lifted):
            for k in range(5):
                saved[:, lanes(k)] = fields[:, lanes(k)] + rates[:, lanes(k)] + lifted[:, lanes(k)]

        def late_3():
            meet(turn, 0, 3, 4)
            for k in range(5):
                fields[:, lanes(k)] = fields[:, lanes(k)] + gain[:, lanes(k)] * source[turn, 1, :, lanes(k)]
            gather(jnp.concatenate(split(held[...]), axis=0), turn + 1, 0)

            @pl.when(turn == 1)
            def _():
                norms = reduce_take(0, 1)
                red_buf[0, 0, 0] = norms
                ratio = entry(norms, 1) / entry(norms, 0)
                for moment in range(2):
                    for k in range(5):
                        ortho[moment, :, lanes(k)] = (
                            source[1, moment, :, lanes(k)] - ratio * source[0, moment, :, lanes(k)]
                        )
                dots = [
                    source_dot(ortho, ortho), source_dot(ortho, source.at[0]), data_dot(left[1], left[1]),
                ]
                for moment in range(2):
                    left[0, moment] = left[1, moment] - ratio * left[0, moment]
                dots += [data_dot(left[0], left[0]), data_dot(left[1], left[0])]
                red_buf[0, 1, 0] = packed_row(dots)
                to_output_order(ortho, 1)

        stage(turn * 3 + 2, early_3, block_3, late_3, merge_3, finish_3, every, electric, True, True, 0.5)

        @pl.when(turn == 0)
        def _():
            for k in range(5):
                set_fields(k, multiple[:, lanes(k)] * saved[:, lanes(k)])
            fields[:, HALF:WIDE] = jnp.zeros((ROWS, HALF), F32)
            prepare(3, False)

        return carry

    first_input = inject(0, 1)
    fields[:, 0:HALF] = first_input
    for k in range(5):
        put_rhs(k, first_input[:, lanes(k)])
    fields[:, HALF:WIDE] = jnp.zeros((ROWS, HALF), F32)
    prepare(0, False)
    pl.semaphore_wait(barrier, greeted)
    for copy, exists in zip(support_copies, to_face):
        start(copy, exists)
    lax.fori_loop(0, 2, sweep, 0)
    gather(jnp.concatenate(split(saved[...]), axis=0), 2, 1)

    norms = red_buf[0, 0, 0]
    sq_b, sq_g = entry(norms, 0), entry(norms, 1)
    ratio = sq_g / sq_b
    for moment in range(2):
        left[2, moment] = left[2, moment] - ratio * left[1, moment]
    p, f, h = left[0], left[1], left[2]
    row = red_buf[0, 1, 0]
    for number, value in ((5, data_dot(h, h)), (6, data_dot(h, f)), (7, data_dot(h, p))):
        row = jnp.where(lane1 == number, value, row)
    reduce_send(1, 0, row)
    reduce_send(1, 1, reduce_take(1, 0))
    total = reduce_take(1, 1)
    oo, og, ff, pp, fp, hh, hf, hp = (entry(total, number) for number in range(8))
    take = pp / sq_g
    sq_q = jnp.maximum(oo - 2.0 * take * og + take * take * sq_g, 0.0)
    beta_1 = jnp.sqrt(sq_b)
    alpha_1 = jnp.sqrt(ratio)
    beta_2 = jnp.sqrt(take)
    alpha_2 = jnp.sqrt(sq_q / pp)
    sq_w = hh - 2.0 * take * hf + take * take * ff
    sq_beta_3 = jnp.maximum(sq_w / sq_q - 2.0 * (hp - take * fp) / pp + sq_q / pp, 0.0)
    rho_1 = jnp.sqrt(alpha_1 * alpha_1 + beta_2 * beta_2)
    cosine, sine = alpha_1 / rho_1, beta_2 / rho_1
    step_1 = cosine * beta_1 / rho_1
    phi_bar = sine * beta_1
    theta = sine * alpha_2
    rho_bar = -cosine * alpha_2
    rho_2 = jnp.sqrt(rho_bar * rho_bar + sq_beta_3)
    step_2 = rho_bar / rho_2 * phi_bar / rho_2
    on_ortho = step_2 / jnp.sqrt(sq_q)
    on_first = (step_1 - step_2 * theta / rho_1) / jnp.sqrt(sq_g) - on_ortho * take
    on_h = phi_bar / rho_2 / jnp.sqrt(sq_q)
    on_p = phi_bar / rho_2 * jnp.sqrt(sq_q) / pp
    for moment in range(2):
        out = on_h * (h[moment] - take * f[moment]) - on_p * p[moment]
        for comp in range(3):
            res_ref[comp, moment : moment + 1, :] = out[comp : comp + 1, :]
    for tile in range(19):
        rows = slice(8 * tile, 8 * tile + 8)
        for block in range(5):
            value = on_first * perm_out[0, block, rows, :] + on_ortho * perm_out[1, block, rows, :]
            for part in range(4):
                node = 4 * tile + part
                if node < 75:
                    est_ref[node // 25, node // 5 % 5, node % 5, :, lanes(block)] = value[2 * part : 2 * part + 2, :]


def solution(mesh):
    n_gx, n_gy = mesh.shape["gx"], mesh.shape["gy"]
    matrices, columns = tables()

    def shards(probe_data, conductivity, support, face_tags, probe_nodes):
        vmem = pl.BlockSpec(memory_space=pltpu.VMEM)
        anywhere = pl.BlockSpec(memory_space=pl.ANY)
        estimate, residual = pl.pallas_call(
            functools.partial(kernel, n_gx, n_gy),
            out_shape=(
                jax.ShapeDtypeStruct((3, 5, 5, 2, HALF), F32),
                jax.ShapeDtypeStruct((3, 2, 128), F32),
            ),
            in_specs=[anywhere] * 7,
            out_specs=(vmem, vmem),
            scratch_shapes=[
                pltpu.VMEM((1, 1, 2), jnp.int32),
                pltpu.VMEM((3, 2, 128), F32),
                pltpu.VMEM((5, 5, HALF), F32),
                pltpu.VMEM((1, 1, 128), jnp.int32),
                pltpu.VMEM((1, 128), jnp.int32),
                pltpu.VMEM(matrices.shape, F32),
                pltpu.VMEM(columns.shape, F32),
                pltpu.VMEM(matrices.shape, BF16),
                pltpu.VMEM((HALF, HALF), BF16),
                pltpu.VMEM((3, ROWS, 128), F32),
                pltpu.VMEM((ROWS, WIDE), F32),
                pltpu.VMEM((ROWS, WIDE), F32),
                pltpu.VMEM((ROWS, WIDE), F32),
                pltpu.VMEM((ROWS, HALF), F32),
                pltpu.VMEM((ROWS, HALF), F32),
                pltpu.VMEM((ROWS, HALF), F32),
                pltpu.VMEM((256, WIDE), BF16),
                pltpu.VMEM((INNER, WIDE), F32),
                pltpu.VMEM((128, HALF), BF16),
                pltpu.VMEM((64, HALF), BF16),
                pltpu.VMEM((ROWS, HALF), F32),
                pltpu.VMEM((ROWS, HALF), F32),
                pltpu.VMEM((64, HALF), F32),
                pltpu.VMEM((ROWS, 128), F32),
                pltpu.VMEM((HALF, 128), BF16),
                pltpu.VMEM((256, HALF), BF16),
                pltpu.VMEM((3, 2, 8, 128), F32),
                pltpu.VMEM((2, 2, ROWS, HALF), F32),
                pltpu.VMEM((2, ROWS, HALF), F32),
                pltpu.VMEM((ROWS, HALF), F32),
                pltpu.VMEM((2, 5, 2 * ROWS, 128), F32),
                pltpu.VMEM((FACES, 1, 128), F32),
                pltpu.VMEM((1, 128), F32),
                pltpu.VMEM((6, FACES, QROWS, 128), F32),
                pltpu.VMEM((6, FACES, QROWS, 128), F32),
                pltpu.VMEM((6, FACES, QROWS, 128), F32),
                pltpu.VMEM((6, FACES, QROWS, 128), F32),
                pltpu.VMEM((6, 4, 24, 128), F32),
                pltpu.VMEM((6, 4, 24, 128), F32),
                pltpu.VMEM((2, 2, max(n_gx, n_gy), 1, 128), F32),
                pltpu.SemaphoreType.DMA((7,)),
                pltpu.SemaphoreType.DMA((6, FACES)),
                pltpu.SemaphoreType.DMA((6, FACES)),
                pltpu.SemaphoreType.DMA((6, FACES)),
                pltpu.SemaphoreType.DMA((6, FACES)),
                pltpu.SemaphoreType.DMA((6, 4)),
                pltpu.SemaphoreType.DMA((6, 4)),
                pltpu.SemaphoreType.DMA((2, 2)),
                pltpu.SemaphoreType.DMA((2, 2)),
                pltpu.SemaphoreType.DMA((FACES,)),
                pltpu.SemaphoreType.DMA((FACES,)),
                pltpu.SemaphoreType.REGULAR((5,)),
            ],
            compiler_params=pltpu.CompilerParams(
                collective_id=0, has_side_effects=True, vmem_limit_bytes=22 * 1024 * 1024
            ),
        )(
            *(
                pltpu.with_memory_space_constraint(array, pltpu.HBM)
                for array in (
                    jnp.transpose(face_tags, (1, 2, 0)), jnp.transpose(probe_data, (1, 0, 2)), conductivity, support,
                    probe_nodes.reshape(1, 128), jnp.asarray(matrices), jnp.asarray(columns),
                )
            )
        )
        return jnp.transpose(estimate, (3, 0, 1, 2, 4)), jnp.transpose(residual, (1, 0, 2))

    return jax.shard_map(
        shards,
        mesh=mesh,
        in_specs=(
            P(None, None, ("gx", "gy")),
            P("gx", "gy", None),
            P("gx", "gy", None),
            P(None, "gx", "gy"),
            P(("gx", "gy")),
        ),
        out_specs=(P(None, None, "gx", "gy", None), P(None, None, ("gx", "gy"))),
        check_vma=False,
    )
```
